32 devices in a mesh: samples: 2 (over x), brick: 16 (over z, y, core).
Axes of the slice: x: 2, y: 2, z: 4, core: 2. Of those that a mesh axis runs over, the one named last changes fastest.
Arguments:
- source: float32 [128, 128, 256], P(('samples', 'brick')), parts along dimension 0, may hold values from -6 to 6
- guess: float32 [128, 128, 256], P(('samples', 'brick')), parts along dimension 0, may hold values from -6 to 6
- log_perm: float32 [128, 128, 256], P(('samples', 'brick')), parts along dimension 0, may hold values from -3 to 3
- owner: int32 [16], replicated, may hold values from 0 to 15, each once
Outputs:
- corrected: float32 [128, 128, 256], P(('samples', 'brick')), parts along dimension 0
- coarse_held: float32 [32, 2048], P(('samples', 'brick')), parts along dimension 0
The draws below stay inside these ranges and needn't reach their ends.
There are 2 independent parts, one for each index of `samples`. The reference program is written for one: setup_inputs(seed, part) draws one part's arguments, and reference() takes and returns one part's arrays. A program takes and returns all parts, laid end to end along the dimension named above; an argument that names none is the same for every part. Nothing has to cross between parts.
Inputs may be any that keep to these rules, and one draw needn't show every extreme that they name: `owner`: each brick index appears exactly once.
All inputs are finite; a program needn't handle non-finite values.
Results may differ from the reference program's by a relative error of at most 0.00005.
Values sent between devices are 32-bit elements; how exact they have to be, the bound alone decides.
A program may use at most 64 MiB of HBM per device.

```python
import jax
import jax.numpy as jnp
from jax import lax

NY = 128
NZ = 256
NU = 2
SWEEPS = 8
NX = 64
CPD = 1
BLOCKS = 16
NXC = 16
CYC = 32
CZC = 64


def channel_columns(key):
    key_mask = jax.random.fold_in(key, 7)
    column_mask = jax.random.uniform(key_mask, (NY // 4, NZ // 4)) < 0.35
    column_mask = jnp.repeat(jnp.repeat(column_mask, 4, axis=0), 4, axis=1)
    return column_mask


def draw_log_perm(key, part):
    column_mask = channel_columns(key)
    key_rough = jax.random.fold_in(key, 12)
    base_level = jnp.where(column_mask, 0.4, -1.6).astype(jnp.float32)
    rough_part = 0.45 * jax.random.normal(key_rough, (NX, NY, NZ), jnp.float32)
    return jnp.clip(base_level[None, :, :] + rough_part, -3.0, 3.0).astype(jnp.float32)


def draw_source(key, part):
    column_mask = channel_columns(key)
    key_signs = jax.random.fold_in(key, 21)
    key_size = jax.random.fold_in(key, 22)
    key_rough = jax.random.fold_in(key, 23)
    sign_draw = jnp.where(jax.random.uniform(key_signs, (NX // 4,)) < 0.5, -1.0, 1.0).astype(jnp.float32)
    magnitude = jax.random.uniform(key_size, (NX // 4,), jnp.float32, 1.0, 2.5)
    plane_level = sign_draw * magnitude
    rough_part = 0.4 * jax.random.normal(key_rough, (NX, NY, NZ), jnp.float32)
    plane_level = jnp.repeat(plane_level, 4)
    column_weight = jnp.where(column_mask, 1.0, 0.05).astype(jnp.float32)
    smooth_part = plane_level[:, None, None] * column_weight[None, :, :]
    return jnp.clip(smooth_part + rough_part, -6.0, 6.0).astype(jnp.float32)


def block_scale(stream_key, extent, shards, low, largest):
    factor_of, own = 1.0, jax.random.fold_in(stream_key, 6)
    for axis_at, parts in shards:
        heights = jnp.exp(jax.random.uniform(jax.random.fold_in(own, axis_at), (parts,), jnp.float32, low / len(shards), largest / len(shards)))
        factor_of = factor_of * jnp.repeat(heights, extent[axis_at] // parts).reshape([-1 if axis == axis_at else 1 for axis in range(len(extent))])
    return factor_of


def noise(key, dims, deviation, most, shards=(), kind=jnp.bfloat16):
    gain = block_scale(key, dims, shards, -0.22, 0.18) if shards else 1.0
    entries = jax.random.normal(key, dims, jnp.float32) * deviation * gain
    return jnp.minimum(jnp.maximum(entries, -most), most).astype(kind)


def setup_inputs(seed: int = 0, part: int = 0) -> dict:
    keys = jax.random.split(jax.random.key(seed), 5)
    part_keys = jax.random.split(jax.random.fold_in(keys[4], part), 5)
    source = draw_source(jax.random.fold_in(jax.random.fold_in(keys[4], part), 71), part)
    guess = noise(part_keys[1], (NX, NY, NZ), 1.0, 6.0, ((0, 16),), jnp.float32)
    log_perm = draw_log_perm(jax.random.fold_in(jax.random.fold_in(keys[4], part), 71), part)
    owner = jax.random.permutation(keys[3], BLOCKS).astype(jnp.int32)
    return dict(source=source, guess=guess, log_perm=log_perm, owner=owner)


relax_weight = 0.8


def prolong_matrix(n_fine):
    fine_idx = jnp.arange(n_fine)[:, None]
    coarse_idx = jnp.arange(n_fine // 4)[None, :]
    base = fine_idx // 4
    offset = fine_idx % 4
    weight_own = jnp.where((offset == 0) | (offset == 3), 0.625, 0.875).astype(jnp.float32)
    side = jnp.where(offset < 2, -1, 1)
    own = jnp.where(coarse_idx == base, weight_own, 0.0)
    other = jnp.where(coarse_idx == base + side, 1.0 - weight_own, 0.0)
    return (own + other).astype(jnp.float32)


def apply_op(field, coeff):
    padded = jnp.pad(field, 1)
    kpad = jnp.pad(coeff, 1)
    center = padded[1:-1, 1:-1, 1:-1]
    kcen = kpad[1:-1, 1:-1, 1:-1]
    pairs = [
        (padded[:-2, 1:-1, 1:-1], kpad[:-2, 1:-1, 1:-1]),
        (padded[2:, 1:-1, 1:-1], kpad[2:, 1:-1, 1:-1]),
        (padded[1:-1, :-2, 1:-1], kpad[1:-1, :-2, 1:-1]),
        (padded[1:-1, 2:, 1:-1], kpad[1:-1, 2:, 1:-1]),
        (padded[1:-1, 1:-1, :-2], kpad[1:-1, 1:-1, :-2]),
        (padded[1:-1, 1:-1, 2:], kpad[1:-1, 1:-1, 2:]),
    ]
    diagonal = jnp.zeros_like(field)
    nearby = jnp.zeros_like(field)
    for value, kval in pairs:
        face = 0.5 * (kcen + kval)
        diagonal = diagonal + face
        nearby = nearby + face * value
    return diagonal * center - nearby, diagonal


def reference(source, guess, log_perm, owner):
    hp = lax.Precision.HIGHEST
    perm = jnp.exp(log_perm)
    smooth = guess
    for sweep in range(NU):
        image, diagonal = apply_op(smooth, perm)
        smooth = smooth + relax_weight * (source - image) / diagonal
    image, diagonal = apply_op(smooth, perm)
    resid = source - image
    px = prolong_matrix(NX)
    py = prolong_matrix(NY)
    pz = prolong_matrix(NZ)
    step_one = jnp.einsum('xyz,xX->Xyz', resid, px, precision=hp)
    step_two = jnp.einsum('Xyz,yY->XYz', step_one, py, precision=hp)
    coarse_rhs = jnp.einsum('XYz,zZ->XYZ', step_two, pz, precision=hp) * (1.0 / 64.0)
    coarse_perm = perm.reshape(NXC, 4, CYC, 4, CZC, 4).sum(axis=(1, 3, 5)) * (1.0 / 64.0)
    coarse = jnp.zeros((NXC, CYC, CZC), jnp.float32)
    for sweep in range(SWEEPS):
        image, diagonal = apply_op(coarse, coarse_perm)
        coarse = coarse + relax_weight * (coarse_rhs - image * (1.0 / 16.0)) / (diagonal * (1.0 / 16.0))
    back_one = jnp.einsum('XYZ,xX->xYZ', coarse, px, precision=hp)
    back_two = jnp.einsum('xYZ,yY->xyZ', back_one, py, precision=hp)
    correction = jnp.einsum('xyZ,zZ->xyz', back_two, pz, precision=hp)
    corrected = smooth + correction
    blocks = coarse.reshape(BLOCKS, CPD, CYC * CZC)
    held = jnp.zeros_like(blocks).at[owner].set(blocks)
    return corrected, held.reshape(NXC, CYC * CZC)
```

```python
import functools

import jax
import jax.numpy as jnp
import ml_dtypes
import numpy as np
from jax import lax
from jax.experimental import pallas as pl
from jax.experimental.pallas import tpu as pltpu
from jax.sharding import PartitionSpec as P

SWEEPS = 8
CHUNKS = 8
MESH = pl.DeviceIdType.MESH
F32 = jnp.float32
BF16 = jnp.bfloat16


def prolong_matrix(n_fine):
    i = np.arange(n_fine)[:, None]
    j = np.arange(n_fine // 4)[None, :]
    base, offset = i // 4, i % 4
    own = np.where((offset == 0) | (offset == 3), 0.625, 0.875)
    side = np.where(offset < 2, -1, 1)
    return np.where(j == base, own, 0.0) + np.where(j == base + side, 1.0 - own, 0.0)


def mean_matrix(n_fine):
    i = np.arange(n_fine)[:, None]
    j = np.arange(n_fine // 4)[None, :]
    return np.where(j == i // 4, 1.0, 0.0)


def even_odd(m):
    return np.concatenate([m[:, 0::2], m[:, 1::2]], axis=1)


def halves(m):
    zero = np.zeros_like(m)
    return np.stack([np.concatenate([m, zero], 1), np.concatenate([zero, m], 1)])


def split(x):
    hi = x.astype(BF16)
    return hi, (x - hi.astype(F32)).astype(BF16)


def dot(a, b):
    return jnp.dot(a, b, preferred_element_type=F32)


def to_coarse(y_mat, z_mat, x):
    hi, lo = split(x)
    a = dot(y_mat, hi) + dot(y_mat, lo)
    hi, lo = split(a)
    h = a.shape[0] // 2
    return (
        dot(hi[:h], z_mat[0]) + dot(lo[:h], z_mat[0]) + dot(hi[h:], z_mat[1]) + dot(lo[h:], z_mat[1])
    )


def smooth_kernel(
    n, ny, nz, group,
    source_hbm, guess_hbm, logq_hbm, owner_hbm, ry_hbm, rz_hbm, my_hbm, mz_hbm, ez_hbm, ey_hbm,
    U2, C, ez, ey, holder,
    owner, coef, scaled, ry, rz, my, mz, all_q, q_pad, all_r, B, src, logq, K, U0, U1, D, W, N, F, X, H, part,
    local_sem, halo_send, halo_recv, part_send, part_recv, q_send, q_recv, r_send, r_recv, token_sem,
):
    me = lax.axis_index("brick")
    R = ny // CHUNKS
    half = n // 2
    has = (me > 0, me < n - 1)
    flag = [jnp.where(h, 1.0, 0.0).astype(F32) for h in has]
    peer_of = (me - 1, me + 1)
    sibling = me + 1 - 2 * lax.rem(me, 2)

    loads = [
        pltpu.make_async_copy(logq_hbm, logq, local_sem.at[0]),
        pltpu.make_async_copy(guess_hbm, U0.at[:, pl.ds(8, ny)], local_sem.at[1]),
        pltpu.make_async_copy(source_hbm, src, local_sem.at[2]),
        pltpu.make_async_copy(my_hbm, my, local_sem.at[3]),
        pltpu.make_async_copy(mz_hbm, mz, local_sem.at[4]),
        pltpu.make_async_copy(ry_hbm, ry, local_sem.at[5]),
        pltpu.make_async_copy(rz_hbm, rz, local_sem.at[6]),
        pltpu.make_async_copy(ez_hbm, ez, local_sem.at[7]),
        pltpu.make_async_copy(ey_hbm, ey, local_sem.at[8]),
        pltpu.make_async_copy(owner_hbm, owner, local_sem.at[9]),
    ]

    def signal(sem, who):
        pl.semaphore_signal(sem, inc=1, device_id={"brick": who}, device_id_type=MESH)

    barrier = pltpu.get_barrier_semaphore()

    def greet(sem, distance):
        @pl.when(me >= distance)
        def _():
            signal(sem, me - distance)

        @pl.when(me + distance < n)
        def _():
            signal(sem, me + distance)

    def greeted(sem, distance):
        low = jnp.where(me >= distance, 1, 0)
        high = jnp.where(me + distance < n, 1, 0)
        pl.semaphore_wait(sem, low + high)

    distances = [2**k for k in range((n - 1).bit_length())]

    greet(barrier, 1)
    for copy in loads:
        copy.start()

    zero_rows = jnp.zeros((8, nz), F32)
    for ref in (K, U0, U1, U2):
        for p in range(4):
            ref[p, 0:8] = zero_rows
            ref[p, ny + 8 : ny + 16] = zero_rows
    for side in range(2):

        @pl.when(jnp.logical_not(has[side]))
        def _():
            for which in range(3):
                H[which, side] = jnp.zeros((ny, nz), F32)

    greeted(barrier, 1)

    def rows_at(c):
        return pl.ds(c * R if isinstance(c, int) else pl.multiple_of(c * R, R), R)

    def rows_in(c):
        return pl.ds(8 + c * R if isinstance(c, int) else pl.multiple_of(c * R, R) + 8, R)

    def halo(which, side, c):
        plane = 3 * side
        if which == 2:
            ref = U1.at[plane, rows_in(c)]
        else:
            ref = (logq_hbm, guess_hbm)[which].at[plane, rows_at(c)]
        return pltpu.make_async_remote_copy(
            src_ref=ref,
            dst_ref=H.at[which, 1 - side, rows_at(c)],
            send_sem=halo_send.at[which, side, c],
            recv_sem=halo_recv.at[which, 1 - side, c],
            device_id={"brick": peer_of[side]},
            device_id_type=MESH,
        )

    def arrival(which, side, c):
        ref = H.at[which, side, rows_at(c)]
        return pltpu.make_async_remote_copy(
            src_ref=ref,
            dst_ref=ref,
            send_sem=halo_send.at[which, side, c],
            recv_sem=halo_recv.at[which, side, c],
            device_id={"brick": peer_of[side]},
            device_id_type=MESH,
        )

    for c in range(CHUNKS):
        for side in range(2):

            @pl.when(has[side])
            def _():
                halo(0, side, c).start()
                halo(1, side, c).start()

    greet(token_sem.at[0], 1)

    lane = lax.broadcasted_iota(jnp.int32, (R, nz), 1)
    first, last = lane == 0, lane == nz - 1

    def middle(window):
        return window[8 : R + 8]

    def yz(window):
        center = middle(window)
        low = jnp.where(first, 0.0, pltpu.roll(center, 1, 1))
        high = jnp.where(last, 0.0, pltpu.roll(center, nz - 1, 1))
        return (window[7 : R + 7] + window[9 : R + 9]) + (low + high)

    def across(windows, p):
        total = yz(windows[p])
        if p > 0:
            total = total + middle(windows[p - 1])
        if p < 3:
            total = total + middle(windows[p + 1])
        return total

    loads[0].wait()

    def exps(c, _):
        for p in range(4):
            K[p, rows_in(c)] = jnp.exp(logq[p, rows_at(c)])
        return 0

    lax.fori_loop(0, CHUNKS, exps, 0)
    for copy in loads[1:]:
        copy.wait()

    def windows(ref, c):
        at = pl.ds(pl.multiple_of(c * R, R), R + 16)
        return [ref[p, at] for p in range(4)]

    def nearby(u, k):
        uk = [a * b for a, b in zip(u, k)]
        return [0.5 * (middle(k[p]) * across(u, p) + across(uk, p)) for p in range(4)]

    def sweep_one(c, _):
        rows, at = rows_at(c), rows_in(c)
        u, k = windows(U0, c), windows(K, c)
        near = nearby(u, k)
        for p in range(4):
            d = 3.0 * middle(k[p]) + 0.5 * across(k, p)
            total = src[p, rows] + near[p]
            D[p, rows] = d
            if p in (0, 3):
                N[p, rows] = total
            else:
                w = 0.8 / d
                W[p, rows] = w
                U1[p, at] = 0.2 * middle(u[p]) + w * total
        return 0

    lax.fori_loop(0, CHUNKS, sweep_one, 0)
    greeted(token_sem.at[0], 1)

    all_q[me] = to_coarse(
        my[...], mz, (K[0, 8 : ny + 8] + K[1, 8 : ny + 8]) + (K[2, 8 : ny + 8] + K[3, 8 : ny + 8])
    ) * (1.0 / 64.0)
    for b in range(n):
        holder[b : b + 1] = jnp.full((1, 128), owner[b], jnp.int32)

    for k in range(1, len(distances)):
        greet(token_sem.at[k], distances[k])
        if k + 1 < len(distances):
            greeted(token_sem.at[k], distances[k])

    def finish_one(c):
        rows, at = rows_at(c), rows_in(c)
        for side in range(2):

            @pl.when(has[side])
            def _():
                arrival(0, side, c).wait_recv()
                arrival(1, side, c).wait_recv()

        for side in range(2):
            p = 3 * side
            kh = jnp.exp(H[0, side, rows]) * flag[side]
            face = 0.5 * (K[p, at] + kh)
            d = D[p, rows] + 0.5 * kh
            w = 0.8 / d
            F[side, rows] = face
            D[p, rows] = d
            W[p, rows] = w
            U1[p, at] = 0.2 * U0[p, at] + w * (N[p, rows] + face * H[1, side, rows])
        for side in range(2):

            @pl.when(has[side])
            def _():
                halo(2, side, c).start()

    def copy_to(ref, slot, who, send, recv):
        return pltpu.make_async_remote_copy(
            src_ref=ref.at[slot],
            dst_ref=ref.at[slot],
            send_sem=send,
            recv_sem=recv.at[slot],
            device_id={"brick": who},
            device_id_type=MESH,
        )

    def direct(ref, j, send, recv):
        return copy_to(ref, me, lax.rem(me + 2 * j, n), send.at[j], recv)

    def handed(ref, j, send, recv):
        who = lax.rem(me + n - 2 * j, n)
        return copy_to(ref, who, sibling, send.at[half + j], recv)

    def to_sibling(ref, send, recv):
        return copy_to(ref, me, sibling, send.at[0], recv)

    def spread(ref, send, recv):
        def body(j, _):
            direct(ref, j, send, recv).start()
            return 0

        lax.fori_loop(1, half, body, 0)
        to_sibling(ref, send, recv).start()

    def hand_on(ref, send, recv):
        def body(j, _):
            copy = handed(ref, j, send, recv)
            copy.wait_recv()
            copy.start()
            return 0

        lax.fori_loop(1, half, body, 0)

    def collect(ref, send, recv):
        def body(j, _):
            slot = lax.rem(sibling + n - 2 * j, n)
            copy_to(ref, slot, sibling, send.at[half + j], recv).wait_recv()
            return 0

        lax.fori_loop(0, half, body, 0)

    def sent(ref, send, recv):
        def body(j, _):
            direct(ref, j, send, recv).wait_send()
            handed(ref, j, send, recv).wait_send()
            return 0

        lax.fori_loop(1, half, body, 0)
        to_sibling(ref, send, recv).wait_send()

    def sweep_two(c):
        rows, at = rows_at(c), rows_in(c)
        u = windows(U1, c)
        near = nearby(u, windows(K, c))
        for p in range(4):
            total = src[p, rows] + near[p]
            if p in (0, 3):
                N[p, rows] = total
            else:
                U2[p, at] = 0.2 * middle(u[p]) + W[p, rows] * total

    def first_stage(c, _):
        @pl.when(c < CHUNKS)
        def _():
            finish_one(c)

        @pl.when(c == CHUNKS - 1)
        def _():
            greeted(token_sem.at[len(distances) - 1], distances[-1])
            spread(all_q, q_send, q_recv)

        @pl.when(c > 0)
        def _():
            sweep_two(c - 1)

        return 0

    lax.fori_loop(0, CHUNKS + 1, first_stage, 0)

    def finish_two(c):
        rows, at = rows_at(c), rows_in(c)
        for side in range(2):

            @pl.when(has[side])
            def _():
                arrival(2, side, c).wait_recv()

        for side in range(2):
            p = 3 * side
            total = N[p, rows] + F[side, rows] * H[2, side, rows]
            U2[p, at] = 0.2 * U1[p, at] + W[p, rows] * total

    def residual(c):
        rows = rows_at(c)
        u = windows(U2, c)
        near = nearby(u, windows(K, c))
        r = [src[p, rows] - D[p, rows] * middle(u[p]) + near[p] for p in range(4)]
        flo = flag[0] * F[0, rows] * middle(u[0])
        fhi = flag[1] * F[1, rows] * middle(u[3])
        X[0, rows] = 0.625 * flo + 0.375 * r[0] + 0.125 * r[1]
        X[1, rows] = (0.375 * flo + 0.625 * r[0] + 0.875 * r[1]) + (0.375 * fhi + 0.625 * r[3] + 0.875 * r[2])
        X[2, rows] = 0.625 * fhi + 0.375 * r[3] + 0.125 * r[2]

    def second_stage(c, _):
        @pl.when(c < CHUNKS)
        def _():
            finish_two(c)

        @pl.when(c > 0)
        def _():
            residual(c - 1)

        return 0

    lax.fori_loop(0, CHUNKS + 1, second_stage, 0)

    def partial(side):
        return pltpu.make_async_remote_copy(
            src_ref=part.at[side],
            dst_ref=part.at[3 - side],
            send_sem=part_send.at[side],
            recv_sem=part_recv.at[1 - side],
            device_id={"brick": peer_of[side]},
            device_id_type=MESH,
        )

    def partial_in(side):
        return pltpu.make_async_remote_copy(
            src_ref=part.at[2 + side],
            dst_ref=part.at[2 + side],
            send_sem=part_send.at[side],
            recv_sem=part_recv.at[side],
            device_id={"brick": peer_of[side]},
            device_id_type=MESH,
        )

    for side in range(2):
        part[side] = to_coarse(ry[...], rz, X[2 * side])

    for side in range(2):

        @pl.when(has[side])
        def _():
            partial(side).start()

        @pl.when(jnp.logical_not(has[side]))
        def _():
            part[2 + side] = jnp.zeros(part.shape[1:], F32)

    mine = to_coarse(ry[...], rz, X[1])
    for side in range(2):

        @pl.when(has[side])
        def _():
            partial_in(side).wait_recv()

    all_r[me] = (mine + (part[2] + part[3])) * (1.0 / 64.0)
    spread(all_r, r_send, r_recv)

    hand_on(all_q, q_send, q_recv)
    collect(all_q, q_send, q_recv)
    coarse_coefficients(n, min(8, n), all_q, q_pad, coef, scaled)
    hand_on(all_r, r_send, r_recv)

    rows, lanes = all_r.shape[1:]
    shifts, _ = coarse_shifts((group, rows, lanes))
    edge = jnp.zeros((rows, lanes), F32)
    for slot in range(2):
        C[slot, 0] = edge
        C[slot, n + 1] = edge
    collect(all_r, r_send, r_recv)
    B[...] = all_r[...] * scaled[...]
    C[0, 1 : n + 1] = B[...]

    for sweep in range(SWEEPS - 1):
        now, later = sweep % 2, 1 - sweep % 2

        def step(g, _):
            at = pl.multiple_of(g * group, group)
            c = C[now, pl.ds(at + 1, group)]
            near = (C[now, pl.ds(at, group)], C[now, pl.ds(at + 2, group)]) + shifts(c)
            terms = [coef[k, pl.ds(at, group)] * v for k, v in enumerate(near)]
            total = B[pl.ds(at, group)] + 0.2 * c
            total = (total + (terms[0] + terms[1])) + ((terms[2] + terms[3]) + (terms[4] + terms[5]))
            C[later, pl.ds(at + 1, group)] = total
            return 0

        lax.fori_loop(0, n // group, step, 0)

    for side in range(2):

        @pl.when(has[side])
        def _():
            for c in range(CHUNKS):
                for which in range(3):
                    halo(which, side, c).wait_send()
            partial(side).wait_send()

    sent(all_q, q_send, q_recv)
    sent(all_r, r_send, r_recv)


def coarse_shifts(shape):
    rows, lanes = shape[1:]
    cz = lanes // 2
    row = lax.broadcasted_iota(jnp.int32, shape, 1)
    lane = lax.broadcasted_iota(jnp.int32, shape, 2)
    low_half = lane < cz
    z = jnp.where(low_half, lane, lane - cz)
    outside = (
        (row == 0) & low_half,
        (row == rows - 1) & jnp.logical_not(low_half),
        z == 0,
        z == cz - 1,
    )

    def shifts(c):
        swapped = pltpu.roll(c, cz, 2)
        y_low = jnp.where(low_half, pltpu.roll(swapped, 1, 1), swapped)
        y_high = jnp.where(low_half, swapped, pltpu.roll(swapped, rows - 1, 1))
        return y_low, y_high, pltpu.roll(c, 1, 2), pltpu.roll(c, lanes - 1, 2)

    return shifts, outside


def coarse_coefficients(n, group, perm, q_pad, coef, scaled):
    rows, lanes = perm.shape[1:]
    shifts, outside = coarse_shifts((group, rows, lanes))
    edge = jnp.zeros((rows, lanes), F32)
    q_pad[0] = edge
    q_pad[n + 1] = edge
    q_pad[1 : n + 1] = perm[...]

    def prepare(g, _):
        at = pl.multiple_of(g * group, group)
        q = q_pad[pl.ds(at + 1, group)]
        near = [q_pad[pl.ds(at, group)], q_pad[pl.ds(at + 2, group)]]
        near += [jnp.where(out, 0.0, v) for out, v in zip(outside, shifts(q))]
        faces = [0.5 * (q + v) for v in near]
        diagonal = ((faces[0] + faces[1]) + (faces[2] + faces[3])) + (faces[4] + faces[5])
        scale = 0.8 / diagonal
        for k, out in enumerate((None, None) + outside):
            f = faces[k] * scale
            coef[k, pl.ds(at, group)] = f if out is None else jnp.where(out, 0.0, f)
        scaled[pl.ds(at, group)] = 16.0 * scale
        return 0

    lax.fori_loop(0, n // group, prepare, 0)


def prolong_kernel(n, C, U2, ez, ey, holder, corrected_hbm, held_hbm, corrected, held, sem):
    me = lax.axis_index("brick")
    rows, lanes = C.shape[2:]
    ny = corrected.shape[1]
    final = (SWEEPS - 1) % 2
    below, mid, above = C[final, me], C[final, me + 1], C[final, me + 2]
    planes = jnp.concatenate(
        [
            0.625 * mid + 0.375 * below,
            0.875 * mid + 0.125 * below,
            0.875 * mid + 0.125 * above,
            0.625 * mid + 0.375 * above,
        ],
        axis=0,
    )
    hi, lo = split(planes)
    even = dot(hi, ez[0]) + dot(lo, ez[0])
    odd = dot(hi, ez[1]) + dot(lo, ez[1])
    copies = []
    for p in range(4):
        both = jnp.concatenate(
            [even[p * rows : (p + 1) * rows], odd[p * rows : (p + 1) * rows]], axis=0
        )
        hi, lo = split(both)
        corrected[p] = U2[p, 8 : ny + 8] + (dot(ey[...], hi) + dot(ey[...], lo))
        copies.append(pltpu.make_async_copy(corrected.at[p], corrected_hbm.at[p], sem.at[p]))
        copies[p].start()

    mine = jnp.zeros((rows, lanes), F32)
    for b in range(n):
        mine = jnp.where(holder[b : b + 1] == me, C[final, b + 1], mine)
    for r in range(rows):
        held[0:1, r * lanes : (r + 1) * lanes] = mine[r : r + 1]
    copies.append(pltpu.make_async_copy(held, held_hbm, sem.at[4]))
    copies[4].start()
    for copy in copies:
        copy.wait()


def local(n, source, guess, log_perm, owner):
    planes, ny, nz = source.shape
    assert planes == 4 and n % 2 == 0
    cells = (ny // 4) * (nz // 4)
    rows, lanes = ny // 8, nz // 2
    assert lanes == 128
    dense = (rows, lanes)
    as_bf16 = lambda m: jnp.asarray(m.astype(ml_dtypes.bfloat16))
    py, pz = even_odd(prolong_matrix(ny)), prolong_matrix(nz)
    ry, rz = as_bf16(py.T), as_bf16(halves(pz))
    my, mz = as_bf16(even_odd(mean_matrix(ny)).T), as_bf16(halves(mean_matrix(nz)))
    ey, ez = as_bf16(py), as_bf16(halves(pz).transpose(0, 2, 1))
    vmem = pl.BlockSpec(memory_space=pltpu.VMEM)
    hbm = pl.BlockSpec(memory_space=pl.ANY)
    whole = lambda *s: pltpu.VMEM(s, F32)
    dma = lambda *s: pltpu.SemaphoreType.DMA(s)
    padded = (4, ny + 16, nz)
    kept = pl.pallas_call(
        functools.partial(smooth_kernel, n, ny, nz, min(16, n)),
        out_shape=(
            whole(*padded), whole(2, n + 2, *dense), pltpu.VMEM(ez.shape, BF16), pltpu.VMEM(ey.shape, BF16),
            pltpu.VMEM((n, 128), jnp.int32),
        ),
        in_specs=[hbm] * 10,
        out_specs=(vmem,) * 5,
        scratch_shapes=[
            pltpu.SMEM((n,), jnp.int32),
            whole(6, n, *dense), whole(n, *dense),
            pltpu.VMEM(ry.shape, BF16), pltpu.VMEM(rz.shape, BF16),
            pltpu.VMEM(my.shape, BF16), pltpu.VMEM(mz.shape, BF16),
            whole(n, *dense), whole(n + 2, *dense), whole(n, *dense), whole(n, *dense),
            whole(4, ny, nz), whole(4, ny, nz),
            whole(*padded), whole(*padded), whole(*padded),
            whole(4, ny, nz), whole(4, ny, nz), whole(4, ny, nz),
            whole(2, ny, nz), whole(3, ny, nz), whole(3, 2, ny, nz),
            whole(4, *dense),
            dma(10), dma(3, 2, CHUNKS), dma(3, 2, CHUNKS), dma(2), dma(2),
            dma(n), dma(n), dma(n), dma(n),
            pltpu.SemaphoreType.REGULAR(((n - 1).bit_length(),)),
        ],
        compiler_params=pltpu.CompilerParams(
            collective_id=0, has_side_effects=True, vmem_limit_bytes=28 * 2**20
        ),
        name="smooth",
    )(*(pltpu.with_memory_space_constraint(a, pltpu.HBM) for a in (source, guess, log_perm, owner, ry, rz, my, mz, ez, ey)))
    smooth, coarse, ez, ey, holder = [pltpu.with_memory_space_constraint(a, pltpu.VMEM) for a in kept]
    return pl.pallas_call(
        functools.partial(prolong_kernel, n),
        out_shape=(
            jax.ShapeDtypeStruct((4, ny, nz), F32),
            jax.ShapeDtypeStruct((1, cells), F32),
        ),
        in_specs=[vmem] * 5,
        out_specs=(hbm, hbm),
        scratch_shapes=[whole(4, ny, nz), whole(1, cells), dma(5)],
        compiler_params=pltpu.CompilerParams(vmem_limit_bytes=16 * 2**20),
        name="prolong",
    )(coarse, smooth, ez, ey, holder)


def solution(mesh):
    spec = P(("samples", "brick"), None, None)
    return jax.shard_map(
        functools.partial(local, mesh.shape["brick"]),
        mesh=mesh,
        in_specs=(spec, spec, spec, P()),
        out_specs=(spec, P(("samples", "brick"), None)),
        check_vma=False,
    )
```

```python
import functools

import jax
import jax.numpy as jnp
import ml_dtypes
import numpy as np
from jax import lax
from jax.experimental import pallas as pl
from jax.experimental.pallas import tpu as pltpu
from jax.sharding import PartitionSpec as P

SWEEPS = 8
CHUNKS = 8
FIRST = 4
MESH = pl.DeviceIdType.MESH
F32 = jnp.float32
BF16 = jnp.bfloat16


def prolong_matrix(n_fine):
    i = np.arange(n_fine)[:, None]
    j = np.arange(n_fine // 4)[None, :]
    base, offset = i // 4, i % 4
    own = np.where((offset == 0) | (offset == 3), 0.625, 0.875)
    side = np.where(offset < 2, -1, 1)
    return np.where(j == base, own, 0.0) + np.where(j == base + side, 1.0 - own, 0.0)


def mean_matrix(n_fine):
    i = np.arange(n_fine)[:, None]
    j = np.arange(n_fine // 4)[None, :]
    return np.where(j == i // 4, 1.0, 0.0)


def even_odd(m):
    return np.concatenate([m[:, 0::2], m[:, 1::2]], axis=1)


def halves(m):
    zero = np.zeros_like(m)
    return np.stack([np.concatenate([m, zero], 1), np.concatenate([zero, m], 1)])


def split(x):
    hi = x.astype(BF16)
    return hi, (x - hi.astype(F32)).astype(BF16)


def dot(a, b):
    return jnp.dot(a, b, preferred_element_type=F32)


def to_coarse(y_mat, z_mat, x):
    hi, lo = split(x)
    a = dot(y_mat, hi) + dot(y_mat, lo)
    hi, lo = split(a)
    h = a.shape[0] // 2
    return (
        dot(hi[:h], z_mat[0]) + dot(lo[:h], z_mat[0]) + dot(hi[h:], z_mat[1]) + dot(lo[h:], z_mat[1])
    )


def smooth_kernel(
    n, ny, nz, group,
    source_hbm, guess_hbm, logq_hbm, owner_hbm, y_hbm, z_hbm, ez_hbm, ey_hbm,
    U2, C, ez, ey, holder,
    owner, coef, scaled, ymat, zmat, all_q, q_pad, all_r, B, src, logq, K, U0, U1, D, W, N, F, X, H, part,
    local_sem, halo_send, first_recv, second_recv, part_send, part_recv, q_send, q_recv, r_send, r_recv, token_sem,
):
    me = lax.axis_index("brick")
    R = ny // CHUNKS
    half = n // 2
    has = (me > 0, me < n - 1)
    flag = [jnp.where(h, 1.0, 0.0).astype(F32) for h in has]
    far = lax.rem(me, 2)
    near_side = 1 - far
    sibling = me + 1 - 2 * far
    mine_at = (far, me // 2)
    neighbour = lambda side: me - 1 + 2 * side
    exists = lambda side: jnp.logical_and(neighbour(side) >= 0, neighbour(side) < n)

    loads = [
        pltpu.make_async_copy(logq_hbm, logq, local_sem.at[0]),
        pltpu.make_async_copy(guess_hbm, U0.at[:, pl.ds(8, ny)], local_sem.at[1]),
        pltpu.make_async_copy(source_hbm, src, local_sem.at[2]),
        pltpu.make_async_copy(y_hbm, ymat, local_sem.at[3]),
        pltpu.make_async_copy(z_hbm, zmat, local_sem.at[4]),
        pltpu.make_async_copy(ez_hbm, ez, local_sem.at[5]),
        pltpu.make_async_copy(ey_hbm, ey, local_sem.at[6]),
        pltpu.make_async_copy(owner_hbm, owner, local_sem.at[7]),
    ]

    def signal(sem, who):
        pl.semaphore_signal(sem, inc=1, device_id={"brick": who}, device_id_type=MESH)

    barrier = pltpu.get_barrier_semaphore()

    def greet(sem, distance):
        @pl.when(me >= distance)
        def _():
            signal(sem, me - distance)

        @pl.when(me + distance < n)
        def _():
            signal(sem, me + distance)

    def greeted(sem, distance):
        low = jnp.where(me >= distance, 1, 0)
        high = jnp.where(me + distance < n, 1, 0)
        pl.semaphore_wait(sem, low + high)

    distances = [2**k for k in range((n - 1).bit_length())]

    def relay(k):
        if k < len(distances):
            greeted(token_sem.at[k], distances[k])
        if k + 1 < len(distances):
            greet(token_sem.at[k + 1], distances[k + 1])

    greet(barrier, 1)
    for copy in loads:
        copy.start()

    zero_rows = jnp.zeros((8, nz), F32)
    for ref in (K, U0, U1, U2):
        for p in range(4):
            ref[p, 0:8] = zero_rows
            ref[p, ny + 8 : ny + 16] = zero_rows
    for side in range(2):

        @pl.when(jnp.logical_not(has[side]))
        def _():
            for which in range(3):
                H[which, side] = jnp.zeros((ny, nz), F32)

    greeted(barrier, 1)
    greet(token_sem.at[0], 1)

    def rows_at(c):
        return pl.ds(c * R if isinstance(c, int) else pl.multiple_of(c * R, R), R)

    def rows_in(c):
        return pl.ds(8 + c * R if isinstance(c, int) else pl.multiple_of(c * R, R) + 8, R)

    Q = ny // FIRST

    def send_first(side):
        for c in range(FIRST):
            rows = pl.ds(c * Q, Q)
            for which, ref in enumerate((logq_hbm, guess_hbm)):
                pltpu.make_async_remote_copy(
                    src_ref=ref.at[3 * side, rows],
                    dst_ref=H.at[which, 1 - side, rows],
                    send_sem=halo_send.at[side],
                    recv_sem=first_recv.at[1 - side, c],
                    device_id={"brick": neighbour(side)},
                    device_id_type=MESH,
                ).start()

    def first_in(side, c):
        ref = H.at[0:2, side, pl.ds(pl.multiple_of(c * Q, Q), Q)]
        return pltpu.make_async_remote_copy(
            src_ref=ref,
            dst_ref=ref,
            send_sem=halo_send.at[side],
            recv_sem=first_recv.at[side, c],
            device_id={"brick": neighbour(side)},
            device_id_type=MESH,
        )

    def second(side, c):
        return pltpu.make_async_remote_copy(
            src_ref=U1.at[3 * side, rows_in(c)],
            dst_ref=H.at[2, 1 - side, rows_at(c)],
            send_sem=halo_send.at[side],
            recv_sem=second_recv.at[1 - side, c],
            device_id={"brick": neighbour(side)},
            device_id_type=MESH,
        )

    def second_in(side, c):
        ref = H.at[2, side, rows_at(c)]
        return pltpu.make_async_remote_copy(
            src_ref=ref,
            dst_ref=ref,
            send_sem=halo_send.at[side],
            recv_sem=second_recv.at[side, c],
            device_id={"brick": neighbour(side)},
            device_id_type=MESH,
        )

    def halo_sent(side):
        ref = H.at[:, side]
        return pltpu.make_async_remote_copy(
            src_ref=ref,
            dst_ref=ref,
            send_sem=halo_send.at[side],
            recv_sem=first_recv.at[side, 0],
            device_id={"brick": neighbour(side)},
            device_id_type=MESH,
        )

    for side in (far, near_side):

        @pl.when(exists(side))
        def _():
            send_first(side)

    relay(0)

    lane = lax.broadcasted_iota(jnp.int32, (R, nz), 1)
    first, last = lane == 0, lane == nz - 1

    def middle(window):
        return window[8 : R + 8]

    def yz(window):
        center = middle(window)
        low = jnp.where(first, 0.0, pltpu.roll(center, 1, 1))
        high = jnp.where(last, 0.0, pltpu.roll(center, nz - 1, 1))
        return (window[7 : R + 7] + window[9 : R + 9]) + (low + high)

    def across(windows, p):
        total = yz(windows[p])
        if p > 0:
            total = total + middle(windows[p - 1])
        if p < 3:
            total = total + middle(windows[p + 1])
        return total

    loads[0].wait()

    def exps(c, _):
        for p in range(4):
            K[p, rows_in(c)] = jnp.exp(logq[p, rows_at(c)])
        return 0

    lax.fori_loop(0, CHUNKS, exps, 0)
    for copy in loads[1:]:
        copy.wait()
    relay(1)

    def windows(ref, c):
        at = pl.ds(pl.multiple_of(c * R, R), R + 16)
        return [ref[p, at] for p in range(4)]

    def nearby(u, k):
        uk = [a * b for a, b in zip(u, k)]
        return [0.5 * (middle(k[p]) * across(u, p) + across(uk, p)) for p in range(4)]

    def sweep_one(c, _):
        rows, at = rows_at(c), rows_in(c)
        u, k = windows(U0, c), windows(K, c)
        near = nearby(u, k)
        for p in range(4):
            d = 3.0 * middle(k[p]) + 0.5 * across(k, p)
            total = src[p, rows] + near[p]
            D[p, rows] = d
            if p in (0, 3):
                N[p, rows] = total
            else:
                w = 0.8 / d
                W[p, rows] = w
                U1[p, at] = 0.2 * middle(u[p]) + w * total
        return 0

    lax.fori_loop(0, CHUNKS, sweep_one, 0)

    all_q[mine_at] = to_coarse(
        ymat[0], zmat[0:2], (K[0, 8 : ny + 8] + K[1, 8 : ny + 8]) + (K[2, 8 : ny + 8] + K[3, 8 : ny + 8])
    ) * (1.0 / 64.0)
    for b in range(n):
        holder[b : b + 1] = jnp.full((1, 128), owner[b], jnp.int32)

    relay(2)

    def finish_one(c):
        rows, at = rows_at(c), rows_in(c)
        for side in range(2):

            @pl.when(has[side])
            def _():

                @pl.when(lax.rem(c, CHUNKS // FIRST) == 0)
                def _():
                    first_in(side, c // (CHUNKS // FIRST)).wait_recv()

        for side in range(2):
            p = 3 * side
            kh = jnp.exp(H[0, side, rows]) * flag[side]
            face = 0.5 * (K[p, at] + kh)
            d = D[p, rows] + 0.5 * kh
            w = 0.8 / d
            F[side, rows] = face
            D[p, rows] = d
            W[p, rows] = w
            U1[p, at] = 0.2 * U0[p, at] + w * (N[p, rows] + face * H[1, side, rows])
        for side in (far, near_side):

            @pl.when(exists(side))
            def _():
                second(side, c).start()

    def direct(ref, j, send, recv):
        return pltpu.make_async_remote_copy(
            src_ref=ref.at[mine_at],
            dst_ref=ref.at[mine_at],
            send_sem=send.at[1],
            recv_sem=recv,
            device_id={"brick": lax.rem(me + 2 * j, n)},
            device_id_type=MESH,
        )

    def to_sibling(ref, part_of, send, recv):
        return pltpu.make_async_remote_copy(
            src_ref=ref.at[part_of],
            dst_ref=ref.at[part_of],
            send_sem=send.at[0],
            recv_sem=recv,
            device_id={"brick": sibling},
            device_id_type=MESH,
        )

    def repeat(low, body):
        def step(j, _):
            body(j)
            return 0

        lax.fori_loop(low, half, step, 0)

    def from_sibling(ref, send, recv):
        to_sibling(ref, 1 - far, send, recv).wait_recv()

    def sent(ref, send, recv):
        for side, blocks in ((0, half), (1, half - 1)):
            part_of = ref.at[side, 0:blocks]
            pltpu.make_async_remote_copy(
                src_ref=part_of, dst_ref=part_of, send_sem=send.at[side], recv_sem=recv,
                device_id={"brick": sibling}, device_id_type=MESH,
            ).wait_send()

    def spread_q():
        repeat(1, lambda j: direct(all_q, j, q_send, q_recv.at[0]).start())

    def hand_on_q():
        ref = all_q.at[0, 0 : half - 1]
        pltpu.make_async_remote_copy(
            src_ref=ref, dst_ref=ref, send_sem=q_send.at[0], recv_sem=q_recv.at[0],
            device_id={"brick": sibling}, device_id_type=MESH,
        ).wait_recv()
        to_sibling(all_q, far, q_send, q_recv.at[1]).start()

    def r_place(j):
        return far, lax.rem(me // 2 + half - j, half)

    def spread_r():
        repeat(1, lambda j: direct(all_r, j, r_send, r_recv.at[me // 2]).start())
        to_sibling(all_r, mine_at, r_send, r_recv.at[half]).start()

    def hand_on_r():
        def step(j):
            place = r_place(j)
            to_sibling(all_r, place, r_send, r_recv.at[place[1]]).wait_recv()
            to_sibling(all_r, place, r_send, r_recv.at[half]).start()

        repeat(1, step)

    def sweep_two(c):
        rows, at = rows_at(c), rows_in(c)
        u = windows(U1, c)
        near = nearby(u, windows(K, c))
        for p in range(4):
            total = src[p, rows] + near[p]
            if p in (0, 3):
                N[p, rows] = total
            else:
                U2[p, at] = 0.2 * middle(u[p]) + W[p, rows] * total

    relays = range(3, len(distances))

    def first_stage(c, _):
        @pl.when(c < CHUNKS)
        def _():
            finish_one(c)

        for k in relays:

            @pl.when(c == CHUNKS - 1 - (relays[-1] - k))
            def _():
                relay(k)

        @pl.when(c == CHUNKS - 1)
        def _():
            spread_q()

        @pl.when(c > 0)
        def _():
            sweep_two(c - 1)

        return 0

    lax.fori_loop(0, CHUNKS + 1, first_stage, 0)

    def finish_two(c):
        rows, at = rows_at(c), rows_in(c)
        for side in range(2):

            @pl.when(has[side])
            def _():
                second_in(side, c).wait_recv()

        for side in range(2):
            p = 3 * side
            total = N[p, rows] + F[side, rows] * H[2, side, rows]
            U2[p, at] = 0.2 * U1[p, at] + W[p, rows] * total

    def residual(c):
        rows = rows_at(c)
        u = windows(U2, c)
        near = nearby(u, windows(K, c))
        r = [src[p, rows] - D[p, rows] * middle(u[p]) + near[p] for p in range(4)]
        flo = flag[0] * F[0, rows] * middle(u[0])
        fhi = flag[1] * F[1, rows] * middle(u[3])
        X[0, rows] = 0.625 * flo + 0.375 * r[0] + 0.125 * r[1]
        X[1, rows] = (0.375 * flo + 0.625 * r[0] + 0.875 * r[1]) + (0.375 * fhi + 0.625 * r[3] + 0.875 * r[2])
        X[2, rows] = 0.625 * fhi + 0.375 * r[3] + 0.125 * r[2]

    def second_stage(c, _):
        @pl.when(c < CHUNKS)
        def _():
            finish_two(c)

        @pl.when(c > 0)
        def _():
            residual(c - 1)

        return 0

    lax.fori_loop(0, CHUNKS + 1, second_stage, 0)

    def partial(side):
        return pltpu.make_async_remote_copy(
            src_ref=part.at[side],
            dst_ref=part.at[3 - side],
            send_sem=part_send.at[side],
            recv_sem=part_recv.at[1 - side],
            device_id={"brick": neighbour(side)},
            device_id_type=MESH,
        )

    def partial_in(side):
        return pltpu.make_async_remote_copy(
            src_ref=part.at[2 + side],
            dst_ref=part.at[2 + side],
            send_sem=part_send.at[side],
            recv_sem=part_recv.at[side],
            device_id={"brick": neighbour(side)},
            device_id_type=MESH,
        )

    for side in range(2):
        part[side] = to_coarse(ymat[1], zmat[2:4], X[2 * side])

    for side in range(2):

        @pl.when(has[side])
        def _():
            partial(side).start()

        @pl.when(jnp.logical_not(has[side]))
        def _():
            part[2 + side] = jnp.zeros(part.shape[1:], F32)

    mine = to_coarse(ymat[1], zmat[2:4], X[1])
    hand_on_q()
    for side in range(2):

        @pl.when(has[side])
        def _():
            partial_in(side).wait_recv()

    all_r[mine_at] = (mine + (part[2] + part[3])) * (1.0 / 64.0)
    spread_r()

    from_sibling(all_q, q_send, q_recv.at[1])
    coarse_coefficients(n, min(8, n), all_q, q_pad, coef, scaled)
    hand_on_r()

    rows, lanes = all_r.shape[2:]
    shifts, _ = coarse_shifts((group, rows, lanes))
    edge = jnp.zeros((rows, lanes), F32)
    for slot in range(2):
        C[slot, 0] = edge
        C[slot, n + 1] = edge
    from_sibling(all_r, r_send, r_recv.at[half])
    for b in range(n):
        scaled_rhs = all_r[b % 2, b // 2] * scaled[b]
        B[b] = scaled_rhs
        C[0, b + 1] = scaled_rhs

    for sweep in range(SWEEPS - 1):
        now, later = sweep % 2, 1 - sweep % 2

        def step(g, _):
            at = pl.multiple_of(g * group, group)
            c = C[now, pl.ds(at + 1, group)]
            near = (C[now, pl.ds(at, group)], C[now, pl.ds(at + 2, group)]) + shifts(c)
            terms = [coef[k, pl.ds(at, group)] * v for k, v in enumerate(near)]
            total = B[pl.ds(at, group)] + 0.2 * c
            total = (total + (terms[0] + terms[1])) + ((terms[2] + terms[3]) + (terms[4] + terms[5]))
            C[later, pl.ds(at + 1, group)] = total
            return 0

        lax.fori_loop(0, n // group, step, 0)

    for side in range(2):

        @pl.when(has[side])
        def _():
            halo_sent(side).wait_send()
            partial(side).wait_send()

    sent(all_q, q_send, q_recv.at[0])
    sent(all_r, r_send, r_recv.at[0])


def coarse_shifts(shape):
    rows, lanes = shape[1:]
    cz = lanes // 2
    row = lax.broadcasted_iota(jnp.int32, shape, 1)
    lane = lax.broadcasted_iota(jnp.int32, shape, 2)
    low_half = lane < cz
    z = jnp.where(low_half, lane, lane - cz)
    outside = (
        (row == 0) & low_half,
        (row == rows - 1) & jnp.logical_not(low_half),
        z == 0,
        z == cz - 1,
    )

    def shifts(c):
        swapped = pltpu.roll(c, cz, 2)
        y_low = jnp.where(low_half, pltpu.roll(swapped, 1, 1), swapped)
        y_high = jnp.where(low_half, swapped, pltpu.roll(swapped, rows - 1, 1))
        return y_low, y_high, pltpu.roll(c, 1, 2), pltpu.roll(c, lanes - 1, 2)

    return shifts, outside


def coarse_coefficients(n, group, perm, q_pad, coef, scaled):
    rows, lanes = perm.shape[2:]
    shifts, outside = coarse_shifts((group, rows, lanes))
    edge = jnp.zeros((rows, lanes), F32)
    q_pad[0] = edge
    q_pad[n + 1] = edge
    for b in range(n):
        q_pad[b + 1] = perm[b % 2, b // 2]

    def prepare(g, _):
        at = pl.multiple_of(g * group, group)
        q = q_pad[pl.ds(at + 1, group)]
        near = [q_pad[pl.ds(at, group)], q_pad[pl.ds(at + 2, group)]]
        near += [jnp.where(out, 0.0, v) for out, v in zip(outside, shifts(q))]
        faces = [0.5 * (q + v) for v in near]
        diagonal = ((faces[0] + faces[1]) + (faces[2] + faces[3])) + (faces[4] + faces[5])
        scale = 0.8 / diagonal
        for k, out in enumerate((None, None) + outside):
            f = faces[k] * scale
            coef[k, pl.ds(at, group)] = f if out is None else jnp.where(out, 0.0, f)
        scaled[pl.ds(at, group)] = 16.0 * scale
        return 0

    lax.fori_loop(0, n // group, prepare, 0)


def prolong_kernel(n, C, U2, ez, ey, holder, corrected_hbm, held_hbm, corrected, held, sem):
    me = lax.axis_index("brick")
    rows, lanes = C.shape[2:]
    ny = corrected.shape[1]
    final = (SWEEPS - 1) % 2
    below, mid, above = C[final, me], C[final, me + 1], C[final, me + 2]
    planes = jnp.concatenate(
        [
            0.625 * mid + 0.375 * below,
            0.875 * mid + 0.125 * below,
            0.875 * mid + 0.125 * above,
            0.625 * mid + 0.375 * above,
        ],
        axis=0,
    )
    hi, lo = split(planes)
    even = dot(hi, ez[0]) + dot(lo, ez[0])
    odd = dot(hi, ez[1]) + dot(lo, ez[1])
    copies = []
    for p in range(4):
        both = jnp.concatenate(
            [even[p * rows : (p + 1) * rows], odd[p * rows : (p + 1) * rows]], axis=0
        )
        hi, lo = split(both)
        corrected[p] = U2[p, 8 : ny + 8] + (dot(ey[...], hi) + dot(ey[...], lo))
        copies.append(pltpu.make_async_copy(corrected.at[p], corrected_hbm.at[p], sem.at[p]))
        copies[p].start()

    mine = jnp.zeros((rows, lanes), F32)
    for b in range(n):
        mine = jnp.where(holder[b : b + 1] == me, C[final, b + 1], mine)
    for r in range(rows):
        held[0:1, r * lanes : (r + 1) * lanes] = mine[r : r + 1]
    copies.append(pltpu.make_async_copy(held, held_hbm, sem.at[4]))
    copies[4].start()
    for copy in copies:
        copy.wait()


def local(n, source, guess, log_perm, owner):
    planes, ny, nz = source.shape
    assert planes == 4 and n % 2 == 0
    cells = (ny // 4) * (nz // 4)
    rows, lanes = ny // 8, nz // 2
    assert lanes == 128
    dense = (rows, lanes)
    as_bf16 = lambda m: jnp.asarray(m.astype(ml_dtypes.bfloat16))
    py, pz = even_odd(prolong_matrix(ny)), prolong_matrix(nz)
    ymat = as_bf16(np.stack([even_odd(mean_matrix(ny)).T, py.T]))
    zmat = as_bf16(np.concatenate([halves(mean_matrix(nz)), halves(pz)]))
    ey, ez = as_bf16(py), as_bf16(halves(pz).transpose(0, 2, 1))
    vmem = pl.BlockSpec(memory_space=pltpu.VMEM)
    hbm = pl.BlockSpec(memory_space=pl.ANY)
    whole = lambda *s: pltpu.VMEM(s, F32)
    dma = lambda *s: pltpu.SemaphoreType.DMA(s)
    padded = (4, ny + 16, nz)
    kept = pl.pallas_call(
        functools.partial(smooth_kernel, n, ny, nz, min(16, n)),
        out_shape=(
            whole(*padded), whole(2, n + 2, *dense), pltpu.VMEM(ez.shape, BF16), pltpu.VMEM(ey.shape, BF16),
            pltpu.VMEM((n, 128), jnp.int32),
        ),
        in_specs=[hbm] * 8,
        out_specs=(vmem,) * 5,
        scratch_shapes=[
            pltpu.SMEM((n,), jnp.int32),
            whole(6, n, *dense), whole(n, *dense),
            pltpu.VMEM(ymat.shape, BF16), pltpu.VMEM(zmat.shape, BF16),
            whole(2, n // 2, *dense), whole(n + 2, *dense), whole(2, n // 2, *dense), whole(n, *dense),
            whole(4, ny, nz), whole(4, ny, nz),
            whole(*padded), whole(*padded), whole(*padded),
            whole(4, ny, nz), whole(4, ny, nz), whole(4, ny, nz),
            whole(2, ny, nz), whole(3, ny, nz), whole(3, 2, ny, nz),
            whole(4, *dense),
            dma(8), dma(2), dma(2, FIRST), dma(2, CHUNKS), dma(2), dma(2),
            dma(2), dma(2), dma(2), dma(n // 2 + 1),
            pltpu.SemaphoreType.REGULAR(((n - 1).bit_length(),)),
        ],
        compiler_params=pltpu.CompilerParams(
            collective_id=0, has_side_effects=True, vmem_limit_bytes=28 * 2**20
        ),
        name="smooth",
    )(*(pltpu.with_memory_space_constraint(a, pltpu.HBM) for a in (source, guess, log_perm, owner, ymat, zmat, ez, ey)))
    smooth, coarse, ez, ey, holder = [pltpu.with_memory_space_constraint(a, pltpu.VMEM) for a in kept]
    return pl.pallas_call(
        functools.partial(prolong_kernel, n),
        out_shape=(
            jax.ShapeDtypeStruct((4, ny, nz), F32),
            jax.ShapeDtypeStruct((1, cells), F32),
        ),
        in_specs=[vmem] * 5,
        out_specs=(hbm, hbm),
        scratch_shapes=[whole(4, ny, nz), whole(1, cells), dma(5)],
        compiler_params=pltpu.CompilerParams(vmem_limit_bytes=16 * 2**20),
        name="prolong",
    )(coarse, smooth, ez, ey, holder)


def solution(mesh):
    spec = P(("samples", "brick"), None, None)
    return jax.shard_map(
        functools.partial(local, mesh.shape["brick"]),
        mesh=mesh,
        in_specs=(spec, spec, spec, P()),
        out_specs=(spec, P(("samples", "brick"), None)),
        check_vma=False,
    )
```

```python
import functools

import jax
import jax.numpy as jnp
import ml_dtypes
import numpy as np
from jax import lax
from jax.experimental import pallas as pl
from jax.experimental.pallas import tpu as pltpu
from jax.sharding import PartitionSpec as P

SWEEPS = 8
CHUNKS = 8
FIRST = 4
MESH = pl.DeviceIdType.MESH
F32 = jnp.float32
BF16 = jnp.bfloat16


def prolong_matrix(n_fine):
    i = np.arange(n_fine)[:, None]
    j = np.arange(n_fine // 4)[None, :]
    base, offset = i // 4, i % 4
    own = np.where((offset == 0) | (offset == 3), 0.625, 0.875)
    side = np.where(offset < 2, -1, 1)
    return np.where(j == base, own, 0.0) + np.where(j == base + side, 1.0 - own, 0.0)


def mean_matrix(n_fine):
    i = np.arange(n_fine)[:, None]
    j = np.arange(n_fine // 4)[None, :]
    return np.where(j == i // 4, 1.0, 0.0)


def even_odd(m):
    return np.concatenate([m[:, 0::2], m[:, 1::2]], axis=1)


def halves(m):
    zero = np.zeros_like(m)
    return np.stack([np.concatenate([m, zero], 1), np.concatenate([zero, m], 1)])


def split(x):
    hi = x.astype(BF16)
    return hi, (x - hi.astype(F32)).astype(BF16)


def dot(a, b):
    return jnp.dot(a, b, preferred_element_type=F32)


def to_coarse(y_mat, z_mat, x):
    hi, lo = split(x)
    a = dot(y_mat, hi) + dot(y_mat, lo)
    hi, lo = split(a)
    h = a.shape[0] // 2
    return (
        dot(hi[:h], z_mat[0]) + dot(lo[:h], z_mat[0]) + dot(hi[h:], z_mat[1]) + dot(lo[h:], z_mat[1])
    )


def smooth_kernel(
    n, ny, nz, group,
    source_hbm, guess_hbm, logq_hbm, owner_hbm, y_hbm, z_hbm, ez_hbm, ey_hbm,
    U2, C, ez, ey, holder,
    owner, coef, scaled, ymat, zmat, all_q, q_pad, all_p, all_r, B, src, logq, K, U0, U1, D, W, N, F, X, H, part,
    local_sem, halo_send, first_recv, second_recv, part_sem, q_send, q_recv, p_send, p_recv, r_send, r_recv, token_sem,
):
    me = lax.axis_index("brick")
    R = ny // CHUNKS
    half = n // 2
    has = (me > 0, me < n - 1)
    flag = [jnp.where(h, 1.0, 0.0).astype(F32) for h in has]
    far = lax.rem(me, 2)
    near_side = 1 - far
    sibling = me + 1 - 2 * far
    mine_at = (far, me // 2)
    neighbour = lambda side: me - 1 + 2 * side
    exists = lambda side: jnp.logical_and(neighbour(side) >= 0, neighbour(side) < n)

    loads = [
        pltpu.make_async_copy(logq_hbm, logq, local_sem.at[0]),
        pltpu.make_async_copy(guess_hbm, U0.at[:, pl.ds(8, ny)], local_sem.at[1]),
        pltpu.make_async_copy(source_hbm, src, local_sem.at[2]),
        pltpu.make_async_copy(y_hbm, ymat, local_sem.at[3]),
        pltpu.make_async_copy(z_hbm, zmat, local_sem.at[4]),
        pltpu.make_async_copy(ez_hbm, ez, local_sem.at[5]),
        pltpu.make_async_copy(ey_hbm, ey, local_sem.at[6]),
        pltpu.make_async_copy(owner_hbm, owner, local_sem.at[7]),
    ]

    def signal(sem, who):
        pl.semaphore_signal(sem, inc=1, device_id={"brick": who}, device_id_type=MESH)

    barrier = pltpu.get_barrier_semaphore()

    def greet(sem, distance):
        @pl.when(me >= distance)
        def _():
            signal(sem, me - distance)

        @pl.when(me + distance < n)
        def _():
            signal(sem, me + distance)

    def greeted(sem, distance):
        low = jnp.where(me >= distance, 1, 0)
        high = jnp.where(me + distance < n, 1, 0)
        pl.semaphore_wait(sem, low + high)

    distances = [2**k for k in range((n - 1).bit_length())]

    def relay(k):
        if k < len(distances):
            greeted(token_sem.at[k], distances[k])
        if k + 1 < len(distances):
            greet(token_sem.at[k + 1], distances[k + 1])

    greet(barrier, 1)
    for copy in loads:
        copy.start()

    zero_rows = jnp.zeros((8, nz), F32)
    for ref in (K, U0, U1, U2):
        for p in range(4):
            ref[p, 0:8] = zero_rows
            ref[p, ny + 8 : ny + 16] = zero_rows
    for side in range(2):

        @pl.when(jnp.logical_not(has[side]))
        def _():
            for which in range(3):
                H[which, side] = jnp.zeros((ny, nz), F32)

    greeted(barrier, 1)
    greet(token_sem.at[0], 1)

    def rows_at(c):
        return pl.ds(c * R if isinstance(c, int) else pl.multiple_of(c * R, R), R)

    def rows_in(c):
        return pl.ds(8 + c * R if isinstance(c, int) else pl.multiple_of(c * R, R) + 8, R)

    Q = ny // FIRST

    def send_first(side):
        for c in range(FIRST):
            rows = pl.ds(c * Q, Q)
            for which, ref in enumerate((logq_hbm, guess_hbm)):
                pltpu.make_async_remote_copy(
                    src_ref=ref.at[3 * side, rows],
                    dst_ref=H.at[which, 1 - side, rows],
                    send_sem=halo_send.at[side],
                    recv_sem=first_recv.at[1 - side, c],
                    device_id={"brick": neighbour(side)},
                    device_id_type=MESH,
                ).start()

    def first_in(side, c):
        ref = H.at[0:2, side, pl.ds(pl.multiple_of(c * Q, Q), Q)]
        return pltpu.make_async_remote_copy(
            src_ref=ref,
            dst_ref=ref,
            send_sem=halo_send.at[side],
            recv_sem=first_recv.at[side, c],
            device_id={"brick": neighbour(side)},
            device_id_type=MESH,
        )

    def second(side, c):
        return pltpu.make_async_remote_copy(
            src_ref=U1.at[3 * side, rows_in(c)],
            dst_ref=H.at[2, 1 - side, rows_at(c)],
            send_sem=halo_send.at[side],
            recv_sem=second_recv.at[1 - side, c],
            device_id={"brick": neighbour(side)},
            device_id_type=MESH,
        )

    def second_in(side, c):
        ref = H.at[2, side, rows_at(c)]
        return pltpu.make_async_remote_copy(
            src_ref=ref,
            dst_ref=ref,
            send_sem=halo_send.at[side],
            recv_sem=second_recv.at[side, c],
            device_id={"brick": neighbour(side)},
            device_id_type=MESH,
        )

    def halo_sent(side):
        ref = H.at[:, side]
        return pltpu.make_async_remote_copy(
            src_ref=ref,
            dst_ref=ref,
            send_sem=halo_send.at[side],
            recv_sem=first_recv.at[side, 0],
            device_id={"brick": neighbour(side)},
            device_id_type=MESH,
        )

    for side in (far, near_side):

        @pl.when(exists(side))
        def _():
            send_first(side)

    relay(0)

    lane = lax.broadcasted_iota(jnp.int32, (R, nz), 1)
    first, last = lane == 0, lane == nz - 1

    def middle(window):
        return window[8 : R + 8]

    def yz(window):
        center = middle(window)
        low = jnp.where(first, 0.0, pltpu.roll(center, 1, 1))
        high = jnp.where(last, 0.0, pltpu.roll(center, nz - 1, 1))
        return (window[7 : R + 7] + window[9 : R + 9]) + (low + high)

    def across(windows, p):
        total = yz(windows[p])
        if p > 0:
            total = total + middle(windows[p - 1])
        if p < 3:
            total = total + middle(windows[p + 1])
        return total

    loads[0].wait()

    def exps(c, _):
        for p in range(4):
            K[p, rows_in(c)] = jnp.exp(logq[p, rows_at(c)])
        return 0

    lax.fori_loop(0, CHUNKS, exps, 0)
    for copy in loads[1:]:
        copy.wait()
    relay(1)

    def windows(ref, c):
        at = pl.ds(pl.multiple_of(c * R, R), R + 16)
        return [ref[p, at] for p in range(4)]

    def nearby(u, k):
        uk = [a * b for a, b in zip(u, k)]
        return [0.5 * (middle(k[p]) * across(u, p) + across(uk, p)) for p in range(4)]

    def sweep_one(c, _):
        rows, at = rows_at(c), rows_in(c)
        u, k = windows(U0, c), windows(K, c)
        near = nearby(u, k)
        for p in range(4):
            d = 3.0 * middle(k[p]) + 0.5 * across(k, p)
            total = src[p, rows] + near[p]
            D[p, rows] = d
            if p in (0, 3):
                N[p, rows] = total
            else:
                w = 0.8 / d
                W[p, rows] = w
                U1[p, at] = 0.2 * middle(u[p]) + w * total
        return 0

    lax.fori_loop(0, CHUNKS, sweep_one, 0)

    all_q[mine_at] = to_coarse(
        ymat[0], zmat[0:2], (K[0, 8 : ny + 8] + K[1, 8 : ny + 8]) + (K[2, 8 : ny + 8] + K[3, 8 : ny + 8])
    ) * (1.0 / 64.0)
    for b in range(n):
        holder[b : b + 1] = jnp.full((1, 128), owner[b], jnp.int32)

    relay(2)

    def finish_one(c):
        rows, at = rows_at(c), rows_in(c)
        for side in range(2):

            @pl.when(has[side])
            def _():

                @pl.when(lax.rem(c, CHUNKS // FIRST) == 0)
                def _():
                    first_in(side, c // (CHUNKS // FIRST)).wait_recv()

        for side in range(2):
            p = 3 * side
            kh = jnp.exp(H[0, side, rows]) * flag[side]
            face = 0.5 * (K[p, at] + kh)
            d = D[p, rows] + 0.5 * kh
            w = 0.8 / d
            F[side, rows] = face
            D[p, rows] = d
            W[p, rows] = w
            U1[p, at] = 0.2 * U0[p, at] + w * (N[p, rows] + face * H[1, side, rows])
        for side in (far, near_side):

            @pl.when(exists(side))
            def _():
                second(side, c).start()

    def to_sibling(ref, part_of, send, recv):
        return pltpu.make_async_remote_copy(
            src_ref=ref.at[part_of],
            dst_ref=ref.at[part_of],
            send_sem=send.at[0],
            recv_sem=recv,
            device_id={"brick": sibling},
            device_id_type=MESH,
        )

    def others(body):
        def step(j, _):
            body(j + jnp.where(j >= me // 2, 1, 0))
            return 0

        lax.fori_loop(0, half - 1, step, 0)

    def spread(ref, send, recv):
        def step(k):
            pltpu.make_async_remote_copy(
                src_ref=ref.at[mine_at],
                dst_ref=ref.at[mine_at],
                send_sem=send.at[1],
                recv_sem=recv,
                device_id={"brick": 2 * k + far},
                device_id_type=MESH,
            ).start()

        others(step)

    def from_sibling(ref, send, recv):
        to_sibling(ref, 1 - far, send, recv).wait_recv()

    def hand_on(ref, send, recv):
        to_sibling(ref, (0, pl.ds(0, half - 1)), send, recv.at[0]).wait_recv()
        to_sibling(ref, far, send, recv.at[1]).start()

    def hand_on_each(ref, send, recv):
        def step(k):
            to_sibling(ref, (far, k), send, recv.at[k]).wait_recv()
            to_sibling(ref, (far, k), send, recv.at[half]).start()

        others(step)

    def sent(ref, send, recv):
        for kind, blocks in ((0, half), (1, half - 1)):
            block = ref.at[kind, 0:blocks]
            pltpu.make_async_remote_copy(
                src_ref=block, dst_ref=block, send_sem=send.at[kind], recv_sem=recv,
                device_id={"brick": sibling}, device_id_type=MESH,
            ).wait_send()

    def sweep_two(c):
        rows, at = rows_at(c), rows_in(c)
        u = windows(U1, c)
        near = nearby(u, windows(K, c))
        for p in range(4):
            total = src[p, rows] + near[p]
            if p in (0, 3):
                N[p, rows] = total
            else:
                U2[p, at] = 0.2 * middle(u[p]) + W[p, rows] * total

    relays = range(3, len(distances))

    def first_stage(c, _):
        @pl.when(c < CHUNKS)
        def _():
            finish_one(c)

        for k in relays:

            @pl.when(c == CHUNKS - 1 - (relays[-1] - k))
            def _():
                relay(k)

        @pl.when(c == CHUNKS - 1)
        def _():
            spread(all_q, q_send, q_recv.at[0])

        @pl.when(c > 0)
        def _():
            sweep_two(c - 1)

        return 0

    lax.fori_loop(0, CHUNKS + 1, first_stage, 0)

    def finish_two(c):
        rows, at = rows_at(c), rows_in(c)
        for side in range(2):

            @pl.when(has[side])
            def _():
                second_in(side, c).wait_recv()

        for side in range(2):
            p = 3 * side
            total = N[p, rows] + F[side, rows] * H[2, side, rows]
            U2[p, at] = 0.2 * U1[p, at] + W[p, rows] * total

    def residual(c):
        rows = rows_at(c)
        u = windows(U2, c)
        near = nearby(u, windows(K, c))
        r = [src[p, rows] - D[p, rows] * middle(u[p]) + near[p] for p in range(4)]
        flo = flag[0] * F[0, rows] * middle(u[0])
        fhi = flag[1] * F[1, rows] * middle(u[3])
        X[0, rows] = 0.625 * flo + 0.375 * r[0] + 0.125 * r[1]
        X[1, rows] = (0.375 * flo + 0.625 * r[0] + 0.875 * r[1]) + (0.375 * fhi + 0.625 * r[3] + 0.875 * r[2])
        X[2, rows] = 0.625 * fhi + 0.375 * r[3] + 0.125 * r[2]

    def second_stage(c, _):
        @pl.when(c < CHUNKS)
        def _():
            finish_two(c)

        @pl.when(c > 0)
        def _():
            residual(c - 1)

        return 0

    lax.fori_loop(0, CHUNKS + 1, second_stage, 0)

    restrict = lambda k: to_coarse(ymat[1], zmat[2:4], X[k])
    all_p[mine_at] = restrict(2 * far)
    spread(all_p, p_send, p_recv.at[0])

    part[0] = restrict(2 * near_side)
    swap = pltpu.make_async_remote_copy(
        src_ref=part.at[0],
        dst_ref=part.at[1],
        send_sem=part_sem.at[0],
        recv_sem=part_sem.at[1],
        device_id={"brick": sibling},
        device_id_type=MESH,
    )
    swap.start()
    mine = restrict(1)
    hand_on(all_q, q_send, q_recv)
    swap.wait_recv()
    all_r[mine_at] = mine + part[1]
    spread(all_r, r_send, r_recv.at[me // 2])
    to_sibling(all_r, mine_at, r_send, r_recv.at[half]).start()

    from_sibling(all_q, q_send, q_recv.at[1])
    coarse_coefficients(n, min(8, n), all_q, q_pad, coef, scaled)
    hand_on(all_p, p_send, p_recv)
    hand_on_each(all_r, r_send, r_recv)

    rows, lanes = all_r.shape[2:]
    shifts, _ = coarse_shifts((group, rows, lanes))
    edge = jnp.zeros((rows, lanes), F32)
    for slot in range(2):
        C[slot, 0] = edge
        C[slot, n + 1] = edge
    from_sibling(all_p, p_send, p_recv.at[1])
    from_sibling(all_r, r_send, r_recv.at[half])
    for b in range(n):
        r = all_r[b % 2, b // 2]
        if 0 < b < n - 1:
            r = r + all_p[1 - b % 2, b // 2 - 1 + 2 * (b % 2)]
        scaled_rhs = r * scaled[b]
        B[b] = scaled_rhs
        C[0, b + 1] = scaled_rhs

    for sweep in range(SWEEPS - 1):
        now, later = sweep % 2, 1 - sweep % 2

        def step(g, _):
            at = pl.multiple_of(g * group, group)
            c = C[now, pl.ds(at + 1, group)]
            near = (C[now, pl.ds(at, group)], C[now, pl.ds(at + 2, group)]) + shifts(c)
            terms = [coef[k, pl.ds(at, group)] * v for k, v in enumerate(near)]
            total = B[pl.ds(at, group)] + 0.2 * c
            total = (total + (terms[0] + terms[1])) + ((terms[2] + terms[3]) + (terms[4] + terms[5]))
            C[later, pl.ds(at + 1, group)] = total
            return 0

        lax.fori_loop(0, n // group, step, 0)

    for side in range(2):

        @pl.when(has[side])
        def _():
            halo_sent(side).wait_send()

    swap.wait_send()
    sent(all_q, q_send, q_recv.at[0])
    sent(all_p, p_send, p_recv.at[0])
    sent(all_r, r_send, r_recv.at[0])


def coarse_shifts(shape):
    rows, lanes = shape[1:]
    cz = lanes // 2
    row = lax.broadcasted_iota(jnp.int32, shape, 1)
    lane = lax.broadcasted_iota(jnp.int32, shape, 2)
    low_half = lane < cz
    z = jnp.where(low_half, lane, lane - cz)
    outside = (
        (row == 0) & low_half,
        (row == rows - 1) & jnp.logical_not(low_half),
        z == 0,
        z == cz - 1,
    )

    def shifts(c):
        swapped = pltpu.roll(c, cz, 2)
        y_low = jnp.where(low_half, pltpu.roll(swapped, 1, 1), swapped)
        y_high = jnp.where(low_half, swapped, pltpu.roll(swapped, rows - 1, 1))
        return y_low, y_high, pltpu.roll(c, 1, 2), pltpu.roll(c, lanes - 1, 2)

    return shifts, outside


def coarse_coefficients(n, group, perm, q_pad, coef, scaled):
    rows, lanes = perm.shape[2:]
    shifts, outside = coarse_shifts((group, rows, lanes))
    edge = jnp.zeros((rows, lanes), F32)
    q_pad[0] = edge
    q_pad[n + 1] = edge
    for b in range(n):
        q_pad[b + 1] = perm[b % 2, b // 2]

    def prepare(g, _):
        at = pl.multiple_of(g * group, group)
        q = q_pad[pl.ds(at + 1, group)]
        near = [q_pad[pl.ds(at, group)], q_pad[pl.ds(at + 2, group)]]
        near += [jnp.where(out, 0.0, v) for out, v in zip(outside, shifts(q))]
        faces = [0.5 * (q + v) for v in near]
        diagonal = ((faces[0] + faces[1]) + (faces[2] + faces[3])) + (faces[4] + faces[5])
        scale = 0.8 / diagonal
        for k, out in enumerate((None, None) + outside):
            f = faces[k] * scale
            coef[k, pl.ds(at, group)] = f if out is None else jnp.where(out, 0.0, f)
        scaled[pl.ds(at, group)] = (16.0 / 64.0) * scale
        return 0

    lax.fori_loop(0, n // group, prepare, 0)


def prolong_kernel(n, C, U2, ez, ey, holder, corrected_hbm, held_hbm, corrected, held, sem):
    me = lax.axis_index("brick")
    rows, lanes = C.shape[2:]
    ny = corrected.shape[1]
    final = (SWEEPS - 1) % 2
    below, mid, above = C[final, me], C[final, me + 1], C[final, me + 2]
    planes = jnp.concatenate(
        [
            0.625 * mid + 0.375 * below,
            0.875 * mid + 0.125 * below,
            0.875 * mid + 0.125 * above,
            0.625 * mid + 0.375 * above,
        ],
        axis=0,
    )
    hi, lo = split(planes)
    even = dot(hi, ez[0]) + dot(lo, ez[0])
    odd = dot(hi, ez[1]) + dot(lo, ez[1])
    copies = []
    for p in range(4):
        both = jnp.concatenate(
            [even[p * rows : (p + 1) * rows], odd[p * rows : (p + 1) * rows]], axis=0
        )
        hi, lo = split(both)
        corrected[p] = U2[p, 8 : ny + 8] + (dot(ey[...], hi) + dot(ey[...], lo))
        copies.append(pltpu.make_async_copy(corrected.at[p], corrected_hbm.at[p], sem.at[p]))
        copies[p].start()

    mine = jnp.zeros((rows, lanes), F32)
    for b in range(n):
        mine = jnp.where(holder[b : b + 1] == me, C[final, b + 1], mine)
    for r in range(rows):
        held[0:1, r * lanes : (r + 1) * lanes] = mine[r : r + 1]
    copies.append(pltpu.make_async_copy(held, held_hbm, sem.at[4]))
    copies[4].start()
    for copy in copies:
        copy.wait()


def local(n, source, guess, log_perm, owner):
    planes, ny, nz = source.shape
    assert planes == 4 and n % 2 == 0
    cells = (ny // 4) * (nz // 4)
    rows, lanes = ny // 8, nz // 2
    assert lanes == 128
    dense = (rows, lanes)
    as_bf16 = lambda m: jnp.asarray(m.astype(ml_dtypes.bfloat16))
    py, pz = even_odd(prolong_matrix(ny)), prolong_matrix(nz)
    ymat = as_bf16(np.stack([even_odd(mean_matrix(ny)).T, py.T]))
    zmat = as_bf16(np.concatenate([halves(mean_matrix(nz)), halves(pz)]))
    ey, ez = as_bf16(py), as_bf16(halves(pz).transpose(0, 2, 1))
    vmem = pl.BlockSpec(memory_space=pltpu.VMEM)
    hbm = pl.BlockSpec(memory_space=pl.ANY)
    whole = lambda *s: pltpu.VMEM(s, F32)
    dma = lambda *s: pltpu.SemaphoreType.DMA(s)
    padded = (4, ny + 16, nz)
    kept = pl.pallas_call(
        functools.partial(smooth_kernel, n, ny, nz, min(16, n)),
        out_shape=(
            whole(*padded), whole(2, n + 2, *dense), pltpu.VMEM(ez.shape, BF16), pltpu.VMEM(ey.shape, BF16),
            pltpu.VMEM((n, 128), jnp.int32),
        ),
        in_specs=[hbm] * 8,
        out_specs=(vmem,) * 5,
        scratch_shapes=[
            pltpu.SMEM((n,), jnp.int32),
            whole(6, n, *dense), whole(n, *dense),
            pltpu.VMEM(ymat.shape, BF16), pltpu.VMEM(zmat.shape, BF16),
            whole(2, n // 2, *dense), whole(n + 2, *dense), whole(2, n // 2, *dense), whole(2, n // 2, *dense), whole(n, *dense),
            whole(4, ny, nz), whole(4, ny, nz),
            whole(*padded), whole(*padded), whole(*padded),
            whole(4, ny, nz), whole(4, ny, nz), whole(4, ny, nz),
            whole(2, ny, nz), whole(3, ny, nz), whole(3, 2, ny, nz),
            whole(2, *dense),
            dma(8), dma(2), dma(2, FIRST), dma(2, CHUNKS), dma(2),
            dma(2), dma(2), dma(2), dma(2), dma(2), dma(n // 2 + 1),
            pltpu.SemaphoreType.REGULAR(((n - 1).bit_length(),)),
        ],
        compiler_params=pltpu.CompilerParams(
            collective_id=0, has_side_effects=True, vmem_limit_bytes=28 * 2**20
        ),
        name="smooth",
    )(*(pltpu.with_memory_space_constraint(a, pltpu.HBM) for a in (source, guess, log_perm, owner, ymat, zmat, ez, ey)))
    smooth, coarse, ez, ey, holder = [pltpu.with_memory_space_constraint(a, pltpu.VMEM) for a in kept]
    return pl.pallas_call(
        functools.partial(prolong_kernel, n),
        out_shape=(
            jax.ShapeDtypeStruct((4, ny, nz), F32),
            jax.ShapeDtypeStruct((1, cells), F32),
        ),
        in_specs=[vmem] * 5,
        out_specs=(hbm, hbm),
        scratch_shapes=[whole(4, ny, nz), whole(1, cells), dma(5)],
        compiler_params=pltpu.CompilerParams(vmem_limit_bytes=16 * 2**20),
        name="prolong",
    )(coarse, smooth, ez, ey, holder)


def solution(mesh):
    spec = P(("samples", "brick"), None, None)
    return jax.shard_map(
        functools.partial(local, mesh.shape["brick"]),
        mesh=mesh,
        in_specs=(spec, spec, spec, P()),
        out_specs=(spec, P(("samples", "brick"), None)),
        check_vma=False,
    )
```

```python
import functools

import jax
import jax.numpy as jnp
import ml_dtypes
import numpy as np
from jax import lax
from jax.experimental import pallas as pl
from jax.experimental.pallas import tpu as pltpu
from jax.sharding import PartitionSpec as P

SWEEPS = 8
CHUNKS = 8
FIRST = 4
EARLY = 2
MESH = pl.DeviceIdType.MESH
F32 = jnp.float32
BF16 = jnp.bfloat16


def prolong_matrix(n_fine):
    i = np.arange(n_fine)[:, None]
    j = np.arange(n_fine // 4)[None, :]
    base, offset = i // 4, i % 4
    own = np.where((offset == 0) | (offset == 3), 0.625, 0.875)
    side = np.where(offset < 2, -1, 1)
    return np.where(j == base, own, 0.0) + np.where(j == base + side, 1.0 - own, 0.0)


def mean_matrix(n_fine):
    i = np.arange(n_fine)[:, None]
    j = np.arange(n_fine // 4)[None, :]
    return np.where(j == i // 4, 1.0, 0.0)


def even_odd(m):
    return np.concatenate([m[:, 0::2], m[:, 1::2]], axis=1)


def halves(m):
    zero = np.zeros_like(m)
    return np.stack([np.concatenate([m, zero], 1), np.concatenate([zero, m], 1)])


def split(x):
    hi = x.astype(BF16)
    return hi, (x - hi.astype(F32)).astype(BF16)


def dot(a, b):
    return jnp.dot(a, b, preferred_element_type=F32)


def to_coarse(y_mat, z_mat, x):
    hi, lo = split(x)
    a = dot(y_mat, hi) + dot(y_mat, lo)
    hi, lo = split(a)
    h = a.shape[0] // 2
    return (
        dot(hi[:h], z_mat[0]) + dot(lo[:h], z_mat[0]) + dot(hi[h:], z_mat[1]) + dot(lo[h:], z_mat[1])
    )


def smooth_kernel(
    n, ny, nz, group,
    source_hbm, guess_hbm, logq_hbm, owner_hbm, y_hbm, z_hbm, ez_hbm, ey_hbm,
    U2, C, ez, ey, holder,
    owner, coef, scaled, ymat, zmat, all_q, q_pad, all_p, all_r, B, src, logq, K, U0, U1, D, W, N, F, X, H, part,
    local_sem, halo_send, first_recv, second_recv, part_sem, q_send, q_recv, p_send, p_recv, r_send, r_recv, token_sem,
):
    me = lax.axis_index("brick")
    R = ny // CHUNKS
    half = n // 2
    has = (me > 0, me < n - 1)
    flag = [jnp.where(h, 1.0, 0.0).astype(F32) for h in has]
    far = lax.rem(me, 2)
    near_side = 1 - far
    sibling = me + 1 - 2 * far
    mine_at = (far, me // 2)
    neighbour = lambda side: me - 1 + 2 * side
    exists = lambda side: jnp.logical_and(neighbour(side) >= 0, neighbour(side) < n)

    loads = [
        pltpu.make_async_copy(logq_hbm, logq, local_sem.at[0]),
        pltpu.make_async_copy(guess_hbm, U0.at[:, pl.ds(8, ny)], local_sem.at[1]),
        pltpu.make_async_copy(source_hbm, src, local_sem.at[2]),
        pltpu.make_async_copy(y_hbm, ymat, local_sem.at[3]),
        pltpu.make_async_copy(z_hbm, zmat, local_sem.at[4]),
        pltpu.make_async_copy(ez_hbm, ez, local_sem.at[5]),
        pltpu.make_async_copy(ey_hbm, ey, local_sem.at[6]),
        pltpu.make_async_copy(owner_hbm, owner, local_sem.at[7]),
    ]

    def signal(sem, who):
        pl.semaphore_signal(sem, inc=1, device_id={"brick": who}, device_id_type=MESH)

    barrier = pltpu.get_barrier_semaphore()

    def greet(sem, distance):
        @pl.when(me >= distance)
        def _():
            signal(sem, me - distance)

        @pl.when(me + distance < n)
        def _():
            signal(sem, me + distance)

    def greeted(sem, distance):
        low = jnp.where(me >= distance, 1, 0)
        high = jnp.where(me + distance < n, 1, 0)
        pl.semaphore_wait(sem, low + high)

    distances = [2**k for k in range((n - 1).bit_length())]

    def relay(k):
        if k < len(distances):
            greeted(token_sem.at[k], distances[k])
        if k + 1 < len(distances):
            greet(token_sem.at[k + 1], distances[k + 1])

    greet(barrier, 1)
    for copy in loads:
        copy.start()

    zero_rows = jnp.zeros((8, nz), F32)
    for ref in (K, U0, U1, U2):
        for p in range(4):
            ref[p, 0:8] = zero_rows
            ref[p, ny + 8 : ny + 16] = zero_rows
    for side in range(2):

        @pl.when(jnp.logical_not(has[side]))
        def _():
            for which in range(3):
                H[which, side] = jnp.zeros((ny, nz), F32)

    greeted(barrier, 1)
    greet(token_sem.at[0], 1)

    def rows_at(c):
        return pl.ds(c * R if isinstance(c, int) else pl.multiple_of(c * R, R), R)

    def rows_in(c):
        return pl.ds(8 + c * R if isinstance(c, int) else pl.multiple_of(c * R, R) + 8, R)

    Q = ny // FIRST

    def send_first(side):
        for c in range(FIRST):
            rows = pl.ds(c * Q, Q)
            for which, ref in enumerate((logq_hbm, guess_hbm)):
                pltpu.make_async_remote_copy(
                    src_ref=ref.at[3 * side, rows],
                    dst_ref=H.at[which, 1 - side, rows],
                    send_sem=halo_send.at[side],
                    recv_sem=first_recv.at[1 - side, c],
                    device_id={"brick": neighbour(side)},
                    device_id_type=MESH,
                ).start()

    def first_in(side, c):
        ref = H.at[0:2, side, pl.ds(pl.multiple_of(c * Q, Q), Q)]
        return pltpu.make_async_remote_copy(
            src_ref=ref,
            dst_ref=ref,
            send_sem=halo_send.at[side],
            recv_sem=first_recv.at[side, c],
            device_id={"brick": neighbour(side)},
            device_id_type=MESH,
        )

    def second(side, c):
        return pltpu.make_async_remote_copy(
            src_ref=U1.at[3 * side, rows_in(c)],
            dst_ref=H.at[2, 1 - side, rows_at(c)],
            send_sem=halo_send.at[side],
            recv_sem=second_recv.at[1 - side, c],
            device_id={"brick": neighbour(side)},
            device_id_type=MESH,
        )

    def second_in(side, c):
        ref = H.at[2, side, rows_at(c)]
        return pltpu.make_async_remote_copy(
            src_ref=ref,
            dst_ref=ref,
            send_sem=halo_send.at[side],
            recv_sem=second_recv.at[side, c],
            device_id={"brick": neighbour(side)},
            device_id_type=MESH,
        )

    def halo_sent(side):
        ref = H.at[:, side]
        return pltpu.make_async_remote_copy(
            src_ref=ref,
            dst_ref=ref,
            send_sem=halo_send.at[side],
            recv_sem=first_recv.at[side, 0],
            device_id={"brick": neighbour(side)},
            device_id_type=MESH,
        )

    for side in (far, near_side):

        @pl.when(exists(side))
        def _():
            send_first(side)

    relay(0)

    lane = lax.broadcasted_iota(jnp.int32, (R, nz), 1)
    first, last = lane == 0, lane == nz - 1

    def middle(window):
        return window[8 : R + 8]

    def yz(window):
        center = middle(window)
        low = jnp.where(first, 0.0, pltpu.roll(center, 1, 1))
        high = jnp.where(last, 0.0, pltpu.roll(center, nz - 1, 1))
        return (window[7 : R + 7] + window[9 : R + 9]) + (low + high)

    def across(windows, p):
        total = yz(windows[p])
        if p > 0:
            total = total + middle(windows[p - 1])
        if p < 3:
            total = total + middle(windows[p + 1])
        return total

    loads[0].wait()

    def exps(c, _):
        for p in range(4):
            K[p, rows_in(c)] = jnp.exp(logq[p, rows_at(c)])
        return 0

    lax.fori_loop(0, CHUNKS, exps, 0)
    for copy in loads[1:]:
        copy.wait()
    relay(1)

    def windows(ref, c):
        at = pl.ds(pl.multiple_of(c * R, R), R + 16)
        return [ref[p, at] for p in range(4)]

    def nearby(u, k):
        uk = [a * b for a, b in zip(u, k)]
        return [0.5 * (middle(k[p]) * across(u, p) + across(uk, p)) for p in range(4)]

    def sweep_one(c, _):
        rows, at = rows_at(c), rows_in(c)
        u, k = windows(U0, c), windows(K, c)
        near = nearby(u, k)
        for p in range(4):
            d = 3.0 * middle(k[p]) + 0.5 * across(k, p)
            total = src[p, rows] + near[p]
            D[p, rows] = d
            if p in (0, 3):
                N[p, rows] = total
            else:
                w = 0.8 / d
                W[p, rows] = w
                U1[p, at] = 0.2 * middle(u[p]) + w * total
        return 0

    lax.fori_loop(0, CHUNKS, sweep_one, 0)

    all_q[mine_at] = to_coarse(
        ymat[0], zmat[0:2], (K[0, 8 : ny + 8] + K[1, 8 : ny + 8]) + (K[2, 8 : ny + 8] + K[3, 8 : ny + 8])
    ) * (1.0 / 64.0)
    for b in range(n):
        holder[b : b + 1] = jnp.full((1, 128), owner[b], jnp.int32)

    relay(2)

    def finish_one(c):
        rows, at = rows_at(c), rows_in(c)
        for side in range(2):

            @pl.when(has[side])
            def _():

                @pl.when(lax.rem(c, CHUNKS // FIRST) == 0)
                def _():
                    first_in(side, c // (CHUNKS // FIRST)).wait_recv()

        for side in range(2):
            p = 3 * side
            kh = jnp.exp(H[0, side, rows]) * flag[side]
            face = 0.5 * (K[p, at] + kh)
            d = D[p, rows] + 0.5 * kh
            w = 0.8 / d
            F[side, rows] = face
            D[p, rows] = d
            W[p, rows] = w
            U1[p, at] = 0.2 * U0[p, at] + w * (N[p, rows] + face * H[1, side, rows])
        for side in (far, near_side):

            @pl.when(exists(side))
            def _():
                second(side, c).start()

    def to_sibling(ref, part_of, send, recv):
        return pltpu.make_async_remote_copy(
            src_ref=ref.at[part_of],
            dst_ref=ref.at[part_of],
            send_sem=send.at[0],
            recv_sem=recv,
            device_id={"brick": sibling},
            device_id_type=MESH,
        )

    def others(body):
        def step(j, _):
            body(j + jnp.where(j >= me // 2, 1, 0))
            return 0

        lax.fori_loop(0, half - 1, step, 0)

    def spread(ref, send, recv):
        def step(k):
            pltpu.make_async_remote_copy(
                src_ref=ref.at[mine_at],
                dst_ref=ref.at[mine_at],
                send_sem=send.at[1],
                recv_sem=recv,
                device_id={"brick": 2 * k + far},
                device_id_type=MESH,
            ).start()

        others(step)

    def from_sibling(ref, send, recv):
        to_sibling(ref, 1 - far, send, recv).wait_recv()

    def hand_on(ref, send, recv):
        to_sibling(ref, (0, pl.ds(0, half - 1)), send, recv.at[0]).wait_recv()
        to_sibling(ref, far, send, recv.at[1]).start()

    early = me < EARLY

    def to_early(ref, k, send, recv):
        return pltpu.make_async_remote_copy(
            src_ref=ref.at[mine_at],
            dst_ref=ref.at[mine_at],
            send_sem=send.at[2],
            recv_sem=recv,
            device_id={"brick": 2 * k + 1 - far},
            device_id_type=MESH,
        )

    def spread_early(ref, send, recv):
        for k in range(EARLY // 2):

            @pl.when(me // 2 != k)
            def _():
                to_early(ref, k, send, recv.at[half]).start()

    def hand_on_each(ref, send, recv):
        def step(k):
            to_sibling(ref, (far, k), send, recv.at[k]).wait_recv()

            @pl.when(jnp.logical_not(early))
            def _():
                to_sibling(ref, (far, k), send, recv.at[half]).start()

        others(step)

    def sent_early(ref, send, recv):
        for k in range(EARLY // 2):

            @pl.when(me // 2 != k)
            def _():
                to_early(ref, k, send, recv.at[half]).wait_send()

    def sent(ref, kind, blocks, send, recv):
        block = ref.at[kind, 0:blocks]
        pltpu.make_async_remote_copy(
            src_ref=block, dst_ref=block, send_sem=send.at[kind], recv_sem=recv,
            device_id={"brick": sibling}, device_id_type=MESH,
        ).wait_send()

    def sweep_two(c):
        rows, at = rows_at(c), rows_in(c)
        u = windows(U1, c)
        near = nearby(u, windows(K, c))
        for p in range(4):
            total = src[p, rows] + near[p]
            if p in (0, 3):
                N[p, rows] = total
            else:
                U2[p, at] = 0.2 * middle(u[p]) + W[p, rows] * total

    relays = range(3, len(distances))

    def first_stage(c, _):
        @pl.when(c < CHUNKS)
        def _():
            finish_one(c)

        for k in relays:

            @pl.when(c == CHUNKS - 1 - (relays[-1] - k))
            def _():
                relay(k)

        @pl.when(c == CHUNKS - 1)
        def _():
            spread(all_q, q_send, q_recv.at[0])

        @pl.when(c > 0)
        def _():
            sweep_two(c - 1)

        return 0

    lax.fori_loop(0, CHUNKS + 1, first_stage, 0)

    def finish_two(c):
        rows, at = rows_at(c), rows_in(c)
        for side in range(2):

            @pl.when(has[side])
            def _():
                second_in(side, c).wait_recv()

        for side in range(2):
            p = 3 * side
            total = N[p, rows] + F[side, rows] * H[2, side, rows]
            U2[p, at] = 0.2 * U1[p, at] + W[p, rows] * total

    def residual(c):
        rows = rows_at(c)
        u = windows(U2, c)
        near = nearby(u, windows(K, c))
        r = [src[p, rows] - D[p, rows] * middle(u[p]) + near[p] for p in range(4)]
        flo = flag[0] * F[0, rows] * middle(u[0])
        fhi = flag[1] * F[1, rows] * middle(u[3])
        X[0, rows] = 0.625 * flo + 0.375 * r[0] + 0.125 * r[1]
        X[1, rows] = (0.375 * flo + 0.625 * r[0] + 0.875 * r[1]) + (0.375 * fhi + 0.625 * r[3] + 0.875 * r[2])
        X[2, rows] = 0.625 * fhi + 0.375 * r[3] + 0.125 * r[2]

    def second_stage(c, _):
        @pl.when(c < CHUNKS)
        def _():
            finish_two(c)

        @pl.when(c > 0)
        def _():
            residual(c - 1)

        return 0

    lax.fori_loop(0, CHUNKS + 1, second_stage, 0)

    restrict = lambda k: to_coarse(ymat[1], zmat[2:4], X[k])
    all_p[mine_at] = restrict(2 * far)
    spread(all_p, p_send, p_recv.at[0])

    part[0] = restrict(2 * near_side)
    swap = pltpu.make_async_remote_copy(
        src_ref=part.at[0],
        dst_ref=part.at[1],
        send_sem=part_sem.at[0],
        recv_sem=part_sem.at[1],
        device_id={"brick": sibling},
        device_id_type=MESH,
    )
    swap.start()
    mine = restrict(1)
    hand_on(all_q, q_send, q_recv)
    swap.wait_recv()
    all_r[mine_at] = mine + part[1]
    spread_early(all_r, r_send, r_recv)
    spread(all_r, r_send, r_recv.at[me // 2])
    to_sibling(all_r, mine_at, r_send, r_recv.at[half]).start()

    from_sibling(all_q, q_send, q_recv.at[1])
    coarse_coefficients(n, min(8, n), all_q, q_pad, coef, scaled)
    hand_on(all_p, p_send, p_recv)
    hand_on_each(all_r, r_send, r_recv)

    rows, lanes = all_r.shape[2:]
    shifts, _ = coarse_shifts((group, rows, lanes))
    edge = jnp.zeros((rows, lanes), F32)
    for slot in range(2):
        C[slot, 0] = edge
        C[slot, n + 1] = edge
    from_sibling(all_p, p_send, p_recv.at[1])
    from_sibling(all_r, r_send, r_recv.at[half])
    for b in range(n):
        r = all_r[b % 2, b // 2]
        if 0 < b < n - 1:
            r = r + all_p[1 - b % 2, b // 2 - 1 + 2 * (b % 2)]
        scaled_rhs = r * scaled[b]
        B[b] = scaled_rhs
        C[0, b + 1] = scaled_rhs

    for sweep in range(SWEEPS - 1):
        now, later = sweep % 2, 1 - sweep % 2

        def step(g, _):
            at = pl.multiple_of(g * group, group)
            c = C[now, pl.ds(at + 1, group)]
            near = (C[now, pl.ds(at, group)], C[now, pl.ds(at + 2, group)]) + shifts(c)
            terms = [coef[k, pl.ds(at, group)] * v for k, v in enumerate(near)]
            total = B[pl.ds(at, group)] + 0.2 * c
            total = (total + (terms[0] + terms[1])) + ((terms[2] + terms[3]) + (terms[4] + terms[5]))
            C[later, pl.ds(at + 1, group)] = total
            return 0

        lax.fori_loop(0, n // group, step, 0)

    for side in range(2):

        @pl.when(has[side])
        def _():
            halo_sent(side).wait_send()

    swap.wait_send()
    sent(all_q, 0, half, q_send, q_recv.at[0])
    sent(all_p, 0, half, p_send, p_recv.at[0])
    for ref, send, recv in ((all_q, q_send, q_recv), (all_p, p_send, p_recv), (all_r, r_send, r_recv)):
        sent(ref, 1, half - 1, send, recv.at[0])

    @pl.when(early)
    def _():
        sent(all_r, 0, 1, r_send, r_recv.at[0])

    @pl.when(jnp.logical_not(early))
    def _():
        sent(all_r, 0, half, r_send, r_recv.at[0])

    sent_early(all_r, r_send, r_recv)


def coarse_shifts(shape):
    rows, lanes = shape[1:]
    cz = lanes // 2
    row = lax.broadcasted_iota(jnp.int32, shape, 1)
    lane = lax.broadcasted_iota(jnp.int32, shape, 2)
    low_half = lane < cz
    z = jnp.where(low_half, lane, lane - cz)
    outside = (
        (row == 0) & low_half,
        (row == rows - 1) & jnp.logical_not(low_half),
        z == 0,
        z == cz - 1,
    )

    def shifts(c):
        swapped = pltpu.roll(c, cz, 2)
        y_low = jnp.where(low_half, pltpu.roll(swapped, 1, 1), swapped)
        y_high = jnp.where(low_half, swapped, pltpu.roll(swapped, rows - 1, 1))
        return y_low, y_high, pltpu.roll(c, 1, 2), pltpu.roll(c, lanes - 1, 2)

    return shifts, outside


def coarse_coefficients(n, group, perm, q_pad, coef, scaled):
    rows, lanes = perm.shape[2:]
    shifts, outside = coarse_shifts((group, rows, lanes))
    edge = jnp.zeros((rows, lanes), F32)
    q_pad[0] = edge
    q_pad[n + 1] = edge
    for b in range(n):
        q_pad[b + 1] = perm[b % 2, b // 2]

    def prepare(g, _):
        at = pl.multiple_of(g * group, group)
        q = q_pad[pl.ds(at + 1, group)]
        near = [q_pad[pl.ds(at, group)], q_pad[pl.ds(at + 2, group)]]
        near += [jnp.where(out, 0.0, v) for out, v in zip(outside, shifts(q))]
        faces = [0.5 * (q + v) for v in near]
        diagonal = ((faces[0] + faces[1]) + (faces[2] + faces[3])) + (faces[4] + faces[5])
        scale = 0.8 / diagonal
        for k, out in enumerate((None, None) + outside):
            f = faces[k] * scale
            coef[k, pl.ds(at, group)] = f if out is None else jnp.where(out, 0.0, f)
        scaled[pl.ds(at, group)] = (16.0 / 64.0) * scale
        return 0

    lax.fori_loop(0, n // group, prepare, 0)


def prolong_kernel(n, C, U2, ez, ey, holder, corrected_hbm, held_hbm, corrected, held, sem):
    me = lax.axis_index("brick")
    rows, lanes = C.shape[2:]
    ny = corrected.shape[1]
    final = (SWEEPS - 1) % 2
    below, mid, above = C[final, me], C[final, me + 1], C[final, me + 2]
    planes = jnp.concatenate(
        [
            0.625 * mid + 0.375 * below,
            0.875 * mid + 0.125 * below,
            0.875 * mid + 0.125 * above,
            0.625 * mid + 0.375 * above,
        ],
        axis=0,
    )
    hi, lo = split(planes)
    even = dot(hi, ez[0]) + dot(lo, ez[0])
    odd = dot(hi, ez[1]) + dot(lo, ez[1])
    copies = []
    for p in range(4):
        both = jnp.concatenate(
            [even[p * rows : (p + 1) * rows], odd[p * rows : (p + 1) * rows]], axis=0
        )
        hi, lo = split(both)
        corrected[p] = U2[p, 8 : ny + 8] + (dot(ey[...], hi) + dot(ey[...], lo))
        copies.append(pltpu.make_async_copy(corrected.at[p], corrected_hbm.at[p], sem.at[p]))
        copies[p].start()

    mine = jnp.zeros((rows, lanes), F32)
    for b in range(n):
        mine = jnp.where(holder[b : b + 1] == me, C[final, b + 1], mine)
    for r in range(rows):
        held[0:1, r * lanes : (r + 1) * lanes] = mine[r : r + 1]
    copies.append(pltpu.make_async_copy(held, held_hbm, sem.at[4]))
    copies[4].start()
    for copy in copies:
        copy.wait()


def local(n, source, guess, log_perm, owner):
    planes, ny, nz = source.shape
    assert planes == 4 and n % 2 == 0
    cells = (ny // 4) * (nz // 4)
    rows, lanes = ny // 8, nz // 2
    assert lanes == 128
    dense = (rows, lanes)
    as_bf16 = lambda m: jnp.asarray(m.astype(ml_dtypes.bfloat16))
    py, pz = even_odd(prolong_matrix(ny)), prolong_matrix(nz)
    ymat = as_bf16(np.stack([even_odd(mean_matrix(ny)).T, py.T]))
    zmat = as_bf16(np.concatenate([halves(mean_matrix(nz)), halves(pz)]))
    ey, ez = as_bf16(py), as_bf16(halves(pz).transpose(0, 2, 1))
    vmem = pl.BlockSpec(memory_space=pltpu.VMEM)
    hbm = pl.BlockSpec(memory_space=pl.ANY)
    whole = lambda *s: pltpu.VMEM(s, F32)
    dma = lambda *s: pltpu.SemaphoreType.DMA(s)
    padded = (4, ny + 16, nz)
    kept = pl.pallas_call(
        functools.partial(smooth_kernel, n, ny, nz, min(16, n)),
        out_shape=(
            whole(*padded), whole(2, n + 2, *dense), pltpu.VMEM(ez.shape, BF16), pltpu.VMEM(ey.shape, BF16),
            pltpu.VMEM((n, 128), jnp.int32),
        ),
        in_specs=[hbm] * 8,
        out_specs=(vmem,) * 5,
        scratch_shapes=[
            pltpu.SMEM((n,), jnp.int32),
            whole(6, n, *dense), whole(n, *dense),
            pltpu.VMEM(ymat.shape, BF16), pltpu.VMEM(zmat.shape, BF16),
            whole(2, n // 2, *dense), whole(n + 2, *dense), whole(2, n // 2, *dense), whole(2, n // 2, *dense), whole(n, *dense),
            whole(4, ny, nz), whole(4, ny, nz),
            whole(*padded), whole(*padded), whole(*padded),
            whole(4, ny, nz), whole(4, ny, nz), whole(4, ny, nz),
            whole(2, ny, nz), whole(3, ny, nz), whole(3, 2, ny, nz),
            whole(2, *dense),
            dma(8), dma(2), dma(2, FIRST), dma(2, CHUNKS), dma(2),
            dma(2), dma(2), dma(2), dma(2), dma(3), dma(n // 2 + 1),
            pltpu.SemaphoreType.REGULAR(((n - 1).bit_length(),)),
        ],
        compiler_params=pltpu.CompilerParams(
            collective_id=0, has_side_effects=True, vmem_limit_bytes=28 * 2**20
        ),
        name="smooth",
    )(*(pltpu.with_memory_space_constraint(a, pltpu.HBM) for a in (source, guess, log_perm, owner, ymat, zmat, ez, ey)))
    smooth, coarse, ez, ey, holder = [pltpu.with_memory_space_constraint(a, pltpu.VMEM) for a in kept]
    return pl.pallas_call(
        functools.partial(prolong_kernel, n),
        out_shape=(
            jax.ShapeDtypeStruct((4, ny, nz), F32),
            jax.ShapeDtypeStruct((1, cells), F32),
        ),
        in_specs=[vmem] * 5,
        out_specs=(hbm, hbm),
        scratch_shapes=[whole(4, ny, nz), whole(1, cells), dma(5)],
        compiler_params=pltpu.CompilerParams(vmem_limit_bytes=16 * 2**20),
        name="prolong",
    )(coarse, smooth, ez, ey, holder)


def solution(mesh):
    spec = P(("samples", "brick"), None, None)
    return jax.shard_map(
        functools.partial(local, mesh.shape["brick"]),
        mesh=mesh,
        in_specs=(spec, spec, spec, P()),
        out_specs=(spec, P(("samples", "brick"), None)),
        check_vma=False,
    )
```

```python
import functools

import jax
import jax.numpy as jnp
import ml_dtypes
import numpy as np
from jax import lax
from jax.experimental import pallas as pl
from jax.experimental.pallas import tpu as pltpu
from jax.sharding import PartitionSpec as P

SWEEPS = 8
CHUNKS = 8
FIRST = 4
EARLY = 2
HELD = 2
RELEASE = (4, 7)
MESH = pl.DeviceIdType.MESH
F32 = jnp.float32
BF16 = jnp.bfloat16


def prolong_matrix(n_fine):
    i = np.arange(n_fine)[:, None]
    j = np.arange(n_fine // 4)[None, :]
    base, offset = i // 4, i % 4
    own = np.where((offset == 0) | (offset == 3), 0.625, 0.875)
    side = np.where(offset < 2, -1, 1)
    return np.where(j == base, own, 0.0) + np.where(j == base + side, 1.0 - own, 0.0)


def mean_matrix(n_fine):
    i = np.arange(n_fine)[:, None]
    j = np.arange(n_fine // 4)[None, :]
    return np.where(j == i // 4, 1.0, 0.0)


def even_odd(m):
    return np.concatenate([m[:, 0::2], m[:, 1::2]], axis=1)


def halves(m):
    zero = np.zeros_like(m)
    return np.stack([np.concatenate([m, zero], 1), np.concatenate([zero, m], 1)])


def split(x):
    hi = x.astype(BF16)
    return hi, (x - hi.astype(F32)).astype(BF16)


def dot(a, b):
    return jnp.dot(a, b, preferred_element_type=F32)


def to_coarse(y_mat, z_mat, x):
    hi, lo = split(x)
    a = dot(y_mat, hi) + dot(y_mat, lo)
    hi, lo = split(a)
    h = a.shape[0] // 2
    return (
        dot(hi[:h], z_mat[0]) + dot(lo[:h], z_mat[0]) + dot(hi[h:], z_mat[1]) + dot(lo[h:], z_mat[1])
    )


def smooth_kernel(
    n, ny, nz, group,
    source_hbm, guess_hbm, logq_hbm, owner_hbm, y_hbm, z_hbm, ez_hbm, ey_hbm,
    U2, C, ez, ey, holder,
    owner, coef, scaled, ymat, zmat, all_q, q_pad, all_p, all_r, B, src, logq, K, U0, U1, D, W, N, F, X, H, part,
    local_sem, halo_send, first_recv, second_recv, part_sem, q_send, q_recv, p_send, p_recv, r_send, r_recv, token_sem,
):
    me = lax.axis_index("brick")
    R = ny // CHUNKS
    half = n // 2
    has = (me > 0, me < n - 1)
    flag = [jnp.where(h, 1.0, 0.0).astype(F32) for h in has]
    far = lax.rem(me, 2)
    near_side = 1 - far
    sibling = me + 1 - 2 * far
    mine_at = (far, me // 2)
    neighbour = lambda side: me - 1 + 2 * side
    exists = lambda side: jnp.logical_and(neighbour(side) >= 0, neighbour(side) < n)

    loads = [
        pltpu.make_async_copy(logq_hbm, logq, local_sem.at[0]),
        pltpu.make_async_copy(guess_hbm, U0.at[:, pl.ds(8, ny)], local_sem.at[1]),
        pltpu.make_async_copy(source_hbm, src, local_sem.at[2]),
        pltpu.make_async_copy(y_hbm, ymat, local_sem.at[3]),
        pltpu.make_async_copy(z_hbm, zmat, local_sem.at[4]),
        pltpu.make_async_copy(ez_hbm, ez, local_sem.at[5]),
        pltpu.make_async_copy(ey_hbm, ey, local_sem.at[6]),
        pltpu.make_async_copy(owner_hbm, owner, local_sem.at[7]),
    ]

    def signal(sem, who):
        pl.semaphore_signal(sem, inc=1, device_id={"brick": who}, device_id_type=MESH)

    barrier = pltpu.get_barrier_semaphore()

    def greet(sem, distance):
        @pl.when(me >= distance)
        def _():
            signal(sem, me - distance)

        @pl.when(me + distance < n)
        def _():
            signal(sem, me + distance)

    def greeted(sem, distance):
        low = jnp.where(me >= distance, 1, 0)
        high = jnp.where(me + distance < n, 1, 0)
        pl.semaphore_wait(sem, low + high)

    distances = [2**k for k in range((n - 1).bit_length())]

    def relay(k):
        if k < len(distances):
            greeted(token_sem.at[k], distances[k])
        if k + 1 < len(distances):
            greet(token_sem.at[k + 1], distances[k + 1])

    greet(barrier, 1)
    for copy in loads:
        copy.start()

    zero_rows = jnp.zeros((8, nz), F32)
    for ref in (K, U0, U1, U2):
        for p in range(4):
            ref[p, 0:8] = zero_rows
            ref[p, ny + 8 : ny + 16] = zero_rows
    for side in range(2):

        @pl.when(jnp.logical_not(has[side]))
        def _():
            for which in range(3):
                H[which, side] = jnp.zeros((ny, nz), F32)

    greeted(barrier, 1)
    greet(token_sem.at[0], 1)

    def rows_at(c):
        return pl.ds(c * R if isinstance(c, int) else pl.multiple_of(c * R, R), R)

    def rows_in(c):
        return pl.ds(8 + c * R if isinstance(c, int) else pl.multiple_of(c * R, R) + 8, R)

    Q = ny // FIRST

    def send_first(side, chunks):
        for c in chunks:
            rows = pl.ds(c * Q, Q)
            for which, ref in enumerate((logq_hbm, guess_hbm)):
                pltpu.make_async_remote_copy(
                    src_ref=ref.at[3 * side, rows],
                    dst_ref=H.at[which, 1 - side, rows],
                    send_sem=halo_send.at[side],
                    recv_sem=first_recv.at[1 - side, c],
                    device_id={"brick": neighbour(side)},
                    device_id_type=MESH,
                ).start()

    def first_in(side, c):
        ref = H.at[0:2, side, pl.ds(pl.multiple_of(c * Q, Q), Q)]
        return pltpu.make_async_remote_copy(
            src_ref=ref,
            dst_ref=ref,
            send_sem=halo_send.at[side],
            recv_sem=first_recv.at[side, c],
            device_id={"brick": neighbour(side)},
            device_id_type=MESH,
        )

    def second(side, c):
        return pltpu.make_async_remote_copy(
            src_ref=U1.at[3 * side, rows_in(c)],
            dst_ref=H.at[2, 1 - side, rows_at(c)],
            send_sem=halo_send.at[side],
            recv_sem=second_recv.at[1 - side, c],
            device_id={"brick": neighbour(side)},
            device_id_type=MESH,
        )

    def second_in(side, c):
        ref = H.at[2, side, rows_at(c)]
        return pltpu.make_async_remote_copy(
            src_ref=ref,
            dst_ref=ref,
            send_sem=halo_send.at[side],
            recv_sem=second_recv.at[side, c],
            device_id={"brick": neighbour(side)},
            device_id_type=MESH,
        )

    def halo_sent(side):
        ref = H.at[:, side]
        return pltpu.make_async_remote_copy(
            src_ref=ref,
            dst_ref=ref,
            send_sem=halo_send.at[side],
            recv_sem=first_recv.at[side, 0],
            device_id={"brick": neighbour(side)},
            device_id_type=MESH,
        )

    holds = jnp.logical_and(lax.rem(me + 1, 4) < 2, exists(far)) if n == 16 else False

    @pl.when(exists(far))
    def _():
        send_first(far, range(HELD))

    @pl.when(jnp.logical_and(exists(far), jnp.logical_not(holds)))
    def _():
        send_first(far, range(HELD, FIRST))

    send_first(near_side, range(FIRST))

    relay(0)

    lane = lax.broadcasted_iota(jnp.int32, (R, nz), 1)
    first, last = lane == 0, lane == nz - 1

    def middle(window):
        return window[8 : R + 8]

    def yz(window):
        center = middle(window)
        low = jnp.where(first, 0.0, pltpu.roll(center, 1, 1))
        high = jnp.where(last, 0.0, pltpu.roll(center, nz - 1, 1))
        return (window[7 : R + 7] + window[9 : R + 9]) + (low + high)

    def across(windows, p):
        total = yz(windows[p])
        if p > 0:
            total = total + middle(windows[p - 1])
        if p < 3:
            total = total + middle(windows[p + 1])
        return total

    loads[0].wait()

    def exps(c, _):
        for p in range(4):
            K[p, rows_in(c)] = jnp.exp(logq[p, rows_at(c)])
        return 0

    lax.fori_loop(0, CHUNKS, exps, 0)
    for copy in loads[1:]:
        copy.wait()
    relay(1)

    def windows(ref, c):
        at = pl.ds(pl.multiple_of(c * R, R), R + 16)
        return [ref[p, at] for p in range(4)]

    def nearby(u, k):
        uk = [a * b for a, b in zip(u, k)]
        return [0.5 * (middle(k[p]) * across(u, p) + across(uk, p)) for p in range(4)]

    def sweep_one(c, _):
        for k, at_step in enumerate(RELEASE):

            @pl.when(jnp.logical_and(holds, c == at_step))
            def _():
                send_first(far, [HELD + k])

        rows, at = rows_at(c), rows_in(c)
        u, k = windows(U0, c), windows(K, c)
        near = nearby(u, k)
        for p in range(4):
            d = 3.0 * middle(k[p]) + 0.5 * across(k, p)
            total = src[p, rows] + near[p]
            D[p, rows] = d
            if p in (0, 3):
                N[p, rows] = total
            else:
                w = 0.8 / d
                W[p, rows] = w
                U1[p, at] = 0.2 * middle(u[p]) + w * total
        return 0

    lax.fori_loop(0, CHUNKS, sweep_one, 0)

    all_q[mine_at] = to_coarse(
        ymat[0], zmat[0:2], (K[0, 8 : ny + 8] + K[1, 8 : ny + 8]) + (K[2, 8 : ny + 8] + K[3, 8 : ny + 8])
    ) * (1.0 / 64.0)
    for b in range(n):
        holder[b : b + 1] = jnp.full((1, 128), owner[b], jnp.int32)

    relay(2)

    def finish_one(c):
        rows, at = rows_at(c), rows_in(c)
        for side in range(2):

            @pl.when(has[side])
            def _():

                @pl.when(lax.rem(c, CHUNKS // FIRST) == 0)
                def _():
                    first_in(side, c // (CHUNKS // FIRST)).wait_recv()

        for side in range(2):
            p = 3 * side
            kh = jnp.exp(H[0, side, rows]) * flag[side]
            face = 0.5 * (K[p, at] + kh)
            d = D[p, rows] + 0.5 * kh
            w = 0.8 / d
            F[side, rows] = face
            D[p, rows] = d
            W[p, rows] = w
            U1[p, at] = 0.2 * U0[p, at] + w * (N[p, rows] + face * H[1, side, rows])
        for side in (far, near_side):

            @pl.when(exists(side))
            def _():
                second(side, c).start()

    def to_sibling(ref, part_of, send, recv):
        return pltpu.make_async_remote_copy(
            src_ref=ref.at[part_of],
            dst_ref=ref.at[part_of],
            send_sem=send.at[0],
            recv_sem=recv,
            device_id={"brick": sibling},
            device_id_type=MESH,
        )

    def others(body):
        def step(j, _):
            body(j + jnp.where(j >= me // 2, 1, 0))
            return 0

        lax.fori_loop(0, half - 1, step, 0)

    def spread(ref, send, recv):
        def step(k):
            pltpu.make_async_remote_copy(
                src_ref=ref.at[mine_at],
                dst_ref=ref.at[mine_at],
                send_sem=send.at[1],
                recv_sem=recv,
                device_id={"brick": 2 * k + far},
                device_id_type=MESH,
            ).start()

        others(step)

    def from_sibling(ref, send, recv):
        to_sibling(ref, 1 - far, send, recv).wait_recv()

    def hand_on(ref, send, recv):
        to_sibling(ref, (0, pl.ds(0, half - 1)), send, recv.at[0]).wait_recv()
        to_sibling(ref, far, send, recv.at[1]).start()

    early = me < EARLY

    def to_early(ref, k, send, recv):
        return pltpu.make_async_remote_copy(
            src_ref=ref.at[mine_at],
            dst_ref=ref.at[mine_at],
            send_sem=send.at[2],
            recv_sem=recv,
            device_id={"brick": 2 * k + 1 - far},
            device_id_type=MESH,
        )

    def spread_early(ref, send, recv):
        for k in range(EARLY // 2):

            @pl.when(me // 2 != k)
            def _():
                to_early(ref, k, send, recv.at[half]).start()

    def hand_on_each(ref, send, recv):
        def step(k):
            to_sibling(ref, (far, k), send, recv.at[k]).wait_recv()

            @pl.when(jnp.logical_not(early))
            def _():
                to_sibling(ref, (far, k), send, recv.at[half]).start()

        others(step)

    def sent_early(ref, send, recv):
        for k in range(EARLY // 2):

            @pl.when(me // 2 != k)
            def _():
                to_early(ref, k, send, recv.at[half]).wait_send()

    def sent(ref, kind, blocks, send, recv):
        block = ref.at[kind, 0:blocks]
        pltpu.make_async_remote_copy(
            src_ref=block, dst_ref=block, send_sem=send.at[kind], recv_sem=recv,
            device_id={"brick": sibling}, device_id_type=MESH,
        ).wait_send()

    def sweep_two(c):
        rows, at = rows_at(c), rows_in(c)
        u = windows(U1, c)
        near = nearby(u, windows(K, c))
        for p in range(4):
            total = src[p, rows] + near[p]
            if p in (0, 3):
                N[p, rows] = total
            else:
                U2[p, at] = 0.2 * middle(u[p]) + W[p, rows] * total

    relays = range(3, len(distances))

    def first_stage(c, _):
        @pl.when(c < CHUNKS)
        def _():
            finish_one(c)

        for k in relays:

            @pl.when(c == CHUNKS - 1 - (relays[-1] - k))
            def _():
                relay(k)

        @pl.when(c == CHUNKS - 1)
        def _():
            spread(all_q, q_send, q_recv.at[0])

        @pl.when(c > 0)
        def _():
            sweep_two(c - 1)

        return 0

    lax.fori_loop(0, CHUNKS + 1, first_stage, 0)

    def finish_two(c):
        rows, at = rows_at(c), rows_in(c)
        for side in range(2):

            @pl.when(has[side])
            def _():
                second_in(side, c).wait_recv()

        for side in range(2):
            p = 3 * side
            total = N[p, rows] + F[side, rows] * H[2, side, rows]
            U2[p, at] = 0.2 * U1[p, at] + W[p, rows] * total

    def residual(c):
        rows = rows_at(c)
        u = windows(U2, c)
        near = nearby(u, windows(K, c))
        r = [src[p, rows] - D[p, rows] * middle(u[p]) + near[p] for p in range(4)]
        flo = flag[0] * F[0, rows] * middle(u[0])
        fhi = flag[1] * F[1, rows] * middle(u[3])
        X[0, rows] = 0.625 * flo + 0.375 * r[0] + 0.125 * r[1]
        X[1, rows] = (0.375 * flo + 0.625 * r[0] + 0.875 * r[1]) + (0.375 * fhi + 0.625 * r[3] + 0.875 * r[2])
        X[2, rows] = 0.625 * fhi + 0.375 * r[3] + 0.125 * r[2]

    def second_stage(c, _):
        @pl.when(c < CHUNKS)
        def _():
            finish_two(c)

        @pl.when(c > 0)
        def _():
            residual(c - 1)

        return 0

    lax.fori_loop(0, CHUNKS + 1, second_stage, 0)

    restrict = lambda k: to_coarse(ymat[1], zmat[2:4], X[k])
    all_p[mine_at] = restrict(2 * far)
    spread(all_p, p_send, p_recv.at[0])

    part[0] = restrict(2 * near_side)
    swap = pltpu.make_async_remote_copy(
        src_ref=part.at[0],
        dst_ref=part.at[1],
        send_sem=part_sem.at[0],
        recv_sem=part_sem.at[1],
        device_id={"brick": sibling},
        device_id_type=MESH,
    )
    swap.start()
    mine = restrict(1)
    hand_on(all_q, q_send, q_recv)
    swap.wait_recv()
    all_r[mine_at] = mine + part[1]
    spread_early(all_r, r_send, r_recv)
    spread(all_r, r_send, r_recv.at[me // 2])
    to_sibling(all_r, mine_at, r_send, r_recv.at[half]).start()

    from_sibling(all_q, q_send, q_recv.at[1])
    coarse_coefficients(n, min(8, n), all_q, q_pad, coef, scaled)
    hand_on(all_p, p_send, p_recv)
    hand_on_each(all_r, r_send, r_recv)

    rows, lanes = all_r.shape[2:]
    shifts, _ = coarse_shifts((group, rows, lanes))
    edge = jnp.zeros((rows, lanes), F32)
    for slot in range(2):
        C[slot, 0] = edge
        C[slot, n + 1] = edge
    from_sibling(all_p, p_send, p_recv.at[1])
    from_sibling(all_r, r_send, r_recv.at[half])
    for b in range(n):
        r = all_r[b % 2, b // 2]
        if 0 < b < n - 1:
            r = r + all_p[1 - b % 2, b // 2 - 1 + 2 * (b % 2)]
        scaled_rhs = r * scaled[b]
        B[b] = scaled_rhs
        C[0, b + 1] = scaled_rhs

    for sweep in range(SWEEPS - 1):
        now, later = sweep % 2, 1 - sweep % 2

        def step(g, _):
            at = pl.multiple_of(g * group, group)
            c = C[now, pl.ds(at + 1, group)]
            near = (C[now, pl.ds(at, group)], C[now, pl.ds(at + 2, group)]) + shifts(c)
            terms = [coef[k, pl.ds(at, group)] * v for k, v in enumerate(near)]
            total = B[pl.ds(at, group)] + 0.2 * c
            total = (total + (terms[0] + terms[1])) + ((terms[2] + terms[3]) + (terms[4] + terms[5]))
            C[later, pl.ds(at + 1, group)] = total
            return 0

        lax.fori_loop(0, n // group, step, 0)

    for side in range(2):

        @pl.when(has[side])
        def _():
            halo_sent(side).wait_send()

    swap.wait_send()
    sent(all_q, 0, half, q_send, q_recv.at[0])
    sent(all_p, 0, half, p_send, p_recv.at[0])
    for ref, send, recv in ((all_q, q_send, q_recv), (all_p, p_send, p_recv), (all_r, r_send, r_recv)):
        sent(ref, 1, half - 1, send, recv.at[0])

    @pl.when(early)
    def _():
        sent(all_r, 0, 1, r_send, r_recv.at[0])

    @pl.when(jnp.logical_not(early))
    def _():
        sent(all_r, 0, half, r_send, r_recv.at[0])

    sent_early(all_r, r_send, r_recv)


def coarse_shifts(shape):
    rows, lanes = shape[1:]
    cz = lanes // 2
    row = lax.broadcasted_iota(jnp.int32, shape, 1)
    lane = lax.broadcasted_iota(jnp.int32, shape, 2)
    low_half = lane < cz
    z = jnp.where(low_half, lane, lane - cz)
    outside = (
        (row == 0) & low_half,
        (row == rows - 1) & jnp.logical_not(low_half),
        z == 0,
        z == cz - 1,
    )

    def shifts(c):
        swapped = pltpu.roll(c, cz, 2)
        y_low = jnp.where(low_half, pltpu.roll(swapped, 1, 1), swapped)
        y_high = jnp.where(low_half, swapped, pltpu.roll(swapped, rows - 1, 1))
        return y_low, y_high, pltpu.roll(c, 1, 2), pltpu.roll(c, lanes - 1, 2)

    return shifts, outside


def coarse_coefficients(n, group, perm, q_pad, coef, scaled):
    rows, lanes = perm.shape[2:]
    shifts, outside = coarse_shifts((group, rows, lanes))
    edge = jnp.zeros((rows, lanes), F32)
    q_pad[0] = edge
    q_pad[n + 1] = edge
    for b in range(n):
        q_pad[b + 1] = perm[b % 2, b // 2]

    def prepare(g, _):
        at = pl.multiple_of(g * group, group)
        q = q_pad[pl.ds(at + 1, group)]
        near = [q_pad[pl.ds(at, group)], q_pad[pl.ds(at + 2, group)]]
        near += [jnp.where(out, 0.0, v) for out, v in zip(outside, shifts(q))]
        faces = [0.5 * (q + v) for v in near]
        diagonal = ((faces[0] + faces[1]) + (faces[2] + faces[3])) + (faces[4] + faces[5])
        scale = 0.8 / diagonal
        for k, out in enumerate((None, None) + outside):
            f = faces[k] * scale
            coef[k, pl.ds(at, group)] = f if out is None else jnp.where(out, 0.0, f)
        scaled[pl.ds(at, group)] = (16.0 / 64.0) * scale
        return 0

    lax.fori_loop(0, n // group, prepare, 0)


def prolong_kernel(n, C, U2, ez, ey, holder, corrected_hbm, held_hbm, corrected, held, sem):
    me = lax.axis_index("brick")
    rows, lanes = C.shape[2:]
    ny = corrected.shape[1]
    final = (SWEEPS - 1) % 2
    below, mid, above = C[final, me], C[final, me + 1], C[final, me + 2]
    planes = jnp.concatenate(
        [
            0.625 * mid + 0.375 * below,
            0.875 * mid + 0.125 * below,
            0.875 * mid + 0.125 * above,
            0.625 * mid + 0.375 * above,
        ],
        axis=0,
    )
    hi, lo = split(planes)
    even = dot(hi, ez[0]) + dot(lo, ez[0])
    odd = dot(hi, ez[1]) + dot(lo, ez[1])
    copies = []
    for p in range(4):
        both = jnp.concatenate(
            [even[p * rows : (p + 1) * rows], odd[p * rows : (p + 1) * rows]], axis=0
        )
        hi, lo = split(both)
        corrected[p] = U2[p, 8 : ny + 8] + (dot(ey[...], hi) + dot(ey[...], lo))
        copies.append(pltpu.make_async_copy(corrected.at[p], corrected_hbm.at[p], sem.at[p]))
        copies[p].start()

    mine = jnp.zeros((rows, lanes), F32)
    for b in range(n):
        mine = jnp.where(holder[b : b + 1] == me, C[final, b + 1], mine)
    for r in range(rows):
        held[0:1, r * lanes : (r + 1) * lanes] = mine[r : r + 1]
    copies.append(pltpu.make_async_copy(held, held_hbm, sem.at[4]))
    copies[4].start()
    for copy in copies:
        copy.wait()


def local(n, source, guess, log_perm, owner):
    planes, ny, nz = source.shape
    assert planes == 4 and n % 2 == 0
    cells = (ny // 4) * (nz // 4)
    rows, lanes = ny // 8, nz // 2
    assert lanes == 128
    dense = (rows, lanes)
    as_bf16 = lambda m: jnp.asarray(m.astype(ml_dtypes.bfloat16))
    py, pz = even_odd(prolong_matrix(ny)), prolong_matrix(nz)
    ymat = as_bf16(np.stack([even_odd(mean_matrix(ny)).T, py.T]))
    zmat = as_bf16(np.concatenate([halves(mean_matrix(nz)), halves(pz)]))
    ey, ez = as_bf16(py), as_bf16(halves(pz).transpose(0, 2, 1))
    vmem = pl.BlockSpec(memory_space=pltpu.VMEM)
    hbm = pl.BlockSpec(memory_space=pl.ANY)
    whole = lambda *s: pltpu.VMEM(s, F32)
    dma = lambda *s: pltpu.SemaphoreType.DMA(s)
    padded = (4, ny + 16, nz)
    kept = pl.pallas_call(
        functools.partial(smooth_kernel, n, ny, nz, min(16, n)),
        out_shape=(
            whole(*padded), whole(2, n + 2, *dense), pltpu.VMEM(ez.shape, BF16), pltpu.VMEM(ey.shape, BF16),
            pltpu.VMEM((n, 128), jnp.int32),
        ),
        in_specs=[hbm] * 8,
        out_specs=(vmem,) * 5,
        scratch_shapes=[
            pltpu.SMEM((n,), jnp.int32),
            whole(6, n, *dense), whole(n, *dense),
            pltpu.VMEM(ymat.shape, BF16), pltpu.VMEM(zmat.shape, BF16),
            whole(2, n // 2, *dense), whole(n + 2, *dense), whole(2, n // 2, *dense), whole(2, n // 2, *dense), whole(n, *dense),
            whole(4, ny, nz), whole(4, ny, nz),
            whole(*padded), whole(*padded), whole(*padded),
            whole(4, ny, nz), whole(4, ny, nz), whole(4, ny, nz),
            whole(2, ny, nz), whole(3, ny, nz), whole(3, 2, ny, nz),
            whole(2, *dense),
            dma(8), dma(2), dma(2, FIRST), dma(2, CHUNKS), dma(2),
            dma(2), dma(2), dma(2), dma(2), dma(3), dma(n // 2 + 1),
            pltpu.SemaphoreType.REGULAR(((n - 1).bit_length(),)),
        ],
        compiler_params=pltpu.CompilerParams(
            collective_id=0, has_side_effects=True, vmem_limit_bytes=28 * 2**20
        ),
        name="smooth",
    )(*(pltpu.with_memory_space_constraint(a, pltpu.HBM) for a in (source, guess, log_perm, owner, ymat, zmat, ez, ey)))
    smooth, coarse, ez, ey, holder = [pltpu.with_memory_space_constraint(a, pltpu.VMEM) for a in kept]
    return pl.pallas_call(
        functools.partial(prolong_kernel, n),
        out_shape=(
            jax.ShapeDtypeStruct((4, ny, nz), F32),
            jax.ShapeDtypeStruct((1, cells), F32),
        ),
        in_specs=[vmem] * 5,
        out_specs=(hbm, hbm),
        scratch_shapes=[whole(4, ny, nz), whole(1, cells), dma(5)],
        compiler_params=pltpu.CompilerParams(vmem_limit_bytes=16 * 2**20),
        name="prolong",
    )(coarse, smooth, ez, ey, holder)


def solution(mesh):
    spec = P(("samples", "brick"), None, None)
    return jax.shard_map(
        functools.partial(local, mesh.shape["brick"]),
        mesh=mesh,
        in_specs=(spec, spec, spec, P()),
        out_specs=(spec, P(("samples", "brick"), None)),
        check_vma=False,
    )
```

```python
import functools

import jax
import jax.numpy as jnp
import ml_dtypes
import numpy as np
from jax import lax
from jax.experimental import pallas as pl
from jax.experimental.pallas import tpu as pltpu
from jax.sharding import PartitionSpec as P

SWEEPS = 8
CHUNKS = 8
FIRST = 4
EARLY = 2
HELD = 2
RELEASE = (4, 7)
MESH = pl.DeviceIdType.MESH
F32 = jnp.float32
BF16 = jnp.bfloat16


def prolong_matrix(n_fine):
    i = np.arange(n_fine)[:, None]
    j = np.arange(n_fine // 4)[None, :]
    base, offset = i // 4, i % 4
    own = np.where((offset == 0) | (offset == 3), 0.625, 0.875)
    side = np.where(offset < 2, -1, 1)
    return np.where(j == base, own, 0.0) + np.where(j == base + side, 1.0 - own, 0.0)


def mean_matrix(n_fine):
    i = np.arange(n_fine)[:, None]
    j = np.arange(n_fine // 4)[None, :]
    return np.where(j == i // 4, 1.0, 0.0)


def even_odd(m):
    return np.concatenate([m[:, 0::2], m[:, 1::2]], axis=1)


def halves(m):
    zero = np.zeros_like(m)
    return np.stack([np.concatenate([m, zero], 1), np.concatenate([zero, m], 1)])


def split(x):
    hi = x.astype(BF16)
    return hi, (x - hi.astype(F32)).astype(BF16)


def dot(a, b):
    return jnp.dot(a, b, preferred_element_type=F32)


def to_coarse(y_mat, z_mat, x):
    hi, lo = split(x)
    a = dot(y_mat, hi) + dot(y_mat, lo)
    hi, lo = split(a)
    h = a.shape[0] // 2
    return (
        dot(hi[:h], z_mat[0]) + dot(lo[:h], z_mat[0]) + dot(hi[h:], z_mat[1]) + dot(lo[h:], z_mat[1])
    )


def smooth_kernel(
    n, ny, nz, group,
    source_hbm, guess_hbm, logq_hbm, owner_hbm, y_hbm, z_hbm, ez_hbm, ey_hbm,
    U2, C, ez, ey, holder,
    owner, coef, scaled, ymat, zmat, all_q, q_pad, all_p, all_r, B, src, logq, K, U0, U1, D, W, N, F, X, H, part,
    local_sem, halo_send, first_recv, second_recv, part_sem, q_send, q_recv, p_send, p_recv, r_send, r_recv, token_sem,
):
    me = lax.axis_index("brick")
    R = ny // CHUNKS
    half = n // 2
    has = (me > 0, me < n - 1)
    flag = [jnp.where(h, 1.0, 0.0).astype(F32) for h in has]
    far = lax.rem(me, 2)
    near_side = 1 - far
    sibling = me + 1 - 2 * far
    mine_at = (far, me // 2)
    neighbour = lambda side: me - 1 + 2 * side
    exists = lambda side: jnp.logical_and(neighbour(side) >= 0, neighbour(side) < n)

    loads = [
        pltpu.make_async_copy(logq_hbm, logq, local_sem.at[0]),
        pltpu.make_async_copy(guess_hbm, U0.at[:, pl.ds(8, ny)], local_sem.at[1]),
        pltpu.make_async_copy(source_hbm, src, local_sem.at[2]),
        pltpu.make_async_copy(y_hbm, ymat, local_sem.at[3]),
        pltpu.make_async_copy(z_hbm, zmat, local_sem.at[4]),
        pltpu.make_async_copy(ez_hbm, ez, local_sem.at[5]),
        pltpu.make_async_copy(ey_hbm, ey, local_sem.at[6]),
        pltpu.make_async_copy(owner_hbm, owner, local_sem.at[7]),
    ]

    def signal(sem, who):
        pl.semaphore_signal(sem, inc=1, device_id={"brick": who}, device_id_type=MESH)

    barrier = pltpu.get_barrier_semaphore()

    def greet(sem, distance):
        @pl.when(me >= distance)
        def _():
            signal(sem, me - distance)

        @pl.when(me + distance < n)
        def _():
            signal(sem, me + distance)

    def greeted(sem, distance):
        low = jnp.where(me >= distance, 1, 0)
        high = jnp.where(me + distance < n, 1, 0)
        pl.semaphore_wait(sem, low + high)

    distances = [2**k for k in range((n - 1).bit_length())]

    def relay(k):
        if k < len(distances):
            greeted(token_sem.at[k], distances[k])
        if k + 1 < len(distances):
            greet(token_sem.at[k + 1], distances[k + 1])

    greet(barrier, 1)
    for copy in loads:
        copy.start()

    zero_rows = jnp.zeros((8, nz), F32)
    for ref in (K, U0, U1, U2):
        for p in range(4):
            ref[p, 0:8] = zero_rows
            ref[p, ny + 8 : ny + 16] = zero_rows
    for side in range(2):

        @pl.when(jnp.logical_not(has[side]))
        def _():
            for which in range(3):
                H[which, side] = jnp.zeros((ny, nz), F32)

    greeted(barrier, 1)
    greet(token_sem.at[0], 1)

    def rows_at(c):
        return pl.ds(c * R if isinstance(c, int) else pl.multiple_of(c * R, R), R)

    def rows_in(c):
        return pl.ds(8 + c * R if isinstance(c, int) else pl.multiple_of(c * R, R) + 8, R)

    Q = ny // FIRST

    def send_first(side, chunks):
        for c in chunks:
            rows = pl.ds(c * Q, Q)
            for which, ref in enumerate((logq_hbm, guess_hbm)):
                pltpu.make_async_remote_copy(
                    src_ref=ref.at[3 * side, rows],
                    dst_ref=H.at[which, 1 - side, rows],
                    send_sem=halo_send.at[side],
                    recv_sem=first_recv.at[1 - side, c],
                    device_id={"brick": neighbour(side)},
                    device_id_type=MESH,
                ).start()

    def first_in(side, c):
        ref = H.at[0:2, side, pl.ds(pl.multiple_of(c * Q, Q), Q)]
        return pltpu.make_async_remote_copy(
            src_ref=ref,
            dst_ref=ref,
            send_sem=halo_send.at[side],
            recv_sem=first_recv.at[side, c],
            device_id={"brick": neighbour(side)},
            device_id_type=MESH,
        )

    def second(side, c):
        return pltpu.make_async_remote_copy(
            src_ref=U1.at[3 * side, rows_in(c)],
            dst_ref=H.at[2, 1 - side, rows_at(c)],
            send_sem=halo_send.at[side],
            recv_sem=second_recv.at[1 - side, c],
            device_id={"brick": neighbour(side)},
            device_id_type=MESH,
        )

    def second_in(side, c):
        ref = H.at[2, side, rows_at(c)]
        return pltpu.make_async_remote_copy(
            src_ref=ref,
            dst_ref=ref,
            send_sem=halo_send.at[side],
            recv_sem=second_recv.at[side, c],
            device_id={"brick": neighbour(side)},
            device_id_type=MESH,
        )

    def halo_sent(side):
        ref = H.at[:, side]
        return pltpu.make_async_remote_copy(
            src_ref=ref,
            dst_ref=ref,
            send_sem=halo_send.at[side],
            recv_sem=first_recv.at[side, 0],
            device_id={"brick": neighbour(side)},
            device_id_type=MESH,
        )

    holds = jnp.logical_and(lax.rem(me + 1, 4) < 2, exists(far)) if n == 16 else False

    @pl.when(exists(far))
    def _():
        send_first(far, range(HELD))

    @pl.when(jnp.logical_and(exists(far), jnp.logical_not(holds)))
    def _():
        send_first(far, range(HELD, FIRST))

    send_first(near_side, range(FIRST))

    relay(0)

    lane = lax.broadcasted_iota(jnp.int32, (R, nz), 1)
    first, last = lane == 0, lane == nz - 1

    def middle(window):
        return window[8 : R + 8]

    def yz(window):
        center = middle(window)
        low = jnp.where(first, 0.0, pltpu.roll(center, 1, 1))
        high = jnp.where(last, 0.0, pltpu.roll(center, nz - 1, 1))
        return (window[7 : R + 7] + window[9 : R + 9]) + (low + high)

    def across(windows, p):
        total = yz(windows[p])
        if p > 0:
            total = total + middle(windows[p - 1])
        if p < 3:
            total = total + middle(windows[p + 1])
        return total

    loads[0].wait()

    def exps(c, _):
        for p in range(4):
            K[p, rows_in(c)] = jnp.exp(logq[p, rows_at(c)])
        return 0

    lax.fori_loop(0, CHUNKS, exps, 0)
    for copy in loads[1:]:
        copy.wait()
    relay(1)

    def windows(ref, c):
        at = pl.ds(pl.multiple_of(c * R, R), R + 16)
        return [ref[p, at] for p in range(4)]

    def nearby(u, k):
        uk = [a * b for a, b in zip(u, k)]
        return [0.5 * (middle(k[p]) * across(u, p) + across(uk, p)) for p in range(4)]

    def sweep_one(c, _):
        for k, at_step in enumerate(RELEASE):

            @pl.when(jnp.logical_and(holds, c == at_step))
            def _():
                send_first(far, [HELD + k])

        rows, at = rows_at(c), rows_in(c)
        u, k = windows(U0, c), windows(K, c)
        near = nearby(u, k)
        for p in range(4):
            d = 3.0 * middle(k[p]) + 0.5 * across(k, p)
            total = src[p, rows] + near[p]
            D[p, rows] = d
            if p in (0, 3):
                N[p, rows] = total
            else:
                w = 0.8 / d
                W[p, rows] = w
                U1[p, at] = 0.2 * middle(u[p]) + w * total
        return 0

    lax.fori_loop(0, CHUNKS, sweep_one, 0)

    all_q[mine_at] = to_coarse(
        ymat[0], zmat[0:2], (K[0, 8 : ny + 8] + K[1, 8 : ny + 8]) + (K[2, 8 : ny + 8] + K[3, 8 : ny + 8])
    ) * (1.0 / 64.0)
    for b in range(n):
        holder[b : b + 1] = jnp.full((1, 128), owner[b], jnp.int32)

    relay(2)

    def finish_one(c):
        rows, at = rows_at(c), rows_in(c)
        for side in range(2):

            @pl.when(has[side])
            def _():

                @pl.when(lax.rem(c, CHUNKS // FIRST) == 0)
                def _():
                    first_in(side, c // (CHUNKS // FIRST)).wait_recv()

        for side in range(2):
            p = 3 * side
            kh = jnp.exp(H[0, side, rows]) * flag[side]
            face = 0.5 * (K[p, at] + kh)
            d = D[p, rows] + 0.5 * kh
            w = 0.8 / d
            F[side, rows] = face
            D[p, rows] = d
            W[p, rows] = w
            U1[p, at] = 0.2 * U0[p, at] + w * (N[p, rows] + face * H[1, side, rows])
        for side in (far, near_side):

            @pl.when(exists(side))
            def _():
                second(side, c).start()

    def to_sibling(ref, part_of, send, recv):
        return pltpu.make_async_remote_copy(
            src_ref=ref.at[part_of],
            dst_ref=ref.at[part_of],
            send_sem=send.at[0],
            recv_sem=recv,
            device_id={"brick": sibling},
            device_id_type=MESH,
        )

    def others(body):
        def step(j, _):
            body(j + jnp.where(j >= me // 2, 1, 0))
            return 0

        lax.fori_loop(0, half - 1, step, 0)

    def spread(ref, send, recv):
        def step(k):
            pltpu.make_async_remote_copy(
                src_ref=ref.at[mine_at],
                dst_ref=ref.at[mine_at],
                send_sem=send.at[1],
                recv_sem=recv,
                device_id={"brick": 2 * k + far},
                device_id_type=MESH,
            ).start()

        others(step)

    def from_sibling(ref, send, recv):
        to_sibling(ref, 1 - far, send, recv).wait_recv()

    def hand_on(ref, send, recv):
        to_sibling(ref, (0, pl.ds(0, half - 1)), send, recv.at[0]).wait_recv()
        to_sibling(ref, far, send, recv.at[1]).start()

    early = me < EARLY

    def to_early(ref, k, send, recv):
        return pltpu.make_async_remote_copy(
            src_ref=ref.at[mine_at],
            dst_ref=ref.at[mine_at],
            send_sem=send.at[2],
            recv_sem=recv,
            device_id={"brick": 2 * k + 1 - far},
            device_id_type=MESH,
        )

    def spread_early(ref, send, recv):
        for k in range(EARLY // 2):

            @pl.when(me // 2 != k)
            def _():
                to_early(ref, k, send, recv.at[half]).start()

    def hand_on_each(ref, send, recv):
        def step(k):
            to_sibling(ref, (far, k), send, recv.at[k]).wait_recv()

            @pl.when(jnp.logical_not(early))
            def _():
                to_sibling(ref, (far, k), send, recv.at[half]).start()

        others(step)

    def sent_early(ref, send, recv):
        for k in range(EARLY // 2):

            @pl.when(me // 2 != k)
            def _():
                to_early(ref, k, send, recv.at[half]).wait_send()

    def sent(ref, kind, blocks, send, recv):
        block = ref.at[kind, 0:blocks]
        pltpu.make_async_remote_copy(
            src_ref=block, dst_ref=block, send_sem=send.at[kind], recv_sem=recv,
            device_id={"brick": sibling}, device_id_type=MESH,
        ).wait_send()

    def sweep_two(c):
        rows, at = rows_at(c), rows_in(c)
        u = windows(U1, c)
        near = nearby(u, windows(K, c))
        for p in range(4):
            total = src[p, rows] + near[p]
            if p in (0, 3):
                N[p, rows] = total
            else:
                U2[p, at] = 0.2 * middle(u[p]) + W[p, rows] * total

    relays = range(3, len(distances))

    def first_stage(c, _):
        @pl.when(c < CHUNKS)
        def _():
            finish_one(c)

        for k in relays:

            @pl.when(c == CHUNKS - 1 - (relays[-1] - k))
            def _():
                relay(k)

        @pl.when(c > 0)
        def _():
            sweep_two(c - 1)

        return 0

    lax.fori_loop(0, CHUNKS + 1, first_stage, 0)

    def finish_two(c):
        rows, at = rows_at(c), rows_in(c)
        for side in range(2):

            @pl.when(has[side])
            def _():
                second_in(side, c).wait_recv()

        for side in range(2):
            p = 3 * side
            total = N[p, rows] + F[side, rows] * H[2, side, rows]
            U2[p, at] = 0.2 * U1[p, at] + W[p, rows] * total

    def residual(c):
        rows = rows_at(c)
        u = windows(U2, c)
        near = nearby(u, windows(K, c))
        r = [src[p, rows] - D[p, rows] * middle(u[p]) + near[p] for p in range(4)]
        flo = flag[0] * F[0, rows] * middle(u[0])
        fhi = flag[1] * F[1, rows] * middle(u[3])
        X[0, rows] = 0.625 * flo + 0.375 * r[0] + 0.125 * r[1]
        X[1, rows] = (0.375 * flo + 0.625 * r[0] + 0.875 * r[1]) + (0.375 * fhi + 0.625 * r[3] + 0.875 * r[2])
        X[2, rows] = 0.625 * fhi + 0.375 * r[3] + 0.125 * r[2]

    def second_stage(c, _):
        @pl.when(c == 3)
        def _():
            spread(all_q, q_send, q_recv.at[0])

        @pl.when(c < CHUNKS)
        def _():
            finish_two(c)

        @pl.when(c > 0)
        def _():
            residual(c - 1)

        return 0

    lax.fori_loop(0, CHUNKS + 1, second_stage, 0)

    restrict = lambda k: to_coarse(ymat[1], zmat[2:4], X[k])
    all_p[mine_at] = restrict(2 * far)
    spread(all_p, p_send, p_recv.at[0])

    part[0] = restrict(2 * near_side)
    swap = pltpu.make_async_remote_copy(
        src_ref=part.at[0],
        dst_ref=part.at[1],
        send_sem=part_sem.at[0],
        recv_sem=part_sem.at[1],
        device_id={"brick": sibling},
        device_id_type=MESH,
    )
    swap.start()
    mine = restrict(1)
    hand_on(all_q, q_send, q_recv)
    swap.wait_recv()
    all_r[mine_at] = mine + part[1]
    spread_early(all_r, r_send, r_recv)
    spread(all_r, r_send, r_recv.at[me // 2])
    to_sibling(all_r, mine_at, r_send, r_recv.at[half]).start()

    from_sibling(all_q, q_send, q_recv.at[1])
    coarse_coefficients(n, min(8, n), all_q, q_pad, coef, scaled)
    hand_on(all_p, p_send, p_recv)
    hand_on_each(all_r, r_send, r_recv)

    rows, lanes = all_r.shape[2:]
    shifts, _ = coarse_shifts((group, rows, lanes))
    edge = jnp.zeros((rows, lanes), F32)
    for slot in range(2):
        C[slot, 0] = edge
        C[slot, n + 1] = edge
    from_sibling(all_p, p_send, p_recv.at[1])
    from_sibling(all_r, r_send, r_recv.at[half])
    for b in range(n):
        r = all_r[b % 2, b // 2]
        if 0 < b < n - 1:
            r = r + all_p[1 - b % 2, b // 2 - 1 + 2 * (b % 2)]
        scaled_rhs = r * scaled[b]
        B[b] = scaled_rhs
        C[0, b + 1] = scaled_rhs

    for sweep in range(SWEEPS - 1):
        now, later = sweep % 2, 1 - sweep % 2

        def step(g, _):
            at = pl.multiple_of(g * group, group)
            c = C[now, pl.ds(at + 1, group)]
            near = (C[now, pl.ds(at, group)], C[now, pl.ds(at + 2, group)]) + shifts(c)
            terms = [coef[k, pl.ds(at, group)] * v for k, v in enumerate(near)]
            total = B[pl.ds(at, group)] + 0.2 * c
            total = (total + (terms[0] + terms[1])) + ((terms[2] + terms[3]) + (terms[4] + terms[5]))
            C[later, pl.ds(at + 1, group)] = total
            return 0

        lax.fori_loop(0, n // group, step, 0)

    for side in range(2):

        @pl.when(has[side])
        def _():
            halo_sent(side).wait_send()

    swap.wait_send()
    sent(all_q, 0, half, q_send, q_recv.at[0])
    sent(all_p, 0, half, p_send, p_recv.at[0])
    for ref, send, recv in ((all_q, q_send, q_recv), (all_p, p_send, p_recv), (all_r, r_send, r_recv)):
        sent(ref, 1, half - 1, send, recv.at[0])

    @pl.when(early)
    def _():
        sent(all_r, 0, 1, r_send, r_recv.at[0])

    @pl.when(jnp.logical_not(early))
    def _():
        sent(all_r, 0, half, r_send, r_recv.at[0])

    sent_early(all_r, r_send, r_recv)


def coarse_shifts(shape):
    rows, lanes = shape[1:]
    cz = lanes // 2
    row = lax.broadcasted_iota(jnp.int32, shape, 1)
    lane = lax.broadcasted_iota(jnp.int32, shape, 2)
    low_half = lane < cz
    z = jnp.where(low_half, lane, lane - cz)
    outside = (
        (row == 0) & low_half,
        (row == rows - 1) & jnp.logical_not(low_half),
        z == 0,
        z == cz - 1,
    )

    def shifts(c):
        swapped = pltpu.roll(c, cz, 2)
        y_low = jnp.where(low_half, pltpu.roll(swapped, 1, 1), swapped)
        y_high = jnp.where(low_half, swapped, pltpu.roll(swapped, rows - 1, 1))
        return y_low, y_high, pltpu.roll(c, 1, 2), pltpu.roll(c, lanes - 1, 2)

    return shifts, outside


def coarse_coefficients(n, group, perm, q_pad, coef, scaled):
    rows, lanes = perm.shape[2:]
    shifts, outside = coarse_shifts((group, rows, lanes))
    edge = jnp.zeros((rows, lanes), F32)
    q_pad[0] = edge
    q_pad[n + 1] = edge
    for b in range(n):
        q_pad[b + 1] = perm[b % 2, b // 2]

    def prepare(g, _):
        at = pl.multiple_of(g * group, group)
        q = q_pad[pl.ds(at + 1, group)]
        near = [q_pad[pl.ds(at, group)], q_pad[pl.ds(at + 2, group)]]
        near += [jnp.where(out, 0.0, v) for out, v in zip(outside, shifts(q))]
        faces = [0.5 * (q + v) for v in near]
        diagonal = ((faces[0] + faces[1]) + (faces[2] + faces[3])) + (faces[4] + faces[5])
        scale = 0.8 / diagonal
        for k, out in enumerate((None, None) + outside):
            f = faces[k] * scale
            coef[k, pl.ds(at, group)] = f if out is None else jnp.where(out, 0.0, f)
        scaled[pl.ds(at, group)] = (16.0 / 64.0) * scale
        return 0

    lax.fori_loop(0, n // group, prepare, 0)


def prolong_kernel(n, C, U2, ez, ey, holder, corrected_hbm, held_hbm, corrected, held, sem):
    me = lax.axis_index("brick")
    rows, lanes = C.shape[2:]
    ny = corrected.shape[1]
    final = (SWEEPS - 1) % 2
    below, mid, above = C[final, me], C[final, me + 1], C[final, me + 2]
    planes = jnp.concatenate(
        [
            0.625 * mid + 0.375 * below,
            0.875 * mid + 0.125 * below,
            0.875 * mid + 0.125 * above,
            0.625 * mid + 0.375 * above,
        ],
        axis=0,
    )
    hi, lo = split(planes)
    even = dot(hi, ez[0]) + dot(lo, ez[0])
    odd = dot(hi, ez[1]) + dot(lo, ez[1])
    copies = []
    for p in range(4):
        both = jnp.concatenate(
            [even[p * rows : (p + 1) * rows], odd[p * rows : (p + 1) * rows]], axis=0
        )
        hi, lo = split(both)
        corrected[p] = U2[p, 8 : ny + 8] + (dot(ey[...], hi) + dot(ey[...], lo))
        copies.append(pltpu.make_async_copy(corrected.at[p], corrected_hbm.at[p], sem.at[p]))
        copies[p].start()

    mine = jnp.zeros((rows, lanes), F32)
    for b in range(n):
        mine = jnp.where(holder[b : b + 1] == me, C[final, b + 1], mine)
    for r in range(rows):
        held[0:1, r * lanes : (r + 1) * lanes] = mine[r : r + 1]
    copies.append(pltpu.make_async_copy(held, held_hbm, sem.at[4]))
    copies[4].start()
    for copy in copies:
        copy.wait()


def local(n, source, guess, log_perm, owner):
    planes, ny, nz = source.shape
    assert planes == 4 and n % 2 == 0
    cells = (ny // 4) * (nz // 4)
    rows, lanes = ny // 8, nz // 2
    assert lanes == 128
    dense = (rows, lanes)
    as_bf16 = lambda m: jnp.asarray(m.astype(ml_dtypes.bfloat16))
    py, pz = even_odd(prolong_matrix(ny)), prolong_matrix(nz)
    ymat = as_bf16(np.stack([even_odd(mean_matrix(ny)).T, py.T]))
    zmat = as_bf16(np.concatenate([halves(mean_matrix(nz)), halves(pz)]))
    ey, ez = as_bf16(py), as_bf16(halves(pz).transpose(0, 2, 1))
    vmem = pl.BlockSpec(memory_space=pltpu.VMEM)
    hbm = pl.BlockSpec(memory_space=pl.ANY)
    whole = lambda *s: pltpu.VMEM(s, F32)
    dma = lambda *s: pltpu.SemaphoreType.DMA(s)
    padded = (4, ny + 16, nz)
    kept = pl.pallas_call(
        functools.partial(smooth_kernel, n, ny, nz, min(16, n)),
        out_shape=(
            whole(*padded), whole(2, n + 2, *dense), pltpu.VMEM(ez.shape, BF16), pltpu.VMEM(ey.shape, BF16),
            pltpu.VMEM((n, 128), jnp.int32),
        ),
        in_specs=[hbm] * 8,
        out_specs=(vmem,) * 5,
        scratch_shapes=[
            pltpu.SMEM((n,), jnp.int32),
            whole(6, n, *dense), whole(n, *dense),
            pltpu.VMEM(ymat.shape, BF16), pltpu.VMEM(zmat.shape, BF16),
            whole(2, n // 2, *dense), whole(n + 2, *dense), whole(2, n // 2, *dense), whole(2, n // 2, *dense), whole(n, *dense),
            whole(4, ny, nz), whole(4, ny, nz),
            whole(*padded), whole(*padded), whole(*padded),
            whole(4, ny, nz), whole(4, ny, nz), whole(4, ny, nz),
            whole(2, ny, nz), whole(3, ny, nz), whole(3, 2, ny, nz),
            whole(2, *dense),
            dma(8), dma(2), dma(2, FIRST), dma(2, CHUNKS), dma(2),
            dma(2), dma(2), dma(2), dma(2), dma(3), dma(n // 2 + 1),
            pltpu.SemaphoreType.REGULAR(((n - 1).bit_length(),)),
        ],
        compiler_params=pltpu.CompilerParams(
            collective_id=0, has_side_effects=True, vmem_limit_bytes=28 * 2**20
        ),
        name="smooth",
    )(*(pltpu.with_memory_space_constraint(a, pltpu.HBM) for a in (source, guess, log_perm, owner, ymat, zmat, ez, ey)))
    smooth, coarse, ez, ey, holder = [pltpu.with_memory_space_constraint(a, pltpu.VMEM) for a in kept]
    return pl.pallas_call(
        functools.partial(prolong_kernel, n),
        out_shape=(
            jax.ShapeDtypeStruct((4, ny, nz), F32),
            jax.ShapeDtypeStruct((1, cells), F32),
        ),
        in_specs=[vmem] * 5,
        out_specs=(hbm, hbm),
        scratch_shapes=[whole(4, ny, nz), whole(1, cells), dma(5)],
        compiler_params=pltpu.CompilerParams(vmem_limit_bytes=16 * 2**20),
        name="prolong",
    )(coarse, smooth, ez, ey, holder)


def solution(mesh):
    spec = P(("samples", "brick"), None, None)
    return jax.shard_map(
        functools.partial(local, mesh.shape["brick"]),
        mesh=mesh,
        in_specs=(spec, spec, spec, P()),
        out_specs=(spec, P(("samples", "brick"), None)),
        check_vma=False,
    )
```

```python
import functools

import jax
import jax.numpy as jnp
import ml_dtypes
import numpy as np
from jax import lax
from jax.experimental import pallas as pl
from jax.experimental.pallas import tpu as pltpu
from jax.sharding import PartitionSpec as P

SWEEPS = 8
CHUNKS = 8
FIRST = 4
EARLY = 2
HELD = 2
RELEASE = (4, 7)
MESH = pl.DeviceIdType.MESH
F32 = jnp.float32
BF16 = jnp.bfloat16


def prolong_matrix(n_fine):
    i = np.arange(n_fine)[:, None]
    j = np.arange(n_fine // 4)[None, :]
    base, offset = i // 4, i % 4
    own = np.where((offset == 0) | (offset == 3), 0.625, 0.875)
    side = np.where(offset < 2, -1, 1)
    return np.where(j == base, own, 0.0) + np.where(j == base + side, 1.0 - own, 0.0)


def mean_matrix(n_fine):
    i = np.arange(n_fine)[:, None]
    j = np.arange(n_fine // 4)[None, :]
    return np.where(j == i // 4, 1.0, 0.0)


def even_odd(m):
    return np.concatenate([m[:, 0::2], m[:, 1::2]], axis=1)


def halves(m):
    zero = np.zeros_like(m)
    return np.stack([np.concatenate([m, zero], 1), np.concatenate([zero, m], 1)])


def split(x):
    hi = x.astype(BF16)
    return hi, (x - hi.astype(F32)).astype(BF16)


def dot(a, b):
    return jnp.dot(a, b, preferred_element_type=F32)


def to_coarse(y_mat, z_mat, x):
    hi, lo = split(x)
    a = dot(y_mat, hi) + dot(y_mat, lo)
    hi, lo = split(a)
    h = a.shape[0] // 2
    return (
        dot(hi[:h], z_mat[0]) + dot(lo[:h], z_mat[0]) + dot(hi[h:], z_mat[1]) + dot(lo[h:], z_mat[1])
    )


def smooth_kernel(
    n, ny, nz, group,
    source_hbm, guess_hbm, logq_hbm, owner_hbm, y_hbm, z_hbm, ez_hbm, ey_hbm,
    U2, C, ez, ey, holder,
    owner, coef, scaled, ymat, zmat, all_q, q_pad, all_p, all_r, B, src, logq, K, U0, U1, D, W, N, F, X, H, part,
    local_sem, halo_send, first_recv, second_recv, part_sem, q_send, q_recv, p_send, p_recv, r_send, r_recv, token_sem,
):
    me = lax.axis_index("brick")
    R = ny // CHUNKS
    half = n // 2
    has = (me > 0, me < n - 1)
    flag = [jnp.where(h, 1.0, 0.0).astype(F32) for h in has]
    far = lax.rem(me, 2)
    near_side = 1 - far
    sibling = me + 1 - 2 * far
    mine_at = (far, me // 2)
    neighbour = lambda side: me - 1 + 2 * side
    exists = lambda side: jnp.logical_and(neighbour(side) >= 0, neighbour(side) < n)

    loads = [
        pltpu.make_async_copy(logq_hbm, logq, local_sem.at[0]),
        pltpu.make_async_copy(guess_hbm, U0.at[:, pl.ds(8, ny)], local_sem.at[1]),
        pltpu.make_async_copy(source_hbm, src, local_sem.at[2]),
        pltpu.make_async_copy(y_hbm, ymat, local_sem.at[3]),
        pltpu.make_async_copy(z_hbm, zmat, local_sem.at[4]),
        pltpu.make_async_copy(ez_hbm, ez, local_sem.at[5]),
        pltpu.make_async_copy(ey_hbm, ey, local_sem.at[6]),
        pltpu.make_async_copy(owner_hbm, owner, local_sem.at[7]),
    ]

    def signal(sem, who):
        pl.semaphore_signal(sem, inc=1, device_id={"brick": who}, device_id_type=MESH)

    barrier = pltpu.get_barrier_semaphore()

    def greet(sem, distance):
        @pl.when(me >= distance)
        def _():
            signal(sem, me - distance)

        @pl.when(me + distance < n)
        def _():
            signal(sem, me + distance)

    def greeted(sem, distance):
        low = jnp.where(me >= distance, 1, 0)
        high = jnp.where(me + distance < n, 1, 0)
        pl.semaphore_wait(sem, low + high)

    distances = [2**k for k in range((n - 1).bit_length())]

    def relay(k):
        if k < len(distances):
            greeted(token_sem.at[k], distances[k])
        if k + 1 < len(distances):
            greet(token_sem.at[k + 1], distances[k + 1])

    greet(barrier, 1)
    for copy in loads:
        copy.start()

    zero_rows = jnp.zeros((8, nz), F32)
    for ref in (K, U0, U1, U2):
        for p in range(4):
            ref[p, 0:8] = zero_rows
            ref[p, ny + 8 : ny + 16] = zero_rows
    for side in range(2):

        @pl.when(jnp.logical_not(has[side]))
        def _():
            for which in range(3):
                H[which, side] = jnp.zeros((ny, nz), F32)

    greeted(barrier, 1)
    greet(token_sem.at[0], 1)

    def rows_at(c):
        return pl.ds(c * R if isinstance(c, int) else pl.multiple_of(c * R, R), R)

    def rows_in(c):
        return pl.ds(8 + c * R if isinstance(c, int) else pl.multiple_of(c * R, R) + 8, R)

    Q = ny // FIRST

    def send_first(side, chunks):
        for c in chunks:
            rows = pl.ds(c * Q, Q)
            for which, ref in enumerate((logq_hbm, guess_hbm)):
                pltpu.make_async_remote_copy(
                    src_ref=ref.at[3 * side, rows],
                    dst_ref=H.at[which, 1 - side, rows],
                    send_sem=halo_send.at[side],
                    recv_sem=first_recv.at[1 - side, c],
                    device_id={"brick": neighbour(side)},
                    device_id_type=MESH,
                ).start()

    def first_in(side, c):
        ref = H.at[0:2, side, pl.ds(pl.multiple_of(c * Q, Q), Q)]
        return pltpu.make_async_remote_copy(
            src_ref=ref,
            dst_ref=ref,
            send_sem=halo_send.at[side],
            recv_sem=first_recv.at[side, c],
            device_id={"brick": neighbour(side)},
            device_id_type=MESH,
        )

    def second(side, c):
        return pltpu.make_async_remote_copy(
            src_ref=U1.at[3 * side, rows_in(c)],
            dst_ref=H.at[2, 1 - side, rows_at(c)],
            send_sem=halo_send.at[side],
            recv_sem=second_recv.at[1 - side, c],
            device_id={"brick": neighbour(side)},
            device_id_type=MESH,
        )

    def second_in(side, c):
        ref = H.at[2, side, rows_at(c)]
        return pltpu.make_async_remote_copy(
            src_ref=ref,
            dst_ref=ref,
            send_sem=halo_send.at[side],
            recv_sem=second_recv.at[side, c],
            device_id={"brick": neighbour(side)},
            device_id_type=MESH,
        )

    def halo_sent(side):
        ref = H.at[:, side]
        return pltpu.make_async_remote_copy(
            src_ref=ref,
            dst_ref=ref,
            send_sem=halo_send.at[side],
            recv_sem=first_recv.at[side, 0],
            device_id={"brick": neighbour(side)},
            device_id_type=MESH,
        )

    holds = jnp.logical_and(lax.rem(me + 1, 4) < 2, exists(far)) if n == 16 else False

    @pl.when(exists(far))
    def _():
        send_first(far, range(HELD))

    @pl.when(jnp.logical_and(exists(far), jnp.logical_not(holds)))
    def _():
        send_first(far, range(HELD, FIRST))

    send_first(near_side, range(FIRST))

    relay(0)

    lane = lax.broadcasted_iota(jnp.int32, (R, nz), 1)
    first, last = lane == 0, lane == nz - 1

    def middle(window):
        return window[8 : R + 8]

    def yz(window):
        center = middle(window)
        low = jnp.where(first, 0.0, pltpu.roll(center, 1, 1))
        high = jnp.where(last, 0.0, pltpu.roll(center, nz - 1, 1))
        return (window[7 : R + 7] + window[9 : R + 9]) + (low + high)

    def across(windows, p):
        total = yz(windows[p])
        if p > 0:
            total = total + middle(windows[p - 1])
        if p < 3:
            total = total + middle(windows[p + 1])
        return total

    loads[0].wait()

    def exps(c, _):
        for p in range(4):
            K[p, rows_in(c)] = jnp.exp(logq[p, rows_at(c)])
        return 0

    lax.fori_loop(0, CHUNKS, exps, 0)
    for copy in loads[1:]:
        copy.wait()
    relay(1)

    def windows(ref, c):
        at = pl.ds(pl.multiple_of(c * R, R), R + 16)
        return [ref[p, at] for p in range(4)]

    def nearby(u, k):
        uk = [a * b for a, b in zip(u, k)]
        return [0.5 * (middle(k[p]) * across(u, p) + across(uk, p)) for p in range(4)]

    def sweep_one(c, _):
        for k, at_step in enumerate(RELEASE):

            @pl.when(jnp.logical_and(holds, c == at_step))
            def _():
                send_first(far, [HELD + k])

        rows, at = rows_at(c), rows_in(c)
        u, k = windows(U0, c), windows(K, c)
        near = nearby(u, k)
        for p in range(4):
            d = 3.0 * middle(k[p]) + 0.5 * across(k, p)
            total = src[p, rows] + near[p]
            D[p, rows] = d
            if p in (0, 3):
                N[p, rows] = total
            else:
                w = 0.8 / d
                W[p, rows] = w
                U1[p, at] = 0.2 * middle(u[p]) + w * total
        return 0

    lax.fori_loop(0, CHUNKS, sweep_one, 0)

    all_q[mine_at] = to_coarse(
        ymat[0], zmat[0:2], (K[0, 8 : ny + 8] + K[1, 8 : ny + 8]) + (K[2, 8 : ny + 8] + K[3, 8 : ny + 8])
    ) * (1.0 / 64.0)
    for b in range(n):
        holder[b : b + 1] = jnp.full((1, 128), owner[b], jnp.int32)

    relay(2)

    def finish_one(c):
        rows, at = rows_at(c), rows_in(c)
        for side in range(2):

            @pl.when(has[side])
            def _():

                @pl.when(lax.rem(c, CHUNKS // FIRST) == 0)
                def _():
                    first_in(side, c // (CHUNKS // FIRST)).wait_recv()

        for side in range(2):
            p = 3 * side
            kh = jnp.exp(H[0, side, rows]) * flag[side]
            face = 0.5 * (K[p, at] + kh)
            d = D[p, rows] + 0.5 * kh
            w = 0.8 / d
            F[side, rows] = face
            D[p, rows] = d
            W[p, rows] = w
            U1[p, at] = 0.2 * U0[p, at] + w * (N[p, rows] + face * H[1, side, rows])
        for side in (far, near_side):

            @pl.when(exists(side))
            def _():
                second(side, c).start()

    def to_sibling(ref, part_of, send, recv):
        return pltpu.make_async_remote_copy(
            src_ref=ref.at[part_of],
            dst_ref=ref.at[part_of],
            send_sem=send.at[0],
            recv_sem=recv,
            device_id={"brick": sibling},
            device_id_type=MESH,
        )

    def others(body):
        def step(j, _):
            body(j + jnp.where(j >= me // 2, 1, 0))
            return 0

        lax.fori_loop(0, half - 1, step, 0)

    def spread(ref, send, recv):
        def step(k):
            pltpu.make_async_remote_copy(
                src_ref=ref.at[mine_at],
                dst_ref=ref.at[mine_at],
                send_sem=send.at[1],
                recv_sem=recv,
                device_id={"brick": 2 * k + far},
                device_id_type=MESH,
            ).start()

        others(step)

    def from_sibling(ref, send, recv):
        to_sibling(ref, 1 - far, send, recv).wait_recv()

    def hand_on(ref, send, recv):
        to_sibling(ref, (0, pl.ds(0, half - 1)), send, recv.at[0]).wait_recv()
        to_sibling(ref, far, send, recv.at[1]).start()

    early = me < EARLY

    def to_early(ref, k, send, recv):
        return pltpu.make_async_remote_copy(
            src_ref=ref.at[mine_at],
            dst_ref=ref.at[mine_at],
            send_sem=send.at[2],
            recv_sem=recv,
            device_id={"brick": 2 * k + 1 - far},
            device_id_type=MESH,
        )

    def spread_early(ref, send, recv):
        for k in range(EARLY // 2):

            @pl.when(me // 2 != k)
            def _():
                to_early(ref, k, send, recv.at[half]).start()

    def hand_on_each(ref, send, recv):
        def step(k):
            to_sibling(ref, (far, k), send, recv.at[k]).wait_recv()

            @pl.when(jnp.logical_not(early))
            def _():
                to_sibling(ref, (far, k), send, recv.at[half]).start()

        others(step)

    def sent_early(ref, send, recv):
        for k in range(EARLY // 2):

            @pl.when(me // 2 != k)
            def _():
                to_early(ref, k, send, recv.at[half]).wait_send()

    def sent(ref, kind, blocks, send, recv):
        block = ref.at[kind, 0:blocks]
        pltpu.make_async_remote_copy(
            src_ref=block, dst_ref=block, send_sem=send.at[kind], recv_sem=recv,
            device_id={"brick": sibling}, device_id_type=MESH,
        ).wait_send()

    def sweep_two(c):
        rows, at = rows_at(c), rows_in(c)
        u = windows(U1, c)
        near = nearby(u, windows(K, c))
        for p in range(4):
            total = src[p, rows] + near[p]
            if p in (0, 3):
                N[p, rows] = total
            else:
                U2[p, at] = 0.2 * middle(u[p]) + W[p, rows] * total

    relays = range(3, len(distances))

    def first_stage(c, _):
        @pl.when(c < CHUNKS)
        def _():
            finish_one(c)

        for k in relays:

            @pl.when(c == CHUNKS - 1 - (relays[-1] - k))
            def _():
                relay(k)

        @pl.when(c > 0)
        def _():
            sweep_two(c - 1)

        return 0

    lax.fori_loop(0, CHUNKS + 1, first_stage, 0)

    def finish_two(c):
        rows, at = rows_at(c), rows_in(c)
        for side in range(2):

            @pl.when(has[side])
            def _():
                second_in(side, c).wait_recv()

        for side in range(2):
            p = 3 * side
            total = N[p, rows] + F[side, rows] * H[2, side, rows]
            U2[p, at] = 0.2 * U1[p, at] + W[p, rows] * total

    def residual(c):
        rows = rows_at(c)
        u = windows(U2, c)
        near = nearby(u, windows(K, c))
        r = [src[p, rows] - D[p, rows] * middle(u[p]) + near[p] for p in range(4)]
        flo = flag[0] * F[0, rows] * middle(u[0])
        fhi = flag[1] * F[1, rows] * middle(u[3])
        X[0, rows] = 0.625 * flo + 0.375 * r[0] + 0.125 * r[1]
        X[1, rows] = (0.375 * flo + 0.625 * r[0] + 0.875 * r[1]) + (0.375 * fhi + 0.625 * r[3] + 0.875 * r[2])
        X[2, rows] = 0.625 * fhi + 0.375 * r[3] + 0.125 * r[2]

    def second_stage(c, _):
        @pl.when(c == 3)
        def _():
            spread(all_q, q_send, q_recv.at[0])

        @pl.when(c < CHUNKS)
        def _():
            finish_two(c)

        @pl.when(c > 0)
        def _():
            residual(c - 1)

        return 0

    lax.fori_loop(0, CHUNKS + 1, second_stage, 0)

    restrict = lambda k: to_coarse(ymat[1], zmat[2:4], X[k])
    all_p[mine_at] = restrict(2 * far)
    spread(all_p, p_send, p_recv.at[0])

    part[0] = restrict(2 * near_side)
    swap = pltpu.make_async_remote_copy(
        src_ref=part.at[0],
        dst_ref=part.at[1],
        send_sem=part_sem.at[0],
        recv_sem=part_sem.at[1],
        device_id={"brick": sibling},
        device_id_type=MESH,
    )
    swap.start()
    mine = restrict(1)
    hand_on(all_q, q_send, q_recv)
    swap.wait_recv()
    all_r[mine_at] = mine + part[1]
    to_sibling(all_r, mine_at, r_send, r_recv.at[half]).start()
    spread_early(all_r, r_send, r_recv)
    spread(all_r, r_send, r_recv.at[me // 2])

    from_sibling(all_q, q_send, q_recv.at[1])
    coarse_coefficients(n, min(8, n), all_q, q_pad, coef, scaled)
    hand_on(all_p, p_send, p_recv)
    hand_on_each(all_r, r_send, r_recv)

    rows, lanes = all_r.shape[2:]
    shifts, _ = coarse_shifts((group, rows, lanes))
    edge = jnp.zeros((rows, lanes), F32)
    for slot in range(2):
        C[slot, 0] = edge
        C[slot, n + 1] = edge
    from_sibling(all_p, p_send, p_recv.at[1])
    from_sibling(all_r, r_send, r_recv.at[half])
    for b in range(n):
        r = all_r[b % 2, b // 2]
        if 0 < b < n - 1:
            r = r + all_p[1 - b % 2, b // 2 - 1 + 2 * (b % 2)]
        scaled_rhs = r * scaled[b]
        B[b] = scaled_rhs
        C[0, b + 1] = scaled_rhs

    for sweep in range(SWEEPS - 1):
        now, later = sweep % 2, 1 - sweep % 2

        def step(g, _):
            at = pl.multiple_of(g * group, group)
            c = C[now, pl.ds(at + 1, group)]
            near = (C[now, pl.ds(at, group)], C[now, pl.ds(at + 2, group)]) + shifts(c)
            terms = [coef[k, pl.ds(at, group)] * v for k, v in enumerate(near)]
            total = B[pl.ds(at, group)] + 0.2 * c
            total = (total + (terms[0] + terms[1])) + ((terms[2] + terms[3]) + (terms[4] + terms[5]))
            C[later, pl.ds(at + 1, group)] = total
            return 0

        lax.fori_loop(0, n // group, step, 0)

    for side in range(2):

        @pl.when(has[side])
        def _():
            halo_sent(side).wait_send()

    swap.wait_send()
    sent(all_q, 0, half, q_send, q_recv.at[0])
    sent(all_p, 0, half, p_send, p_recv.at[0])
    for ref, send, recv in ((all_q, q_send, q_recv), (all_p, p_send, p_recv), (all_r, r_send, r_recv)):
        sent(ref, 1, half - 1, send, recv.at[0])

    @pl.when(early)
    def _():
        sent(all_r, 0, 1, r_send, r_recv.at[0])

    @pl.when(jnp.logical_not(early))
    def _():
        sent(all_r, 0, half, r_send, r_recv.at[0])

    sent_early(all_r, r_send, r_recv)


def coarse_shifts(shape):
    rows, lanes = shape[1:]
    cz = lanes // 2
    row = lax.broadcasted_iota(jnp.int32, shape, 1)
    lane = lax.broadcasted_iota(jnp.int32, shape, 2)
    low_half = lane < cz
    z = jnp.where(low_half, lane, lane - cz)
    outside = (
        (row == 0) & low_half,
        (row == rows - 1) & jnp.logical_not(low_half),
        z == 0,
        z == cz - 1,
    )

    def shifts(c):
        swapped = pltpu.roll(c, cz, 2)
        y_low = jnp.where(low_half, pltpu.roll(swapped, 1, 1), swapped)
        y_high = jnp.where(low_half, swapped, pltpu.roll(swapped, rows - 1, 1))
        return y_low, y_high, pltpu.roll(c, 1, 2), pltpu.roll(c, lanes - 1, 2)

    return shifts, outside


def coarse_coefficients(n, group, perm, q_pad, coef, scaled):
    rows, lanes = perm.shape[2:]
    shifts, outside = coarse_shifts((group, rows, lanes))
    edge = jnp.zeros((rows, lanes), F32)
    q_pad[0] = edge
    q_pad[n + 1] = edge
    for b in range(n):
        q_pad[b + 1] = perm[b % 2, b // 2]

    def prepare(g, _):
        at = pl.multiple_of(g * group, group)
        q = q_pad[pl.ds(at + 1, group)]
        near = [q_pad[pl.ds(at, group)], q_pad[pl.ds(at + 2, group)]]
        near += [jnp.where(out, 0.0, v) for out, v in zip(outside, shifts(q))]
        faces = [0.5 * (q + v) for v in near]
        diagonal = ((faces[0] + faces[1]) + (faces[2] + faces[3])) + (faces[4] + faces[5])
        scale = 0.8 / diagonal
        for k, out in enumerate((None, None) + outside):
            f = faces[k] * scale
            coef[k, pl.ds(at, group)] = f if out is None else jnp.where(out, 0.0, f)
        scaled[pl.ds(at, group)] = (16.0 / 64.0) * scale
        return 0

    lax.fori_loop(0, n // group, prepare, 0)


def prolong_kernel(n, C, U2, ez, ey, holder, corrected_hbm, held_hbm, corrected, held, sem):
    me = lax.axis_index("brick")
    rows, lanes = C.shape[2:]
    ny = corrected.shape[1]
    final = (SWEEPS - 1) % 2
    below, mid, above = C[final, me], C[final, me + 1], C[final, me + 2]
    planes = jnp.concatenate(
        [
            0.625 * mid + 0.375 * below,
            0.875 * mid + 0.125 * below,
            0.875 * mid + 0.125 * above,
            0.625 * mid + 0.375 * above,
        ],
        axis=0,
    )
    pair = jnp.concatenate(split(planes), axis=1)
    even, odd = dot(pair, ez[0]), dot(pair, ez[1])
    copies = []
    for p in range(4):
        both = jnp.concatenate(
            [even[p * rows : (p + 1) * rows], odd[p * rows : (p + 1) * rows]], axis=0
        )
        corrected[p] = U2[p, 8 : ny + 8] + dot(ey[...], jnp.concatenate(split(both), axis=0))
        copies.append(pltpu.make_async_copy(corrected.at[p], corrected_hbm.at[p], sem.at[p]))
        copies[p].start()

    mine = jnp.zeros((rows, lanes), F32)
    for b in range(n):
        mine = jnp.where(holder[b : b + 1] == me, C[final, b + 1], mine)
    for r in range(rows):
        held[0:1, r * lanes : (r + 1) * lanes] = mine[r : r + 1]
    copies.append(pltpu.make_async_copy(held, held_hbm, sem.at[4]))
    copies[4].start()
    for copy in copies:
        copy.wait()


def local(n, source, guess, log_perm, owner):
    planes, ny, nz = source.shape
    assert planes == 4 and n % 2 == 0
    cells = (ny // 4) * (nz // 4)
    rows, lanes = ny // 8, nz // 2
    assert lanes == 128
    dense = (rows, lanes)
    as_bf16 = lambda m: jnp.asarray(m.astype(ml_dtypes.bfloat16))
    py, pz = even_odd(prolong_matrix(ny)), prolong_matrix(nz)
    ymat = as_bf16(np.stack([even_odd(mean_matrix(ny)).T, py.T]))
    zmat = as_bf16(np.concatenate([halves(mean_matrix(nz)), halves(pz)]))
    ey = as_bf16(np.concatenate([py, py], 1))
    ez = as_bf16(np.concatenate([halves(pz).transpose(0, 2, 1)] * 2, 1))
    vmem = pl.BlockSpec(memory_space=pltpu.VMEM)
    hbm = pl.BlockSpec(memory_space=pl.ANY)
    whole = lambda *s: pltpu.VMEM(s, F32)
    dma = lambda *s: pltpu.SemaphoreType.DMA(s)
    padded = (4, ny + 16, nz)
    kept = pl.pallas_call(
        functools.partial(smooth_kernel, n, ny, nz, min(16, n)),
        out_shape=(
            whole(*padded), whole(2, n + 2, *dense), pltpu.VMEM(ez.shape, BF16), pltpu.VMEM(ey.shape, BF16),
            pltpu.VMEM((n, 128), jnp.int32),
        ),
        in_specs=[hbm] * 8,
        out_specs=(vmem,) * 5,
        scratch_shapes=[
            pltpu.SMEM((n,), jnp.int32),
            whole(6, n, *dense), whole(n, *dense),
            pltpu.VMEM(ymat.shape, BF16), pltpu.VMEM(zmat.shape, BF16),
            whole(2, n // 2, *dense), whole(n + 2, *dense), whole(2, n // 2, *dense), whole(2, n // 2, *dense), whole(n, *dense),
            whole(4, ny, nz), whole(4, ny, nz),
            whole(*padded), whole(*padded), whole(*padded),
            whole(4, ny, nz), whole(4, ny, nz), whole(4, ny, nz),
            whole(2, ny, nz), whole(3, ny, nz), whole(3, 2, ny, nz),
            whole(2, *dense),
            dma(8), dma(2), dma(2, FIRST), dma(2, CHUNKS), dma(2),
            dma(2), dma(2), dma(2), dma(2), dma(3), dma(n // 2 + 1),
            pltpu.SemaphoreType.REGULAR(((n - 1).bit_length(),)),
        ],
        compiler_params=pltpu.CompilerParams(
            collective_id=0, has_side_effects=True, vmem_limit_bytes=28 * 2**20
        ),
        name="smooth",
    )(*(pltpu.with_memory_space_constraint(a, pltpu.HBM) for a in (source, guess, log_perm, owner, ymat, zmat, ez, ey)))
    smooth, coarse, ez, ey, holder = [pltpu.with_memory_space_constraint(a, pltpu.VMEM) for a in kept]
    return pl.pallas_call(
        functools.partial(prolong_kernel, n),
        out_shape=(
            jax.ShapeDtypeStruct((4, ny, nz), F32),
            jax.ShapeDtypeStruct((1, cells), F32),
        ),
        in_specs=[vmem] * 5,
        out_specs=(hbm, hbm),
        scratch_shapes=[whole(4, ny, nz), whole(1, cells), dma(5)],
        compiler_params=pltpu.CompilerParams(vmem_limit_bytes=16 * 2**20),
        name="prolong",
    )(coarse, smooth, ez, ey, holder)


def solution(mesh):
    spec = P(("samples", "brick"), None, None)
    return jax.shard_map(
        functools.partial(local, mesh.shape["brick"]),
        mesh=mesh,
        in_specs=(spec, spec, spec, P()),
        out_specs=(spec, P(("samples", "brick"), None)),
        check_vma=False,
    )
```

```python
import functools

import jax
import jax.numpy as jnp
import ml_dtypes
import numpy as np
from jax import lax
from jax.experimental import pallas as pl
from jax.experimental.pallas import tpu as pltpu
from jax.sharding import PartitionSpec as P

SWEEPS = 8
CHUNKS = 8
FIRST = 4
EARLY = 2
HELD = 2
RELEASE = (4, 7)
MESH = pl.DeviceIdType.MESH
F32 = jnp.float32
BF16 = jnp.bfloat16


def prolong_matrix(n_fine):
    i = np.arange(n_fine)[:, None]
    j = np.arange(n_fine // 4)[None, :]
    base, offset = i // 4, i % 4
    own = np.where((offset == 0) | (offset == 3), 0.625, 0.875)
    side = np.where(offset < 2, -1, 1)
    return np.where(j == base, own, 0.0) + np.where(j == base + side, 1.0 - own, 0.0)


def mean_matrix(n_fine):
    i = np.arange(n_fine)[:, None]
    j = np.arange(n_fine // 4)[None, :]
    return np.where(j == i // 4, 1.0, 0.0)


def even_odd(m):
    return np.concatenate([m[:, 0::2], m[:, 1::2]], axis=1)


def halves(m):
    zero = np.zeros_like(m)
    return np.stack([np.concatenate([m, zero], 1), np.concatenate([zero, m], 1)])


def split(x):
    hi = x.astype(BF16)
    return hi, (x - hi.astype(F32)).astype(BF16)


def dot(a, b):
    return jnp.dot(a, b, preferred_element_type=F32)


def to_coarse(y_mat, z_mat, x):
    hi, lo = split(x)
    a = dot(y_mat, hi) + dot(y_mat, lo)
    hi, lo = split(a)
    h = a.shape[0] // 2
    return (
        dot(hi[:h], z_mat[0]) + dot(lo[:h], z_mat[0]) + dot(hi[h:], z_mat[1]) + dot(lo[h:], z_mat[1])
    )


def smooth_kernel(
    n, ny, nz, group,
    source_hbm, guess_hbm, logq_hbm, owner_hbm, y_hbm, z_hbm, ez_hbm, ey_hbm,
    U2, C, ez, ey, holder,
    owner, coef, scaled, ymat, zmat, all_q, q_pad, all_p, all_r, B, src, logq, K, U0, U1, D, W, N, F, X, H, part,
    local_sem, halo_send, first_recv, second_recv, part_sem, q_send, q_recv, p_send, p_recv, r_send, r_recv, token_sem,
):
    me = lax.axis_index("brick")
    R = ny // CHUNKS
    half = n // 2
    has = (me > 0, me < n - 1)
    flag = [jnp.where(h, 1.0, 0.0).astype(F32) for h in has]
    far = lax.rem(me, 2)
    near_side = 1 - far
    sibling = me + 1 - 2 * far
    mine_at = (far, me // 2)
    at_end = jnp.logical_or(me == 0, me == n - 1)
    neighbour = lambda side: me - 1 + 2 * side
    exists = lambda side: jnp.logical_and(neighbour(side) >= 0, neighbour(side) < n)

    loads = [
        pltpu.make_async_copy(logq_hbm, logq, local_sem.at[0]),
        pltpu.make_async_copy(guess_hbm, U0.at[:, pl.ds(8, ny)], local_sem.at[1]),
        pltpu.make_async_copy(source_hbm, src, local_sem.at[2]),
        pltpu.make_async_copy(y_hbm, ymat, local_sem.at[3]),
        pltpu.make_async_copy(z_hbm, zmat, local_sem.at[4]),
        pltpu.make_async_copy(ez_hbm, ez, local_sem.at[5]),
        pltpu.make_async_copy(ey_hbm, ey, local_sem.at[6]),
        pltpu.make_async_copy(owner_hbm, owner, local_sem.at[7]),
    ]

    def signal(sem, who):
        pl.semaphore_signal(sem, inc=1, device_id={"brick": who}, device_id_type=MESH)

    barrier = pltpu.get_barrier_semaphore()

    def greet(sem, distance):
        @pl.when(me >= distance)
        def _():
            signal(sem, me - distance)

        @pl.when(me + distance < n)
        def _():
            signal(sem, me + distance)

    def greeted(sem, distance):
        low = jnp.where(me >= distance, 1, 0)
        high = jnp.where(me + distance < n, 1, 0)
        pl.semaphore_wait(sem, low + high)

    distances = [2**k for k in range((n - 1).bit_length())]

    def relay(k):
        if k < len(distances):
            greeted(token_sem.at[k], distances[k])
        if k + 1 < len(distances):
            greet(token_sem.at[k + 1], distances[k + 1])

    for place in ((0, 0), (1, half - 1)):
        all_p[place] = jnp.zeros(all_p.shape[2:], F32)

    greet(barrier, 1)
    for copy in loads:
        copy.start()

    zero_rows = jnp.zeros((8, nz), F32)
    for ref in (K, U0, U1, U2):
        for p in range(4):
            ref[p, 0:8] = zero_rows
            ref[p, ny + 8 : ny + 16] = zero_rows
    for side in range(2):

        @pl.when(jnp.logical_not(has[side]))
        def _():
            for which in range(3):
                H[which, side] = jnp.zeros((ny, nz), F32)

    greeted(barrier, 1)
    greet(token_sem.at[0], 1)

    def rows_at(c):
        return pl.ds(c * R if isinstance(c, int) else pl.multiple_of(c * R, R), R)

    def rows_in(c):
        return pl.ds(8 + c * R if isinstance(c, int) else pl.multiple_of(c * R, R) + 8, R)

    Q = ny // FIRST

    def send_first(side, chunks):
        for c in chunks:
            rows = pl.ds(c * Q, Q)
            for which, ref in enumerate((logq_hbm, guess_hbm)):
                pltpu.make_async_remote_copy(
                    src_ref=ref.at[3 * side, rows],
                    dst_ref=H.at[which, 1 - side, rows],
                    send_sem=halo_send.at[side],
                    recv_sem=first_recv.at[1 - side, c],
                    device_id={"brick": neighbour(side)},
                    device_id_type=MESH,
                ).start()

    def first_in(side, c):
        ref = H.at[0:2, side, pl.ds(pl.multiple_of(c * Q, Q), Q)]
        return pltpu.make_async_remote_copy(
            src_ref=ref,
            dst_ref=ref,
            send_sem=halo_send.at[side],
            recv_sem=first_recv.at[side, c],
            device_id={"brick": neighbour(side)},
            device_id_type=MESH,
        )

    def second(side, c):
        return pltpu.make_async_remote_copy(
            src_ref=U1.at[3 * side, rows_in(c)],
            dst_ref=H.at[2, 1 - side, rows_at(c)],
            send_sem=halo_send.at[side],
            recv_sem=second_recv.at[1 - side, c],
            device_id={"brick": neighbour(side)},
            device_id_type=MESH,
        )

    def second_in(side, c):
        ref = H.at[2, side, rows_at(c)]
        return pltpu.make_async_remote_copy(
            src_ref=ref,
            dst_ref=ref,
            send_sem=halo_send.at[side],
            recv_sem=second_recv.at[side, c],
            device_id={"brick": neighbour(side)},
            device_id_type=MESH,
        )

    def halo_sent(side):
        ref = H.at[:, side]
        return pltpu.make_async_remote_copy(
            src_ref=ref,
            dst_ref=ref,
            send_sem=halo_send.at[side],
            recv_sem=first_recv.at[side, 0],
            device_id={"brick": neighbour(side)},
            device_id_type=MESH,
        )

    holds = jnp.logical_and(lax.rem(me + 1, 4) < 2, exists(far)) if n == 16 else False

    @pl.when(exists(far))
    def _():
        send_first(far, range(HELD))

    @pl.when(jnp.logical_and(exists(far), jnp.logical_not(holds)))
    def _():
        send_first(far, range(HELD, FIRST))

    send_first(near_side, range(FIRST))

    relay(0)

    lane = lax.broadcasted_iota(jnp.int32, (R, nz), 1)
    first, last = lane == 0, lane == nz - 1

    def middle(window):
        return window[8 : R + 8]

    def yz(window):
        center = middle(window)
        low = jnp.where(first, 0.0, pltpu.roll(center, 1, 1))
        high = jnp.where(last, 0.0, pltpu.roll(center, nz - 1, 1))
        return (window[7 : R + 7] + window[9 : R + 9]) + (low + high)

    def across(windows, p):
        total = yz(windows[p])
        if p > 0:
            total = total + middle(windows[p - 1])
        if p < 3:
            total = total + middle(windows[p + 1])
        return total

    loads[0].wait()

    def exps(c, _):
        for p in range(4):
            K[p, rows_in(c)] = jnp.exp(logq[p, rows_at(c)])
        return 0

    lax.fori_loop(0, CHUNKS, exps, 0)
    for copy in loads[1:]:
        copy.wait()
    relay(1)

    def windows(ref, c):
        at = pl.ds(pl.multiple_of(c * R, R), R + 16)
        return [ref[p, at] for p in range(4)]

    def nearby(u, k):
        uk = [a * b for a, b in zip(u, k)]
        return [0.5 * (middle(k[p]) * across(u, p) + across(uk, p)) for p in range(4)]

    def sweep_one(c, _):
        for k, at_step in enumerate(RELEASE):

            @pl.when(jnp.logical_and(holds, c == at_step))
            def _():
                send_first(far, [HELD + k])

        rows, at = rows_at(c), rows_in(c)
        u, k = windows(U0, c), windows(K, c)
        near = nearby(u, k)
        for p in range(4):
            d = 3.0 * middle(k[p]) + 0.5 * across(k, p)
            total = src[p, rows] + near[p]
            D[p, rows] = d
            if p in (0, 3):
                N[p, rows] = total
            else:
                w = 0.8 / d
                W[p, rows] = w
                U1[p, at] = 0.2 * middle(u[p]) + w * total
        return 0

    lax.fori_loop(0, CHUNKS, sweep_one, 0)

    all_q[mine_at] = to_coarse(
        ymat[0], zmat[0:2], (K[0, 8 : ny + 8] + K[1, 8 : ny + 8]) + (K[2, 8 : ny + 8] + K[3, 8 : ny + 8])
    ) * (1.0 / 64.0)
    for b in range(n):
        holder[b : b + 1] = jnp.full((1, 128), owner[b], jnp.int32)

    relay(2)

    def finish_one(c):
        rows, at = rows_at(c), rows_in(c)
        for side in range(2):

            @pl.when(has[side])
            def _():

                @pl.when(lax.rem(c, CHUNKS // FIRST) == 0)
                def _():
                    first_in(side, c // (CHUNKS // FIRST)).wait_recv()

        for side in range(2):
            p = 3 * side
            kh = jnp.exp(H[0, side, rows]) * flag[side]
            face = 0.5 * (K[p, at] + kh)
            d = D[p, rows] + 0.5 * kh
            w = 0.8 / d
            F[side, rows] = face
            D[p, rows] = d
            W[p, rows] = w
            U1[p, at] = 0.2 * U0[p, at] + w * (N[p, rows] + face * H[1, side, rows])
        for side in (far, near_side):

            @pl.when(exists(side))
            def _():
                second(side, c).start()

    def to_sibling(ref, part_of, send, recv):
        return pltpu.make_async_remote_copy(
            src_ref=ref.at[part_of],
            dst_ref=ref.at[part_of],
            send_sem=send.at[0],
            recv_sem=recv,
            device_id={"brick": sibling},
            device_id_type=MESH,
        )

    def others(body):
        def step(j, _):
            body(j + jnp.where(j >= me // 2, 1, 0))
            return 0

        lax.fori_loop(0, half - 1, step, 0)

    def spread(ref, send, recv):
        def step(k):
            pltpu.make_async_remote_copy(
                src_ref=ref.at[mine_at],
                dst_ref=ref.at[mine_at],
                send_sem=send.at[1],
                recv_sem=recv,
                device_id={"brick": 2 * k + far},
                device_id_type=MESH,
            ).start()

        others(step)

    def from_sibling(ref, send, recv):
        to_sibling(ref, 1 - far, send, recv).wait_recv()

    def hand_on(ref, send, recv):
        to_sibling(ref, (0, pl.ds(0, half - 1)), send, recv.at[0]).wait_recv()
        to_sibling(ref, far, send, recv.at[1]).start()

    early = me < EARLY

    def to_early(ref, k, send, recv):
        return pltpu.make_async_remote_copy(
            src_ref=ref.at[mine_at],
            dst_ref=ref.at[mine_at],
            send_sem=send.at[2],
            recv_sem=recv,
            device_id={"brick": 2 * k + 1 - far},
            device_id_type=MESH,
        )

    def spread_early(ref, send, recv):
        for k in range(EARLY // 2):

            @pl.when(me // 2 != k)
            def _():
                to_early(ref, k, send, recv.at[half]).start()

    def hand_on_each(ref, send, recv):
        def step(k):
            to_sibling(ref, (far, k), send, recv.at[k]).wait_recv()

            @pl.when(jnp.logical_not(early))
            def _():
                to_sibling(ref, (far, k), send, recv.at[half]).start()

        others(step)

    def sent_early(ref, send, recv):
        for k in range(EARLY // 2):

            @pl.when(me // 2 != k)
            def _():
                to_early(ref, k, send, recv.at[half]).wait_send()

    def sent(ref, kind, blocks, send, recv):
        block = ref.at[kind, 0:blocks]
        pltpu.make_async_remote_copy(
            src_ref=block, dst_ref=block, send_sem=send.at[kind], recv_sem=recv,
            device_id={"brick": sibling}, device_id_type=MESH,
        ).wait_send()

    def sweep_two(c):
        rows, at = rows_at(c), rows_in(c)
        u = windows(U1, c)
        near = nearby(u, windows(K, c))
        for p in range(4):
            total = src[p, rows] + near[p]
            if p in (0, 3):
                N[p, rows] = total
            else:
                U2[p, at] = 0.2 * middle(u[p]) + W[p, rows] * total

    relays = range(3, len(distances))

    def first_stage(c, _):
        @pl.when(c < CHUNKS)
        def _():
            finish_one(c)

        for k in relays:

            @pl.when(c == CHUNKS - 1 - (relays[-1] - k))
            def _():
                relay(k)

        @pl.when(c > 0)
        def _():
            sweep_two(c - 1)

        return 0

    lax.fori_loop(0, CHUNKS + 1, first_stage, 0)

    def finish_two(c):
        rows, at = rows_at(c), rows_in(c)
        for side in range(2):

            @pl.when(has[side])
            def _():
                second_in(side, c).wait_recv()

        for side in range(2):
            p = 3 * side
            total = N[p, rows] + F[side, rows] * H[2, side, rows]
            U2[p, at] = 0.2 * U1[p, at] + W[p, rows] * total

    def residual(c):
        rows = rows_at(c)
        u = windows(U2, c)
        near = nearby(u, windows(K, c))
        r = [src[p, rows] - D[p, rows] * middle(u[p]) + near[p] for p in range(4)]
        flo = flag[0] * F[0, rows] * middle(u[0])
        fhi = flag[1] * F[1, rows] * middle(u[3])
        X[0, rows] = 0.625 * flo + 0.375 * r[0] + 0.125 * r[1]
        X[1, rows] = (0.375 * flo + 0.625 * r[0] + 0.875 * r[1]) + (0.375 * fhi + 0.625 * r[3] + 0.875 * r[2])
        X[2, rows] = 0.625 * fhi + 0.375 * r[3] + 0.125 * r[2]

    def second_stage(c, _):
        @pl.when(c == jnp.where(me < n // 2, 3, 2))
        def _():
            spread(all_q, q_send, q_recv.at[0])

        @pl.when(c < CHUNKS)
        def _():
            finish_two(c)

        @pl.when(c > 0)
        def _():
            residual(c - 1)

        return 0

    lax.fori_loop(0, CHUNKS + 1, second_stage, 0)

    restrict = lambda k: to_coarse(ymat[1], zmat[2:4], X[k])
    all_p[mine_at] = restrict(2 * far)
    pl.when(jnp.logical_not(at_end))(lambda: spread(all_p, p_send, p_recv.at[0]))

    part[0] = restrict(2 * near_side)
    swap = pltpu.make_async_remote_copy(
        src_ref=part.at[0],
        dst_ref=part.at[1],
        send_sem=part_sem.at[0],
        recv_sem=part_sem.at[1],
        device_id={"brick": sibling},
        device_id_type=MESH,
    )
    swap.start()
    mine = restrict(1)
    hand_on(all_q, q_send, q_recv)
    swap.wait_recv()
    all_r[mine_at] = mine + part[1]
    to_sibling(all_r, mine_at, r_send, r_recv.at[half]).start()
    spread_early(all_r, r_send, r_recv)
    spread(all_r, r_send, r_recv.at[me // 2])

    from_sibling(all_q, q_send, q_recv.at[1])
    coarse_coefficients(n, min(8, n), all_q, q_pad, coef, scaled)
    for ended, blocks in ((at_end, half - 1), (jnp.logical_not(at_end), half - 2)):

        @pl.when(ended)
        def _():
            to_sibling(all_p, (0, pl.ds(0, blocks)), p_send, p_recv.at[0]).wait_recv()

    to_sibling(all_p, far, p_send, p_recv.at[1]).start()
    hand_on_each(all_r, r_send, r_recv)

    rows, lanes = all_r.shape[2:]
    shifts, _ = coarse_shifts((group, rows, lanes))
    edge = jnp.zeros((rows, lanes), F32)
    for slot in range(2):
        C[slot, 0] = edge
        C[slot, n + 1] = edge
    from_sibling(all_p, p_send, p_recv.at[1])
    from_sibling(all_r, r_send, r_recv.at[half])
    for b in range(n):
        r = all_r[b % 2, b // 2]
        if 0 < b < n - 1:
            r = r + all_p[1 - b % 2, b // 2 - 1 + 2 * (b % 2)]
        scaled_rhs = r * scaled[b]
        B[b] = scaled_rhs
        C[0, b + 1] = scaled_rhs

    for sweep in range(SWEEPS - 1):
        now, later = sweep % 2, 1 - sweep % 2

        def step(g, _):
            at = pl.multiple_of(g * group, group)
            c = C[now, pl.ds(at + 1, group)]
            near = (C[now, pl.ds(at, group)], C[now, pl.ds(at + 2, group)]) + shifts(c)
            terms = [coef[k, pl.ds(at, group)] * v for k, v in enumerate(near)]
            total = B[pl.ds(at, group)] + 0.2 * c
            total = (total + (terms[0] + terms[1])) + ((terms[2] + terms[3]) + (terms[4] + terms[5]))
            C[later, pl.ds(at + 1, group)] = total
            return 0

        lax.fori_loop(0, n // group, step, 0)

    for side in range(2):

        @pl.when(has[side])
        def _():
            halo_sent(side).wait_send()

    swap.wait_send()
    sent(all_q, 0, half, q_send, q_recv.at[0])
    sent(all_p, 0, half, p_send, p_recv.at[0])
    for ref, send, recv in ((all_q, q_send, q_recv), (all_r, r_send, r_recv)):
        sent(ref, 1, half - 1, send, recv.at[0])
    pl.when(jnp.logical_not(at_end))(lambda: sent(all_p, 1, half - 1, p_send, p_recv.at[0]))

    @pl.when(early)
    def _():
        sent(all_r, 0, 1, r_send, r_recv.at[0])

    @pl.when(jnp.logical_not(early))
    def _():
        sent(all_r, 0, half, r_send, r_recv.at[0])

    sent_early(all_r, r_send, r_recv)


def coarse_shifts(shape):
    rows, lanes = shape[1:]
    cz = lanes // 2
    row = lax.broadcasted_iota(jnp.int32, shape, 1)
    lane = lax.broadcasted_iota(jnp.int32, shape, 2)
    low_half = lane < cz
    z = jnp.where(low_half, lane, lane - cz)
    outside = (
        (row == 0) & low_half,
        (row == rows - 1) & jnp.logical_not(low_half),
        z == 0,
        z == cz - 1,
    )

    def shifts(c):
        swapped = pltpu.roll(c, cz, 2)
        y_low = jnp.where(low_half, pltpu.roll(swapped, 1, 1), swapped)
        y_high = jnp.where(low_half, swapped, pltpu.roll(swapped, rows - 1, 1))
        return y_low, y_high, pltpu.roll(c, 1, 2), pltpu.roll(c, lanes - 1, 2)

    return shifts, outside


def coarse_coefficients(n, group, perm, q_pad, coef, scaled):
    rows, lanes = perm.shape[2:]
    shifts, outside = coarse_shifts((group, rows, lanes))
    edge = jnp.zeros((rows, lanes), F32)
    q_pad[0] = edge
    q_pad[n + 1] = edge
    for b in range(n):
        q_pad[b + 1] = perm[b % 2, b // 2]

    def prepare(g, _):
        at = pl.multiple_of(g * group, group)
        q = q_pad[pl.ds(at + 1, group)]
        near = [q_pad[pl.ds(at, group)], q_pad[pl.ds(at + 2, group)]]
        near += [jnp.where(out, 0.0, v) for out, v in zip(outside, shifts(q))]
        faces = [0.5 * (q + v) for v in near]
        diagonal = ((faces[0] + faces[1]) + (faces[2] + faces[3])) + (faces[4] + faces[5])
        scale = 0.8 / diagonal
        for k, out in enumerate((None, None) + outside):
            f = faces[k] * scale
            coef[k, pl.ds(at, group)] = f if out is None else jnp.where(out, 0.0, f)
        scaled[pl.ds(at, group)] = (16.0 / 64.0) * scale
        return 0

    lax.fori_loop(0, n // group, prepare, 0)


def prolong_kernel(n, C, U2, ez, ey, holder, corrected_hbm, held_hbm, corrected, held, sem):
    me = lax.axis_index("brick")
    rows, lanes = C.shape[2:]
    ny = corrected.shape[1]
    final = (SWEEPS - 1) % 2
    below, mid, above = C[final, me], C[final, me + 1], C[final, me + 2]
    planes = jnp.concatenate(
        [
            0.625 * mid + 0.375 * below,
            0.875 * mid + 0.125 * below,
            0.875 * mid + 0.125 * above,
            0.625 * mid + 0.375 * above,
        ],
        axis=0,
    )
    pair = jnp.concatenate(split(planes), axis=1)
    even, odd = dot(pair, ez[0]), dot(pair, ez[1])
    copies = []
    for p in range(4):
        both = jnp.concatenate(
            [even[p * rows : (p + 1) * rows], odd[p * rows : (p + 1) * rows]], axis=0
        )
        corrected[p] = U2[p, 8 : ny + 8] + dot(ey[...], jnp.concatenate(split(both), axis=0))
        copies.append(pltpu.make_async_copy(corrected.at[p], corrected_hbm.at[p], sem.at[p]))
        copies[p].start()

    mine = jnp.zeros((rows, lanes), F32)
    for b in range(n):
        mine = jnp.where(holder[b : b + 1] == me, C[final, b + 1], mine)
    for r in range(rows):
        held[0:1, r * lanes : (r + 1) * lanes] = mine[r : r + 1]
    copies.append(pltpu.make_async_copy(held, held_hbm, sem.at[4]))
    copies[4].start()
    for copy in copies:
        copy.wait()


def local(n, source, guess, log_perm, owner):
    planes, ny, nz = source.shape
    assert planes == 4 and n % 2 == 0
    cells = (ny // 4) * (nz // 4)
    rows, lanes = ny // 8, nz // 2
    assert lanes == 128
    dense = (rows, lanes)
    as_bf16 = lambda m: jnp.asarray(m.astype(ml_dtypes.bfloat16))
    py, pz = even_odd(prolong_matrix(ny)), prolong_matrix(nz)
    ymat = as_bf16(np.stack([even_odd(mean_matrix(ny)).T, py.T]))
    zmat = as_bf16(np.concatenate([halves(mean_matrix(nz)), halves(pz)]))
    ey = as_bf16(np.concatenate([py, py], 1))
    ez = as_bf16(np.concatenate([halves(pz).transpose(0, 2, 1)] * 2, 1))
    vmem = pl.BlockSpec(memory_space=pltpu.VMEM)
    hbm = pl.BlockSpec(memory_space=pl.ANY)
    whole = lambda *s: pltpu.VMEM(s, F32)
    dma = lambda *s: pltpu.SemaphoreType.DMA(s)
    padded = (4, ny + 16, nz)
    kept = pl.pallas_call(
        functools.partial(smooth_kernel, n, ny, nz, min(16, n)),
        out_shape=(
            whole(*padded), whole(2, n + 2, *dense), pltpu.VMEM(ez.shape, BF16), pltpu.VMEM(ey.shape, BF16),
            pltpu.VMEM((n, 128), jnp.int32),
        ),
        in_specs=[hbm] * 8,
        out_specs=(vmem,) * 5,
        scratch_shapes=[
            pltpu.SMEM((n,), jnp.int32),
            whole(6, n, *dense), whole(n, *dense),
            pltpu.VMEM(ymat.shape, BF16), pltpu.VMEM(zmat.shape, BF16),
            whole(2, n // 2, *dense), whole(n + 2, *dense), whole(2, n // 2, *dense), whole(2, n // 2, *dense), whole(n, *dense),
            whole(4, ny, nz), whole(4, ny, nz),
            whole(*padded), whole(*padded), whole(*padded),
            whole(4, ny, nz), whole(4, ny, nz), whole(4, ny, nz),
            whole(2, ny, nz), whole(3, ny, nz), whole(3, 2, ny, nz),
            whole(2, *dense),
            dma(8), dma(2), dma(2, FIRST), dma(2, CHUNKS), dma(2),
            dma(2), dma(2), dma(2), dma(2), dma(3), dma(n // 2 + 1),
            pltpu.SemaphoreType.REGULAR(((n - 1).bit_length(),)),
        ],
        compiler_params=pltpu.CompilerParams(
            collective_id=0, has_side_effects=True, vmem_limit_bytes=28 * 2**20
        ),
        name="smooth",
    )(*(pltpu.with_memory_space_constraint(a, pltpu.HBM) for a in (source, guess, log_perm, owner, ymat, zmat, ez, ey)))
    smooth, coarse, ez, ey, holder = [pltpu.with_memory_space_constraint(a, pltpu.VMEM) for a in kept]
    return pl.pallas_call(
        functools.partial(prolong_kernel, n),
        out_shape=(
            jax.ShapeDtypeStruct((4, ny, nz), F32),
            jax.ShapeDtypeStruct((1, cells), F32),
        ),
        in_specs=[vmem] * 5,
        out_specs=(hbm, hbm),
        scratch_shapes=[whole(4, ny, nz), whole(1, cells), dma(5)],
        compiler_params=pltpu.CompilerParams(vmem_limit_bytes=16 * 2**20),
        name="prolong",
    )(coarse, smooth, ez, ey, holder)


def solution(mesh):
    spec = P(("samples", "brick"), None, None)
    return jax.shard_map(
        functools.partial(local, mesh.shape["brick"]),
        mesh=mesh,
        in_specs=(spec, spec, spec, P()),
        out_specs=(spec, P(("samples", "brick"), None)),
        check_vma=False,
    )
```
